32 devices in a mesh: parts: 2 (over y), ctx: 4 (over z), grid: 4 (over x, core).
Axes of the slice: x: 2, y: 2, z: 4, core: 2. Of those that a mesh axis runs over, the one named last changes fastest.
Arguments:
- frames_in: bfloat16 [4096, 1536], P(('parts', 'ctx'), 'grid'), parts along dimension 0, may hold values from -230 to 230
- norm1_gain: bfloat16 [1536], P('grid'), may hold values from 0.25 to 1.75
- norm1_bias: bfloat16 [1536], P('grid'), may hold values from -3 to 3
- w_query: bfloat16 [1536, 1536], P(None, 'grid'), may hold values from -0.5 to 0.5
- w_key: bfloat16 [1536, 1536], P(None, 'grid'), may hold values from -2 to 2
- w_value: bfloat16 [1536, 1536], P(None, 'grid'), may hold values from -0.15625 to 0.15625
- w_out: bfloat16 [1536, 1536], P('grid'), may hold values from -0.15625 to 0.15625
- norm2_gain: bfloat16 [1536], P('grid'), may hold values from 0.099609375 to 1.8984375
- norm2_bias: bfloat16 [1536], P('grid'), may hold values from -3 to 3
- w_glu_value: bfloat16 [1536, 1536], P(None, 'grid'), may hold values from -0.15625 to 0.15625
- w_glu_gate: bfloat16 [1536, 1536], P(None, 'grid'), may hold values from -0.15625 to 0.15625
- depth_kernel: float32 [31, 1536], P(None, 'grid'), may hold values from -1 to 1
- bn_scale: float32 [1536], P('grid'), may hold values from 0.25 to 1.75
- bn_shift: float32 [1536], P('grid'), may hold values from -3 to 3
- w_proj: bfloat16 [1536, 1536], P('grid'), may hold values from -0.3125 to 0.3125
Outputs:
- layer_out: bfloat16 [4096, 1536], P(('parts', 'ctx'), 'grid'), parts along dimension 0
The draws below stay inside these ranges and needn't reach their ends.
There are 2 independent parts, one for each index of `parts`. The reference program is written for one: setup_inputs(seed, part) draws one part's arguments, and reference() takes and returns one part's arrays. A program takes and returns all parts, laid end to end along the dimension named above; an argument that names none is the same for every part. Nothing has to cross between parts.
All inputs are finite; a program needn't handle non-finite values.
Results may differ from the reference program's by a relative error of at most 0.009.
Values may be sent and summed in bfloat16 or wider, within the bound.
No kernel may reach another device: no remote copies, remote signals or barrier semaphores. Data moves between devices by JAX's collectives and lax.ppermute only.
A program may use at most 256 MiB of HBM per device.

```python
import math
import jax
import jax.numpy as jnp
from jax import lax

D = 1536
HEADS = 24
HEAD_DIM = 64
KERNEL = 31
HALF = 15
FRAMES = 2048
N_GRID = 4


def draw_frames_in(key, part):
    first_key = jax.random.fold_in(key, 0)
    columns = jnp.arange(D, dtype=jnp.float32)
    column_scale = jnp.exp(math.log(10.0) * columns / (D - 1))
    base = jnp.clip(jax.random.normal(first_key, (FRAMES, D), jnp.float32), -4.0, 4.0)
    result = base * column_scale
    return result.astype(jnp.bfloat16)


def query_key_base(key):
    base_key = jax.random.fold_in(key, 101)
    first_key, second_key = jax.random.split(base_key, 2)
    first_normal = jnp.clip(jax.random.normal(first_key, (D, D), jnp.float32), -6.0, 6.0)
    second_normal = jnp.clip(jax.random.normal(second_key, (D, D), jnp.float32), -6.0, 6.0)
    return (first_normal, second_normal)


def draw_w_query(key, part):
    first_normal, second_normal = query_key_base(key)
    return jnp.clip(3.0 * first_normal / math.sqrt(D), -0.5, 0.5).astype(jnp.bfloat16)


def draw_w_key(key, part):
    first_normal, second_normal = query_key_base(key)
    result = second_normal / math.sqrt(D)
    return jnp.clip(result, -2.0, 2.0).astype(jnp.bfloat16)


def steps_of(key, extent, pieces, low, high):
    level, own = 1.0, jax.random.fold_in(key, 6)
    for dim, parts in pieces:
        draws = jnp.exp(jax.random.uniform(jax.random.fold_in(own, dim), (parts,), jnp.float32, low / len(pieces), high / len(pieces)))
        level = level * jnp.repeat(draws, extent[dim] // parts).reshape([-1 if axis == dim else 1 for axis in range(len(extent))])
    return level


def centred(rng, dims, width, limit, cuts=(), held_as=jnp.bfloat16):
    drawn = width * jax.random.normal(rng, dims, jnp.float32)
    if cuts:
        drawn = drawn * steps_of(rng, dims, cuts, -0.22, 0.18)
    return jnp.clip(drawn, -limit, limit).astype(held_as)


def setup_inputs(seed: int = 0, part: int = 0) -> dict:
    key_list = jax.random.split(jax.random.key(seed), 16)
    own_keys = jax.random.split(jax.random.fold_in(key_list[15], part), 16)
    frames_in = draw_frames_in(jax.random.fold_in(jax.random.fold_in(key_list[15], part), 71), part)
    norm1_gain = jnp.clip(1.0 + 0.15 * jax.random.normal(key_list[1], (D,), jnp.float32), 0.25, 1.75).astype(jnp.bfloat16)
    norm1_bias = centred(key_list[2], (D,), 0.5, 3.0, ((0, 4),))
    w_query = draw_w_query(jax.random.fold_in(key_list[15], 71), part)
    w_key = draw_w_key(jax.random.fold_in(key_list[15], 71), part)
    w_value = centred(key_list[5], (D, D), D ** -0.5, 0.15625, ((1, 4),))
    w_out = centred(key_list[6], (D, D), D ** -0.5, 0.15625, ((0, 4),))
    norm2_gain = jnp.clip(1.0 + 0.18 * jax.random.normal(key_list[7], (D,), jnp.float32), 0.099609375, 1.8984375).astype(jnp.bfloat16)
    norm2_bias = centred(key_list[8], (D,), 0.5, 3.0, ((0, 4),))
    w_glu_value = centred(key_list[9], (D, D), D ** -0.5, 0.15625, ((1, 4),))
    w_glu_gate = centred(key_list[10], (D, D), D ** -0.5, 0.15625, ((1, 4),))
    depth_kernel = centred(key_list[11], (KERNEL, D), KERNEL ** -0.5, 1.0, ((1, 4),), jnp.float32)
    bn_scale = jnp.clip(1.0 + 0.15 * jax.random.normal(key_list[12], (D,), jnp.float32), 0.25, 1.75)
    bn_shift = centred(key_list[13], (D,), 0.5, 3.0, ((0, 4),), jnp.float32)
    w_proj = centred(key_list[14], (D, D), (D // 4) ** -0.5, 0.3125, ((0, 4),))
    return dict(frames_in=frames_in, norm1_gain=norm1_gain, norm1_bias=norm1_bias, w_query=w_query, w_key=w_key, w_value=w_value, w_out=w_out, norm2_gain=norm2_gain, norm2_bias=norm2_bias, w_glu_value=w_glu_value, w_glu_gate=w_glu_gate, depth_kernel=depth_kernel, bn_scale=bn_scale, bn_shift=bn_shift, w_proj=w_proj)


EPSILON = 1e-05

def layer_norm(values, gain_vec, shift_vec):
    values = values.astype(jnp.float32)
    row_mean = lax.optimization_barrier(jnp.mean(values, axis=1, keepdims=True))
    variance = lax.optimization_barrier(jnp.mean(jnp.square(values - row_mean), axis=1, keepdims=True))
    scaled = (values - row_mean) * lax.rsqrt(variance + EPSILON)
    return (scaled * gain_vec.astype(jnp.float32) + shift_vec.astype(jnp.float32)).astype(jnp.bfloat16)

def grouped_product(activation, weight):
    group_width = activation.shape[1] // N_GRID
    running = jnp.zeros((activation.shape[0], weight.shape[1]), jnp.float32)
    for group_index in range(N_GRID):
        lower = group_index * group_width
        partial_sum = jnp.dot(activation[:, lower:lower + group_width], weight[lower:lower + group_width], preferred_element_type=jnp.float32)
        rounded = lax.optimization_barrier(partial_sum.astype(jnp.bfloat16))
        running = running + rounded.astype(jnp.float32)
    return running

def attend_all(queries, key_rows, value_rows):
    frame_count = queries.shape[0]
    block_rows = math.gcd(frame_count, 512)
    key_heads = key_rows.reshape(frame_count, HEADS, HEAD_DIM).astype(jnp.float32)
    value_heads = value_rows.reshape(frame_count, HEADS, HEAD_DIM).astype(jnp.float32)

    def one_block(query_block):
        query_heads = query_block.reshape(block_rows, HEADS, HEAD_DIM).astype(jnp.float32)
        scores = jnp.einsum('qhd,khd->hqk', query_heads, key_heads) * (1.0 / math.sqrt(HEAD_DIM))
        peak = lax.optimization_barrier(jnp.max(scores, axis=2, keepdims=True))
        soft = jnp.exp(scores - peak)
        totals = lax.optimization_barrier(jnp.sum(soft, axis=2))
        soft_rounded = lax.optimization_barrier(soft.astype(jnp.bfloat16))
        mixed = jnp.einsum('hqk,khd->qhd', soft_rounded.astype(jnp.float32), value_heads)
        mixed = mixed / jnp.transpose(totals)[:, :, None]
        return mixed.reshape(block_rows, HEADS * HEAD_DIM).astype(jnp.bfloat16)
    blocks = queries.reshape(frame_count // block_rows, block_rows, HEADS * HEAD_DIM)
    return lax.map(one_block, blocks).reshape(frame_count, HEADS * HEAD_DIM)

def reference(frames_in, norm1_gain, norm1_bias, w_query, w_key, w_value, w_out, norm2_gain, norm2_bias, w_glu_value, w_glu_gate, depth_kernel, bn_scale, bn_shift, w_proj):
    normed = layer_norm(frames_in, norm1_gain, norm1_bias)
    queries = jnp.dot(normed, w_query, preferred_element_type=jnp.float32).astype(jnp.bfloat16)
    key_rows = jnp.dot(normed, w_key, preferred_element_type=jnp.float32).astype(jnp.bfloat16)
    value_rows = jnp.dot(normed, w_value, preferred_element_type=jnp.float32).astype(jnp.bfloat16)
    attended = attend_all(queries, key_rows, value_rows)
    middle = (frames_in.astype(jnp.float32) + grouped_product(attended, w_out)).astype(jnp.bfloat16)
    normed_conv = layer_norm(middle, norm2_gain, norm2_bias)
    value_part = jnp.dot(normed_conv, w_glu_value, preferred_element_type=jnp.float32)
    gate_part = jnp.dot(normed_conv, w_glu_gate, preferred_element_type=jnp.float32)
    gated = lax.optimization_barrier((value_part * jax.nn.sigmoid(gate_part)).astype(jnp.bfloat16))
    padded = jnp.pad(gated.astype(jnp.float32), ((HALF, HALF), (0, 0)))
    frame_count = frames_in.shape[0]
    convolved = jnp.zeros((frame_count, frames_in.shape[1]), jnp.float32)
    for tap_index in range(KERNEL):
        convolved = convolved + depth_kernel[tap_index] * padded[tap_index:tap_index + frame_count]
    activated = jax.nn.silu(convolved * bn_scale + bn_shift).astype(jnp.bfloat16)
    return (middle.astype(jnp.float32) + grouped_product(activated, w_proj)).astype(jnp.bfloat16)
```

```python
import functools
import math

import jax
import jax.numpy as jnp
from jax import lax
from jax.experimental import pallas as pl
from jax.experimental.pallas import tpu as pltpu
from jax.sharding import PartitionSpec as P

HEAD_DIM = 64
PAIR = 2 * HEAD_DIM
KERNEL = 31
HALF = 15
HALO = 16
EPSILON = 1e-05
CORES = 2
VMEM_BYTES = 48 * 1024 * 1024
BF16 = jnp.bfloat16
F32 = jnp.float32


def exchange(cells, axis, distance):
    count = lax.axis_size(axis)
    return lax.ppermute(cells, axis, [(i, i ^ distance) for i in range(count)])


def whole(shape):
    return pl.BlockSpec(shape, lambda j: (0,) * len(shape))


def cost(flops, bytes_accessed, transcendentals=0):
    return pl.CostEstimate(
        flops=int(flops), bytes_accessed=int(bytes_accessed), transcendentals=int(transcendentals)
    )


def after(cells, *done):
    def body(*refs):
        pass

    anywhere = pl.BlockSpec(memory_space=pl.ANY)
    return pl.pallas_call(
        body,
        in_specs=[anywhere] * (1 + len(done)),
        out_specs=anywhere,
        out_shape=jax.ShapeDtypeStruct(cells.shape, cells.dtype),
        input_output_aliases={0: 0},
        cost_estimate=cost(0, 0),
    )(cells, *done)


def rows_by_distance(me, order, *refs):
    width = refs[0].shape[0] // len(order)
    pieces = []
    for r in order:
        rows = pl.ds(pl.multiple_of((me ^ r) * width, width), width)
        pieces.append(jnp.concatenate([ref[rows, :] for ref in refs], axis=1))
    return jnp.concatenate(pieces, axis=0)


def params():
    return pltpu.CompilerParams(
        vmem_limit_bytes=VMEM_BYTES, dimension_semantics=("arbitrary",)
    )


def norm_rows(halves, norm_ref, normed_ref, rows):
    total, half = normed_ref.shape
    width = half // len(halves)

    def step(index, carry):
        start = pl.multiple_of(index * rows, rows)
        parts = [ref[pl.ds(start, rows), :].astype(F32) for ref in halves]
        mean = sum(jnp.sum(part, axis=1, keepdims=True) for part in parts) / half
        parts = [part - mean for part in parts]
        variance = sum(jnp.sum(part * part, axis=1, keepdims=True) for part in parts) / half
        scale = lax.rsqrt(variance + EPSILON)
        for k, part in enumerate(parts):
            cols = slice(k * width, (k + 1) * width)
            normed = part * scale * norm_ref[0:1, cols] + norm_ref[1:2, cols]
            normed_ref[pl.ds(start, rows), cols] = normed.astype(BF16)
        return carry

    lax.fori_loop(0, total // rows, step, 0, unroll=2)


def project_kernel(order, splits, me_ref, even_ref, odd_ref, norm_ref, *refs):
    weight_refs, (key_ref, value_ref, *query_refs, normed) = refs[:splits], refs[splits:]

    @pl.when(pl.program_id(0) == 0)
    def _():
        norm_rows((even_ref, odd_ref), norm_ref, normed, 32)

    weights = rows_by_distance(me_ref[0], order, *weight_refs)
    projected = jnp.dot(normed[...], weights, preferred_element_type=F32)
    key_ref[...] = projected[:, :PAIR].astype(BF16)
    lanes = lax.broadcasted_iota(jnp.int32, (1, PAIR), 1)
    low = lanes < HEAD_DIM
    values = projected[:, PAIR : 2 * PAIR]
    low_sum = ((lanes >= HEAD_DIM) & (lanes < HEAD_DIM + 32)).astype(F32)
    high_sum = (lanes < 32).astype(F32)
    value_ref[:, :PAIR] = jnp.where(low, values, low_sum).astype(BF16)
    value_ref[:, PAIR:] = jnp.where(low, high_sum, values).astype(BF16)
    if query_refs:
        queries = projected[:, 2 * PAIR :] * (math.log2(math.e) / math.sqrt(HEAD_DIM))
        query_refs[0][:, :PAIR] = jnp.where(low, queries, 0.0).astype(BF16)
        query_refs[0][:, PAIR:] = jnp.where(low, 0.0, queries).astype(BF16)


def project_slot(me, order, even, odd, norm, *weights):
    frames, half = even.shape
    width, columns = weights[0].shape
    pairs = columns // PAIR
    narrow = (jax.ShapeDtypeStruct((frames, columns), BF16), pl.BlockSpec((frames, PAIR), lambda j: (0, j)))
    wide = (jax.ShapeDtypeStruct((frames, 2 * columns), BF16), pl.BlockSpec((frames, 2 * PAIR), lambda j: (0, j)))
    outs = [narrow, wide] + [wide] * (len(weights) - 2)
    return pl.pallas_call(
        functools.partial(project_kernel, order, len(weights)),
        grid=(pairs,),
        in_specs=[
            pl.BlockSpec(memory_space=pltpu.SMEM),
            whole((frames, half)),
            whole((frames, half)),
            whole(norm.shape),
            *[pl.BlockSpec((width, PAIR), lambda j: (0, j))] * len(weights),
        ],
        out_shape=tuple(shape for shape, _ in outs),
        out_specs=tuple(spec for _, spec in outs),
        scratch_shapes=[pltpu.VMEM((frames, width), BF16)],
        compiler_params=params(),
        cost_estimate=cost(2 * frames * width * columns * len(weights), 4 * frames * width + 2 * width * columns * len(weights)),
    )(me, even, odd, norm, *weights)


def attend_kernel(first, last, query_rows, query_ref, key_ref, value_ref, *refs):
    refs = list(refs)
    old_ref = None if first else refs.pop(0)
    if last:
        out_w_ref, _, keep_ref, send_ref, attended = refs
    else:
        _, state_ref, token_ref = refs
        token_ref[...] = jnp.zeros_like(token_ref)
    pair = pl.program_id(0)
    total = query_ref.shape[0]
    lanes = lax.broadcasted_iota(jnp.int32, (1, PAIR), 1)
    keys = key_ref[...]
    for start in range(0, total, query_rows):
        rows = slice(start, start + query_rows)
        finished = []
        for head in range(2):
            sum_lane = HEAD_DIM if head == 0 else 0
            max_lane = sum_lane + 32
            cols = slice(head * PAIR, (head + 1) * PAIR)
            scores = lax.dot_general(
                query_ref[rows, cols], keys, (((1,), (1,)), ((), ())), preferred_element_type=F32
            )
            peak = jnp.max(scores, axis=1, keepdims=True)
            if not first:
                old = old_ref[rows, cols]
                old_peak = old[:, max_lane : max_lane + 1]
                peak = jnp.maximum(peak, old_peak)
            soft = jnp.exp2(scores - peak).astype(BF16)
            state = jnp.dot(soft, value_ref[:, cols], preferred_element_type=F32)
            if not first:
                state = old * jnp.exp2(old_peak - peak) + state
            if last:
                finished.append(state / state[:, sum_lane : sum_lane + 1])
            else:
                is_max = (lanes >= max_lane) & (lanes < max_lane + 32)
                state_ref[rows, cols] = jnp.where(is_max, peak, state)
        if last:
            attended[pair, rows, :] = jnp.where(lanes < HEAD_DIM, *finished).astype(BF16)
    if last:

        @pl.when(pair == pl.num_programs(0) - 1)
        def _():
            half = keep_ref.shape[1]
            for ref, offset in ((keep_ref, 0), (send_ref, half)):
                share = sum(
                    jnp.dot(
                        attended[k],
                        out_w_ref[k * PAIR : (k + 1) * PAIR, offset : offset + half],
                        preferred_element_type=F32,
                    )
                    for k in range(attended.shape[0])
                )
                ref[...] = share.astype(BF16)


def attend_slot(queries, keys, values, state=None, w_out=None, behind=None):
    first, last = state is None, w_out is not None
    frames, columns = keys.shape
    pairs = columns // PAIR
    behind = queries if behind is None else behind
    row_spec = pl.BlockSpec((frames, 2 * PAIR), lambda j: (0, j))
    anywhere = pl.BlockSpec(memory_space=pl.ANY)
    operands, in_specs = [queries, keys, values], [row_spec, pl.BlockSpec((frames, PAIR), lambda j: (0, j)), row_spec]
    aliases, scratch = {}, []
    if not first:
        operands.append(state)
        in_specs.append(row_spec)
    if last:
        half = w_out.shape[1] // 2
        operands.append(w_out)
        in_specs.append(whole(w_out.shape))
        out_shape = (jax.ShapeDtypeStruct((frames, half), BF16),) * 2
        out_specs = (whole((frames, half)),) * 2
        scratch.append(pltpu.VMEM((pairs, frames, PAIR), BF16))
    else:
        out_shape = (jax.ShapeDtypeStruct(values.shape, F32), jax.ShapeDtypeStruct((8, 128), F32))
        out_specs = (row_spec, whole((8, 128)))
        aliases = {} if first else {3: 0}
    return pl.pallas_call(
        functools.partial(attend_kernel, first, last, math.gcd(frames, 256)),
        grid=(pairs,),
        in_specs=in_specs + [anywhere],
        out_specs=out_specs,
        out_shape=out_shape,
        scratch_shapes=scratch,
        input_output_aliases=aliases,
        compiler_params=params(),
        cost_estimate=cost(16 * frames * frames * columns, 20 * frames * columns, 2 * frames * frames * pairs),
    )(*operands, behind)


def glu_kernel(order, me_ref, even_ref, odd_ref, norm_ref, value_ref, gate_ref, out_ref, normed):
    @pl.when(pl.program_id(0) == 0)
    def _():
        norm_rows((even_ref, odd_ref), norm_ref, normed, 32)

    weights = rows_by_distance(me_ref[0], order, value_ref, gate_ref)
    both = jnp.dot(normed[...], weights, preferred_element_type=F32)
    out_ref[...] = (both[:, :PAIR] * jax.nn.sigmoid(both[:, PAIR:])).astype(BF16)


def gated_units(me, order, even, odd, norm, w_value, w_gate):
    frames, half = even.shape
    blocks = w_value.shape[1] // PAIR
    weight_spec = pl.BlockSpec((2 * half, PAIR), lambda j: (0, j))
    return pl.pallas_call(
        functools.partial(glu_kernel, order),
        grid=(blocks,),
        in_specs=[
            pl.BlockSpec(memory_space=pltpu.SMEM),
            whole((frames, half)),
            whole((frames, half)),
            whole(norm.shape),
            weight_spec,
            weight_spec,
        ],
        out_specs=pl.BlockSpec((frames, PAIR), lambda j: (0, j)),
        out_shape=jax.ShapeDtypeStruct((frames, blocks * PAIR), BF16),
        scratch_shapes=[pltpu.VMEM((frames, 2 * half), BF16)],
        compiler_params=params(),
        cost_estimate=cost(8 * frames * half * blocks * PAIR, 4 * frames * half + 8 * half * blocks * PAIR),
    )(me, even, odd, norm, w_value, w_gate)


def conv_kernel(gated_ref, left_ref, right_ref, taps_ref, bn_ref, w_ref, keep_ref, send_ref, padded, activated):
    step = pl.program_id(0)
    total, width = gated_ref.shape
    rows = keep_ref.shape[0]
    piece = 32

    @pl.when(step == 0)
    def _():
        padded[0:HALO, :] = left_ref[...].astype(F32)
        padded[HALO : HALO + total, :] = gated_ref[...].astype(F32)
        padded[HALO + total :, :] = right_ref[...].astype(F32)

    for col in range(0, width, PAIR):
        cols = slice(col, col + PAIR)
        taps = [taps_ref[j : j + 1, cols] for j in range(KERNEL)]
        scale, shift = bn_ref[0:1, cols], bn_ref[1:2, cols]

        def block(index, carry):
            start = pl.multiple_of(step * rows + index * piece, piece)
            window = padded[pl.ds(start, piece + 2 * HALO), cols]
            convolved = None
            for residue in range(8):
                part = None
                for offset in range(residue, KERNEL + 1, 8):
                    if offset == 0:
                        continue
                    base = offset - residue
                    term = taps[offset - 1] * window[base : base + piece + 8]
                    part = term if part is None else part + term
                part = part[residue : residue + piece]
                convolved = part if convolved is None else convolved + part
            value = convolved * scale + shift
            local = pl.multiple_of(index * piece, piece)
            activated[pl.ds(local, piece), cols] = (value / (1.0 + jnp.exp(-value))).astype(BF16)
            return carry

        lax.fori_loop(0, rows // piece, block, 0, unroll=2)
    half = keep_ref.shape[1]
    keep_ref[...] = jnp.dot(activated[...], w_ref[:, :half], preferred_element_type=F32).astype(BF16)
    send_ref[...] = jnp.dot(activated[...], w_ref[:, half:], preferred_element_type=F32).astype(BF16)


def conv_project(gated, left, right, taps, bn, w_proj):
    frames, width = gated.shape
    half = w_proj.shape[1] // 2
    rows = math.gcd(frames, 128)
    row_spec = pl.BlockSpec((rows, half), lambda j: (j, 0))
    return pl.pallas_call(
        conv_kernel,
        grid=(frames // rows,),
        in_specs=[
            whole(gated.shape),
            whole(left.shape),
            whole(right.shape),
            whole(taps.shape),
            whole(bn.shape),
            whole(w_proj.shape),
        ],
        out_specs=(row_spec, row_spec),
        out_shape=(jax.ShapeDtypeStruct((frames, half), BF16),) * 2,
        scratch_shapes=[
            pltpu.VMEM((frames + 2 * HALO, width), F32),
            pltpu.VMEM((rows, width), BF16),
        ],
        compiler_params=params(),
        cost_estimate=cost(4 * frames * width * half + 64 * frames * width, 8 * frames * half),
    )(gated, left, right, taps, bn, w_proj)


def pad_columns(weight, width):
    if weight.shape[1] == width:
        return weight
    return jnp.pad(weight, ((0, 0), (0, width - weight.shape[1])))


def halo_rows(gated):
    count = lax.axis_size("ctx")
    frames = gated.shape[0]
    left = lax.ppermute(gated[frames - HALO :], "ctx", [(i, i + 1) for i in range(count - 1)])
    right = lax.ppermute(gated[:HALO], "ctx", [(i + 1, i) for i in range(count - 1)])
    return left, right


def on_device(
    frames_in,
    norm1_gain,
    norm1_bias,
    w_query,
    w_key,
    w_value,
    w_out,
    norm2_gain,
    norm2_bias,
    w_glu_value,
    w_glu_gate,
    depth_kernel,
    bn_scale,
    bn_shift,
    w_proj,
):
    frames, width = frames_in.shape
    grid, ctx = lax.axis_size("grid"), lax.axis_size("ctx")
    me = lax.axis_index("grid")
    order = list(range(0, grid, CORES)) + list(range(1, grid, CORES))
    padded = -(-width // PAIR) * PAIR

    def by_distance(cells, axis):
        return jnp.concatenate(
            [lax.dynamic_slice_in_dim(cells, (me ^ r) * width, width, axis) for r in order], axis=axis
        )

    def over_chips(block):
        return [block] + [exchange(block, "grid", CORES * a) for a in range(1, grid // CORES)]

    gains = lax.all_gather(
        jnp.stack([norm1_gain, norm1_bias, norm2_gain, norm2_bias]), "grid", axis=1, tiled=True
    )
    gains = by_distance(gains, 1).astype(F32)
    norm1, norm2 = gains[:2], gains[2:]
    w_query, w_key, w_value, w_glu_value, w_glu_gate = (
        pad_columns(weight, padded) for weight in (w_query, w_key, w_value, w_glu_value, w_glu_gate)
    )
    row_pad = ((0, padded - width), (0, 0))
    w_o = jnp.pad(by_distance(w_out, 1), row_pad)
    w_p = jnp.pad(by_distance(w_proj, 1), row_pad)
    taps = pad_columns(depth_kernel, padded)
    bn = pad_columns(jnp.stack([bn_scale, bn_shift]), padded)
    place = me.astype(jnp.int32).reshape(1)

    steps = [1 << k for k in range(ctx.bit_length() - 1)]
    raw = {0: frames_in}
    parts = {0: over_chips(frames_in)}
    for distance in reversed(steps):
        raw[distance] = exchange(frames_in, "ctx", distance)
    queries = state = own_even = token = None
    for s in range(ctx):
        if s == 1:
            parts[1] = over_chips(raw[1])
        pieces = parts[s]
        if s > 0:
            pieces = pieces[:1] + [after(piece, token) for piece in pieces[1:]]
        even = jnp.concatenate(pieces, axis=1)
        odd = exchange(even, "grid", 1)
        ahead = s + 2
        if ahead < ctx:
            low = ahead & -ahead
            if ahead != low:
                raw[ahead] = exchange(raw[ahead ^ low], "ctx", low)
            parts[ahead] = over_chips(raw[ahead])
        if s == 0:
            own_even = even
            keys, values, queries = project_slot(place, order, even, odd, norm1, w_key, w_value, w_query)
        else:
            keys, values = project_slot(place, order, even, odd, norm1, w_key, w_value)
        if s < ctx - 1:
            state, token = attend_slot(queries, keys, values, state=state, behind=raw.get(ahead))
        else:
            keep, send = attend_slot(queries, keys, values, state=state, w_out=w_o)
    half = keep.shape[1]
    pair_sum = (keep.astype(F32) + exchange(send, "grid", 1).astype(F32)).astype(BF16)
    middle = own_even.astype(F32) + pair_sum.astype(F32)
    for a in range(1, grid // CORES):
        theirs = exchange(pair_sum, "grid", CORES * a).astype(F32)
        middle = middle + jnp.concatenate(
            [theirs[:, (k ^ a) * width : (k ^ a) * width + width] for k in range(grid // CORES)], axis=1
        )
    middle = middle.astype(BF16)
    gated = gated_units(
        place, order, middle, exchange(middle, "grid", 1), norm2, w_glu_value, w_glu_gate
    )
    left, right = halo_rows(gated)
    keep, send = conv_project(gated, left, right, taps, bn, w_p)
    pair_sum = keep.astype(F32) + exchange(send, "grid", 1).astype(F32)
    result = middle[:, :width].astype(F32) + pair_sum[:, :width]
    for a in range(1, grid // CORES):
        share = pair_sum[:, a * width : (a + 1) * width].astype(BF16)
        result = result + exchange(share, "grid", CORES * a).astype(F32)
    return result.astype(BF16)


def solution(mesh):
    return jax.shard_map(
        on_device,
        mesh=mesh,
        in_specs=(
            P(("parts", "ctx"), "grid"),
            P("grid"),
            P("grid"),
            P(None, "grid"),
            P(None, "grid"),
            P(None, "grid"),
            P("grid", None),
            P("grid"),
            P("grid"),
            P(None, "grid"),
            P(None, "grid"),
            P(None, "grid"),
            P("grid"),
            P("grid"),
            P("grid", None),
        ),
        out_specs=P(("parts", "ctx"), "grid"),
        check_vma=False,
    )
```

```python
import functools
import math

import jax
import jax.numpy as jnp
from jax import lax
from jax.experimental import pallas as pl
from jax.experimental.pallas import tpu as pltpu
from jax.sharding import PartitionSpec as P

HEAD_DIM = 64
PAIR = 2 * HEAD_DIM
KERNEL = 31
HALF = 15
HALO = 16
EPSILON = 1e-05
CORES = 2
VMEM_BYTES = 40 * 1024 * 1024
BF16 = jnp.bfloat16
F32 = jnp.float32
SCORE_SCALE = math.log2(math.e) / math.sqrt(HEAD_DIM)


def exchange(cells, axis, distance):
    count = lax.axis_size(axis)
    return lax.ppermute(cells, axis, [(i, i ^ distance) for i in range(count)])


def kernel_call(body, outs, operands, spaces=None, scratch=(), aliases=None):
    spaces = spaces or {}
    in_specs = [
        pl.BlockSpec(memory_space=spaces.get(i, pltpu.VMEM)) for i in range(len(operands))
    ]
    return pl.pallas_call(
        body,
        in_specs=in_specs,
        out_specs=tuple(pl.BlockSpec(memory_space=pltpu.VMEM) for _ in outs),
        out_shape=tuple(jax.ShapeDtypeStruct(shape, dtype) for shape, dtype in outs),
        scratch_shapes=list(scratch),
        input_output_aliases=aliases or {},
        compiler_params=pltpu.CompilerParams(vmem_limit_bytes=VMEM_BYTES),
        cost_estimate=pl.CostEstimate(flops=1000, bytes_accessed=1000, transcendentals=0),
    )(*operands)


def after(cells, *done):
    def body(*refs):
        pass

    anywhere = pl.BlockSpec(memory_space=pl.ANY)
    return pl.pallas_call(
        body,
        in_specs=[anywhere] * (1 + len(done)),
        out_specs=anywhere,
        out_shape=jax.ShapeDtypeStruct(cells.shape, cells.dtype),
        input_output_aliases={0: 0},
        cost_estimate=pl.CostEstimate(flops=0, bytes_accessed=0, transcendentals=0),
    )(cells, *done)


def fold_kernel(order, which, count, me_ref, *refs):
    gains, weights, (folded_ref, sums_ref) = refs[: len(order)], refs[len(order) : -2], refs[-2:]
    width = gains[0].shape[1]
    columns = weights[0].shape[1]
    rows = math.gcd(width, 64)
    bias_parts = [[] for _ in weights]
    for k, r in enumerate(order):
        gain = gains[k][which : which + 1, :].astype(F32)
        gain = jnp.transpose(jnp.broadcast_to(gain, (PAIR, width)))
        bias = jnp.broadcast_to(gains[k][which + 1 : which + 2, :].astype(F32), (8, width)).astype(BF16)
        start = pl.multiple_of((me_ref[0] ^ r) * width, width)
        for n, ref in enumerate(weights):
            block = ref[pl.ds(start, width), :]
            bias_parts[n].append(jnp.dot(bias, block, preferred_element_type=F32))
            for j in range(columns // PAIR):
                target = (j * count + n) * PAIR
                product = block[:, j * PAIR : (j + 1) * PAIR].astype(F32) * gain
                folded_ref[k * width : (k + 1) * width, target : target + PAIR] = product.astype(BF16)
    sums = jnp.dot(jnp.ones((8, folded_ref.shape[0]), BF16), folded_ref[...], preferred_element_type=F32)
    sums_ref[0:1, :] = sums[0:1]
    for n, parts in enumerate(bias_parts):
        total = sum(parts)
        for j in range(columns // PAIR):
            target = (j * count + n) * PAIR
            sums_ref[1:2, target : target + PAIR] = total[0:1, j * PAIR : (j + 1) * PAIR]


def folded(me, order, which, gains, weights):
    rows, columns = weights[0].shape
    total = columns * len(weights)
    return kernel_call(
        functools.partial(fold_kernel, order, which, len(weights)),
        [((rows, total), BF16), ((2, total), F32)],
        [me, *gains, *weights],
        spaces={0: pltpu.SMEM},
    )


def row_statistics(refs):
    rows, width = refs[0].shape
    full = width * len(refs)
    means, scales = [], []
    step = math.gcd(rows, 64)
    for start in range(0, rows, step):
        parts = [ref[start : start + step, :].astype(F32) for ref in refs]
        mean = sum(jnp.sum(part, axis=1, keepdims=True) for part in parts) / full
        variance = sum(jnp.sum(jnp.square(part - mean), axis=1, keepdims=True) for part in parts) / full
        means.append(mean)
        scales.append(lax.rsqrt(variance + EPSILON))
    return jnp.concatenate(means, axis=0), jnp.concatenate(scales, axis=0)


def norm_product(cells, mean, scale, folded_ref, sums_ref, start, columns):
    cols = slice(start, start + columns)
    product = jnp.dot(cells, folded_ref[:, cols], preferred_element_type=F32)
    return (product - mean * sums_ref[0:1, cols]) * scale + sums_ref[1:2, cols]


def lane_masks():
    lanes = lax.broadcasted_iota(jnp.int32, (1, PAIR), 1)
    return lanes < HEAD_DIM


def keys_values(projected):
    low = lane_masks()
    values = projected[:, PAIR : 2 * PAIR]
    return (
        projected[:, :PAIR].astype(BF16),
        jnp.where(low, values, 1.0).astype(BF16),
        jnp.where(low, 1.0, values).astype(BF16),
    )


def project_kernel(count, *refs):
    blocks, (folded_ref, sums_ref, _, query_ref, key_ref, value_ref) = refs[:count], refs[count:]
    mean, scale = row_statistics(blocks)
    cells = jnp.concatenate([ref[...] for ref in blocks], axis=1)
    low = lane_masks()
    for j in range(key_ref.shape[1] // PAIR):
        projected = norm_product(cells, mean, scale, folded_ref, sums_ref, j * 3 * PAIR, 3 * PAIR)
        keys, low_values, high_values = keys_values(projected)
        queries = projected[:, 2 * PAIR :] * SCORE_SCALE
        base = 2 * j * PAIR
        key_ref[:, j * PAIR : (j + 1) * PAIR] = keys
        value_ref[:, base : base + PAIR] = low_values
        value_ref[:, base + PAIR : base + 2 * PAIR] = high_values
        query_ref[:, base : base + PAIR] = jnp.where(low, queries, 0.0).astype(BF16)
        query_ref[:, base + PAIR : base + 2 * PAIR] = jnp.where(low, 0.0, queries).astype(BF16)


def attend_pair(pair, query_rows, query_ref, keys, values, old_ref, state_ref, attended_ref):
    total = query_ref.shape[0]
    for start in range(0, total, query_rows):
        rows = slice(start, start + query_rows)
        finished = []
        for head in range(2):
            index = 2 * pair + head
            queries = query_ref[rows, index * PAIR : (index + 1) * PAIR]
            sums = slice(2 * index * PAIR, (2 * index + 1) * PAIR)
            peaks = slice((2 * index + 1) * PAIR, (2 * index + 2) * PAIR)
            scores = lax.dot_general(
                queries, keys, (((1,), (1,)), ((), ())), preferred_element_type=F32
            )
            peak = jnp.max(scores, axis=1, keepdims=True)
            if old_ref is not None:
                peak = jnp.maximum(jnp.broadcast_to(peak, (query_rows, PAIR)), old_ref[rows, peaks])
                wide = jnp.concatenate([peak] * (scores.shape[1] // PAIR), axis=1)
            else:
                wide = peak
                peak = jnp.broadcast_to(peak, (query_rows, PAIR))
            soft = jnp.exp2(scores - wide).astype(BF16)
            state = jnp.dot(soft, values[head], preferred_element_type=F32)
            if old_ref is not None:
                state = old_ref[rows, sums] * jnp.exp2(old_ref[rows, peaks] - peak) + state
            if attended_ref is None:
                state_ref[rows, sums] = state
                state_ref[rows, peaks] = peak
            else:
                lane = HEAD_DIM if head == 0 else 0
                finished.append(state / state[:, lane : lane + 1])
        if attended_ref is not None:
            cols = slice(pair * PAIR, (pair + 1) * PAIR)
            attended_ref[rows, cols] = jnp.where(lane_masks(), *finished).astype(BF16)


def first_kernel(query_rows, query_ref, key_ref, value_ref, _, state_ref, token_ref):
    token_ref[...] = jnp.zeros_like(token_ref)
    for j in range(key_ref.shape[1] // PAIR):
        values = [value_ref[:, n * PAIR : (n + 1) * PAIR] for n in (2 * j, 2 * j + 1)]
        attend_pair(
            j, query_rows, query_ref, key_ref[:, j * PAIR : (j + 1) * PAIR], values, None, state_ref, None
        )


def slot_kernel(count, last, query_rows, *refs):
    blocks, (folded_ref, sums_ref, query_ref, old_ref, *refs) = refs[:count], refs[count:]
    if last:
        out_w_ref, keep_ref, send_ref, attended = refs
        state_ref = None
    else:
        _, state_ref, token_ref = refs
        token_ref[...] = jnp.zeros_like(token_ref)
        attended = None
    mean, scale = row_statistics(blocks)
    cells = jnp.concatenate([ref[...] for ref in blocks], axis=1)
    for j in range(query_ref.shape[1] // (2 * PAIR)):
        projected = norm_product(cells, mean, scale, folded_ref, sums_ref, j * 3 * PAIR, 2 * PAIR)
        keys, *values = keys_values(projected)
        attend_pair(j, query_rows, query_ref, keys, values, old_ref, state_ref, attended)
    if last:
        half = keep_ref.shape[1]
        share = attended[...]
        keep_ref[...] = jnp.dot(share, out_w_ref[:, :half], preferred_element_type=F32).astype(BF16)
        send_ref[...] = jnp.dot(share, out_w_ref[:, half:], preferred_element_type=F32).astype(BF16)


def glu_kernel(even_ref, odd_ref, folded_ref, sums_ref, out_ref, head_ref, tail_ref):
    mean, scale = row_statistics((even_ref, odd_ref))
    cells = jnp.concatenate([even_ref[...], odd_ref[...]], axis=1)
    for j in range(out_ref.shape[1] // PAIR):
        both = norm_product(cells, mean, scale, folded_ref, sums_ref, j * 2 * PAIR, 2 * PAIR)
        out_ref[:, j * PAIR : (j + 1) * PAIR] = (
            both[:, :PAIR] / (1.0 + jnp.exp(-both[:, PAIR:]))
        ).astype(BF16)
    frames = out_ref.shape[0]
    head_ref[...] = out_ref[:HALO, :]
    tail_ref[...] = out_ref[frames - HALO :, :]


def conv_kernel(gated_ref, left_ref, right_ref, taps_ref, bn_ref, w_ref, keep_ref, send_ref, padded, activated):
    total, width = gated_ref.shape
    half = keep_ref.shape[1]
    piece = 32
    padded[0:HALO, :] = left_ref[...].astype(F32)
    padded[HALO : HALO + total, :] = gated_ref[...].astype(F32)
    padded[HALO + total :, :] = right_ref[...].astype(F32)
    for col in range(0, width, PAIR):
        cols = slice(col, col + PAIR)
        taps = [taps_ref[j : j + 1, cols] for j in range(KERNEL)]
        scale, shift = bn_ref[0:1, cols], bn_ref[1:2, cols]

        def block(index, carry):
            start = pl.multiple_of(index * piece, piece)
            window = padded[pl.ds(start, piece + 2 * HALO), cols]
            convolved = None
            for residue in range(8):
                part = None
                for offset in range(residue, KERNEL + 1, 8):
                    if offset == 0:
                        continue
                    base = offset - residue
                    term = taps[offset - 1] * window[base : base + piece + 8]
                    part = term if part is None else part + term
                part = part[residue : residue + piece]
                convolved = part if convolved is None else convolved + part
            value = convolved * scale + shift
            activated[pl.ds(start, piece), cols] = (value / (1.0 + jnp.exp(-value))).astype(BF16)
            return carry

        lax.fori_loop(0, total // piece, block, 0, unroll=2)
    share = activated[...]
    keep_ref[...] = jnp.dot(share, w_ref[:, :half], preferred_element_type=F32).astype(BF16)
    send_ref[...] = jnp.dot(share, w_ref[:, half:], preferred_element_type=F32).astype(BF16)


def pad_columns(weight, width):
    if weight.shape[1] == width:
        return weight
    return jnp.pad(weight, ((0, 0), (0, width - weight.shape[1])))


def on_device(
    frames_in,
    norm1_gain,
    norm1_bias,
    w_query,
    w_key,
    w_value,
    w_out,
    norm2_gain,
    norm2_bias,
    w_glu_value,
    w_glu_gate,
    depth_kernel,
    bn_scale,
    bn_shift,
    w_proj,
):
    frames, width = frames_in.shape
    grid, ctx = lax.axis_size("grid"), lax.axis_size("ctx")
    me = lax.axis_index("grid")
    place = me.astype(jnp.int32).reshape(1)
    order = list(range(0, grid, CORES)) + list(range(1, grid, CORES))
    padded = -(-width // PAIR) * PAIR
    query_rows = math.gcd(frames, 256)

    def by_distance(cells):
        return jnp.concatenate(
            [lax.dynamic_slice_in_dim(cells, (me ^ r) * width, width, 1) for r in order], axis=1
        )

    def over_chips(block):
        return [exchange(block, "grid", CORES * a) for a in range(1, grid // CORES)]

    def other_core(blocks):
        return [exchange(block, "grid", 1) for block in blocks]

    steps = [1 << k for k in range(ctx.bit_length() - 1)]
    raw = {0: frames_in}
    chips = {0: over_chips(frames_in)}
    for distance in steps:
        raw[distance] = exchange(frames_in, "ctx", distance)
    gains = jnp.pad(
        jnp.stack([norm1_gain, norm1_bias, norm2_gain, norm2_bias]), ((0, 12), (0, 0))
    )
    gains = [gains] + over_chips(gains)
    gains = gains + other_core(gains)

    w_query, w_key, w_value, w_glu_value, w_glu_gate = (
        pad_columns(weight, padded) for weight in (w_query, w_key, w_value, w_glu_value, w_glu_gate)
    )
    row_pad = ((0, padded - width), (0, 0))
    w_o = jnp.pad(by_distance(w_out), row_pad)
    w_p = jnp.pad(by_distance(w_proj), row_pad)
    taps = pad_columns(depth_kernel, padded)
    bn = pad_columns(jnp.stack([bn_scale, bn_shift]), padded)
    qkv, qkv_sums = folded(place, order, 0, gains, (w_key, w_value, w_query))
    chips[0] = [after(block, qkv_sums) for block in chips[0]]
    raw[1] = after(raw[1], qkv_sums)
    glu, glu_sums = folded(place, order, 2, gains, (w_glu_value, w_glu_gate))

    state_shape = ((frames, 4 * padded), F32)
    token_shape = ((8, 128), F32)
    queries = state = own = token = None
    for s in range(ctx):
        if s == 1:
            chips[1] = over_chips(raw[1])
        mine = [raw[s]] + (chips[s] if s == 0 else [after(block, token) for block in chips[s]])
        blocks = mine + other_core(mine)
        ahead = s + 2
        if ahead < ctx:
            low = ahead & -ahead
            if ahead != low:
                raw[ahead] = exchange(raw[ahead ^ low], "ctx", low)
            chips[ahead] = over_chips(raw[ahead])
        behind = raw.get(ahead, raw[0])
        if s == 0:
            own = mine
            n = len(blocks)
            queries, keys, values = kernel_call(
                functools.partial(project_kernel, n),
                [((frames, 2 * padded), BF16), ((frames, padded), BF16), ((frames, 2 * padded), BF16)],
                [*blocks, qkv, qkv_sums, raw[1]],
                spaces={n + 2: pl.ANY},
            )
            state, token = kernel_call(
                functools.partial(first_kernel, query_rows),
                [state_shape, token_shape],
                [queries, keys, values, behind],
                spaces={3: pl.ANY},
            )
        elif s < ctx - 1:
            state, token = kernel_call(
                functools.partial(slot_kernel, n, False, query_rows),
                [state_shape, token_shape],
                [*blocks, qkv, qkv_sums, queries, state, behind],
                spaces={n + 4: pl.ANY},
                aliases={n + 3: 0},
            )
        else:
            keep, send = kernel_call(
                functools.partial(slot_kernel, n, True, query_rows),
                [((frames, grid // CORES * width), BF16)] * 2,
                [*blocks, qkv, qkv_sums, queries, state, w_o],
                scratch=[pltpu.VMEM((frames, padded), BF16)],
            )
    pair_sum = (keep.astype(F32) + exchange(send, "grid", 1).astype(F32)).astype(BF16)
    middle = jnp.concatenate(own, axis=1).astype(F32) + pair_sum.astype(F32)
    for a in range(1, grid // CORES):
        theirs = exchange(pair_sum, "grid", CORES * a).astype(F32)
        middle = middle + jnp.concatenate(
            [theirs[:, (k ^ a) * width : (k ^ a) * width + width] for k in range(grid // CORES)], axis=1
        )
    middle = middle.astype(BF16)
    gated, head, tail = kernel_call(
        glu_kernel,
        [((frames, padded), BF16), ((HALO, padded), BF16), ((HALO, padded), BF16)],
        [middle, exchange(middle, "grid", 1), glu, glu_sums],
    )
    left = lax.ppermute(tail, "ctx", [(i, i + 1) for i in range(ctx - 1)])
    right = lax.ppermute(head, "ctx", [(i + 1, i) for i in range(ctx - 1)])
    keep, send = kernel_call(
        conv_kernel,
        [((frames, grid // CORES * width), BF16)] * 2,
        [gated, left, right, taps, bn, w_p],
        scratch=[pltpu.VMEM((frames + 2 * HALO, padded), F32), pltpu.VMEM((frames, padded), BF16)],
    )
    pair_sum = keep.astype(F32) + exchange(send, "grid", 1).astype(F32)
    result = middle[:, :width].astype(F32) + pair_sum[:, :width]
    for a in range(1, grid // CORES):
        share = pair_sum[:, a * width : (a + 1) * width].astype(BF16)
        result = result + exchange(share, "grid", CORES * a).astype(F32)
    return result.astype(BF16)


def solution(mesh):
    return jax.shard_map(
        on_device,
        mesh=mesh,
        in_specs=(
            P(("parts", "ctx"), "grid"),
            P("grid"),
            P("grid"),
            P(None, "grid"),
            P(None, "grid"),
            P(None, "grid"),
            P("grid", None),
            P("grid"),
            P("grid"),
            P(None, "grid"),
            P(None, "grid"),
            P(None, "grid"),
            P("grid"),
            P("grid"),
            P("grid", None),
        ),
        out_specs=P(("parts", "ctx"), "grid"),
        check_vma=False,
    )
```

```python
import functools
import math

import jax
import jax.numpy as jnp
from jax import lax
from jax.experimental import pallas as pl
from jax.experimental.pallas import tpu as pltpu
from jax.sharding import PartitionSpec as P

HEAD_DIM = 64
PAIR = 2 * HEAD_DIM
KERNEL = 31
HALF = 15
HALO = 16
EPSILON = 1e-05
CORES = 2
VMEM_BYTES = 12 * 1024 * 1024
BF16 = jnp.bfloat16
F32 = jnp.float32
SCORE_SCALE = math.log2(math.e) / math.sqrt(HEAD_DIM)


def exchange(cells, axis, distance):
    count = lax.axis_size(axis)
    return lax.ppermute(cells, axis, [(i, i ^ distance) for i in range(count)])


def kernel_call(body, outs, operands, spaces=None, scratch=(), aliases=None):
    spaces = spaces or {}
    in_specs = [
        pl.BlockSpec(memory_space=spaces.get(i, pltpu.VMEM)) for i in range(len(operands))
    ]
    return pl.pallas_call(
        body,
        in_specs=in_specs,
        out_specs=tuple(pl.BlockSpec(memory_space=pltpu.VMEM) for _ in outs),
        out_shape=tuple(jax.ShapeDtypeStruct(shape, dtype) for shape, dtype in outs),
        scratch_shapes=list(scratch),
        input_output_aliases=aliases or {},
        compiler_params=pltpu.CompilerParams(vmem_limit_bytes=VMEM_BYTES),
        cost_estimate=pl.CostEstimate(flops=1000, bytes_accessed=1000, transcendentals=0),
    )(*operands)


def after(cells, *done):
    def body(*refs):
        pass

    anywhere = pl.BlockSpec(memory_space=pl.ANY)
    return pl.pallas_call(
        body,
        in_specs=[anywhere] * (1 + len(done)),
        out_specs=anywhere,
        out_shape=jax.ShapeDtypeStruct(cells.shape, cells.dtype),
        input_output_aliases={0: 0},
        compiler_params=pltpu.CompilerParams(vmem_limit_bytes=64 * 1024),
        cost_estimate=pl.CostEstimate(flops=0, bytes_accessed=0, transcendentals=0),
    )(cells, *done)


def fold_kernel(order, which, me_ref, *refs):
    gains, weights, (folded_ref, sums_ref) = refs[: len(order)], refs[len(order) : -2], refs[-2:]
    width = gains[0].shape[1]
    products = [[] for _ in weights]
    for k, r in enumerate(order):
        gain = jnp.transpose(jnp.broadcast_to(gains[k][which : which + 1, :], (PAIR, width)))
        bias = jnp.broadcast_to(gains[k][which + 1 : which + 2, :], (8, width)).astype(BF16)
        start = pl.multiple_of((me_ref[0] ^ r) * width, width)
        for n, ref in enumerate(weights):
            block = ref[pl.ds(start, width), :]
            products[n].append(jnp.dot(bias, block, preferred_element_type=F32))
            folded_ref[k * width : (k + 1) * width, n * PAIR : (n + 1) * PAIR] = (
                block.astype(F32) * gain
            ).astype(BF16)
    sums = jnp.dot(jnp.ones((8, folded_ref.shape[0]), BF16), folded_ref[...], preferred_element_type=F32)
    sums_ref[0:1, :] = sums[0:1]
    for n, parts in enumerate(products):
        sums_ref[1:2, n * PAIR : (n + 1) * PAIR] = sum(parts)[0:1]


def folded(me, order, which, gains, weights):
    rows, columns = weights[0].shape
    total = PAIR * len(weights)
    inside = pl.BlockSpec(memory_space=pltpu.VMEM)
    return pl.pallas_call(
        functools.partial(fold_kernel, order, which),
        grid=(columns // PAIR,),
        in_specs=[
            pl.BlockSpec(memory_space=pltpu.SMEM),
            *[inside] * len(gains),
            *[pl.BlockSpec((rows, PAIR), lambda j: (0, j))] * len(weights),
        ],
        out_specs=(
            pl.BlockSpec((rows, total), lambda j: (0, j)),
            pl.BlockSpec((2, total), lambda j: (0, j)),
        ),
        out_shape=(
            jax.ShapeDtypeStruct((rows, columns * len(weights)), BF16),
            jax.ShapeDtypeStruct((2, columns * len(weights)), F32),
        ),
        compiler_params=pltpu.CompilerParams(vmem_limit_bytes=VMEM_BYTES),
        cost_estimate=pl.CostEstimate(flops=1000, bytes_accessed=1000, transcendentals=0),
    )(me, *gains, *weights)


def stack_kernel(*refs):
    rows, out_ref = refs[:-1], refs[-1]
    out_ref[...] = jnp.zeros_like(out_ref)
    for i, ref in enumerate(rows):
        out_ref[i : i + 1, :] = ref[...].astype(F32).reshape(1, ref.shape[0])


def reorder_kernel(order, me_ref, *refs):
    half = len(refs) // 2
    width = refs[0].shape[1] // len(order)
    for source, target in zip(refs[:half], refs[half:]):
        for k, r in enumerate(order):
            cols = pl.ds(pl.multiple_of((me_ref[0] ^ r) * width, PAIR), width)
            target[:, k * width : (k + 1) * width] = source[:, cols]


def row_statistics(refs):
    rows, width = refs[0].shape
    full = width * len(refs)
    means, scales = [], []
    step = math.gcd(rows, 64)
    for start in range(0, rows, step):
        parts = [ref[start : start + step, :].astype(F32) for ref in refs]
        mean = sum(jnp.sum(part, axis=1, keepdims=True) for part in parts) / full
        variance = sum(jnp.sum(jnp.square(part - mean), axis=1, keepdims=True) for part in parts) / full
        means.append(mean)
        scales.append(lax.rsqrt(variance + EPSILON))
    return jnp.concatenate(means, axis=0), jnp.concatenate(scales, axis=0)


def norm_product(cells, mean, scale, folded_ref, sums_ref, start, columns):
    cols = slice(start, start + columns)
    product = jnp.dot(cells, folded_ref[:, cols], preferred_element_type=F32)
    return (product - mean * sums_ref[0:1, cols]) * scale + sums_ref[1:2, cols]


def lane_masks():
    lanes = lax.broadcasted_iota(jnp.int32, (1, PAIR), 1)
    return lanes < HEAD_DIM


def keys_values(projected):
    low = lane_masks()
    values = projected[:, PAIR : 2 * PAIR]
    return (
        projected[:, :PAIR].astype(BF16),
        jnp.where(low, values, 1.0).astype(BF16),
        jnp.where(low, 1.0, values).astype(BF16),
    )


def project_kernel(count, *refs):
    blocks, (folded_ref, sums_ref), (query_ref, key_ref, value_ref) = refs[:count], refs[count : count + 2], refs[-3:]
    mean, scale = row_statistics(blocks)
    cells = jnp.concatenate([ref[...] for ref in blocks], axis=1)
    low = lane_masks()
    for j in range(key_ref.shape[1] // PAIR):
        projected = norm_product(cells, mean, scale, folded_ref, sums_ref, j * 3 * PAIR, 3 * PAIR)
        keys, low_values, high_values = keys_values(projected)
        queries = projected[:, 2 * PAIR :] * SCORE_SCALE
        base = 2 * j * PAIR
        key_ref[:, j * PAIR : (j + 1) * PAIR] = keys
        value_ref[:, base : base + PAIR] = low_values
        value_ref[:, base + PAIR : base + 2 * PAIR] = high_values
        query_ref[:, base : base + PAIR] = jnp.where(low, queries, 0.0).astype(BF16)
        query_ref[:, base + PAIR : base + 2 * PAIR] = jnp.where(low, 0.0, queries).astype(BF16)


def attend_pair(pair, query_rows, query_ref, keys, values, state_ref):
    total = query_ref.shape[0]
    for start in range(0, total, query_rows):
        rows = slice(start, start + query_rows)
        for head in range(2):
            index = 2 * pair + head
            queries = query_ref[rows, index * PAIR : (index + 1) * PAIR]
            scores = lax.dot_general(
                queries, keys, (((1,), (1,)), ((), ())), preferred_element_type=F32
            )
            peak = jnp.max(scores, axis=1, keepdims=True)
            soft = jnp.exp2(scores - peak).astype(BF16)
            sums = jnp.dot(soft, values[head], preferred_element_type=F32)
            state_ref[rows, 2 * index * PAIR : (2 * index + 1) * PAIR] = sums
            state_ref[rows, (2 * index + 1) * PAIR : (2 * index + 2) * PAIR] = jnp.broadcast_to(
                peak, (query_rows, PAIR)
            )


def merge_head(old_ref, part_ref, rows, index):
    sums = slice(2 * index * PAIR, (2 * index + 1) * PAIR)
    peaks = slice((2 * index + 1) * PAIR, (2 * index + 2) * PAIR)
    old_peak, part_peak = old_ref[rows, peaks], part_ref[rows, peaks]
    peak = jnp.maximum(old_peak, part_peak)
    total = old_ref[rows, sums] * jnp.exp2(old_peak - peak) + part_ref[rows, sums] * jnp.exp2(part_peak - peak)
    return total, peak


def first_kernel(query_rows, query_ref, key_ref, value_ref, _, state_ref, token_ref):
    token_ref[...] = jnp.zeros_like(token_ref)
    for j in range(key_ref.shape[1] // PAIR):
        values = [value_ref[:, n * PAIR : (n + 1) * PAIR] for n in (2 * j, 2 * j + 1)]
        attend_pair(j, query_rows, query_ref, key_ref[:, j * PAIR : (j + 1) * PAIR], values, state_ref)


def slot_kernel(count, last, query_rows, *refs):
    blocks, (folded_ref, sums_ref, query_ref, old_ref, *refs) = refs[:count], refs[count:]
    if last:
        out_w_ref, keep_ref, send_ref, part, attended = refs
    else:
        _, state_ref, token_ref, part = refs
        token_ref[...] = jnp.zeros_like(token_ref)
    mean, scale = row_statistics(blocks)
    cells = jnp.concatenate([ref[...] for ref in blocks], axis=1)
    pairs = query_ref.shape[1] // (2 * PAIR)
    for j in range(pairs):
        projected = norm_product(cells, mean, scale, folded_ref, sums_ref, j * 3 * PAIR, 2 * PAIR)
        keys, *values = keys_values(projected)
        attend_pair(j, query_rows, query_ref, keys, values, part)
    total = query_ref.shape[0]
    low = lane_masks()
    for start in range(0, total, query_rows):
        rows = slice(start, start + query_rows)
        for j in range(pairs):
            heads = [merge_head(old_ref, part, rows, 2 * j + head) for head in range(2)]
            if last:
                (one, _), (two, _) = heads
                both = jnp.where(low, one, two)
                weight = pltpu.roll(jnp.where(low, two, one), HEAD_DIM, 1)
                attended[rows, j * PAIR : (j + 1) * PAIR] = (both / weight).astype(BF16)
            else:
                for head, (sums, peak) in enumerate(heads):
                    at = 2 * (2 * j + head) * PAIR
                    state_ref[rows, at : at + PAIR] = sums
                    state_ref[rows, at + PAIR : at + 2 * PAIR] = peak
    if last:
        half = keep_ref.shape[1]
        share = attended[...]
        keep_ref[...] = jnp.dot(share, out_w_ref[:, :half], preferred_element_type=F32).astype(BF16)
        send_ref[...] = jnp.dot(share, out_w_ref[:, half:], preferred_element_type=F32).astype(BF16)


def glu_kernel(even_ref, odd_ref, folded_ref, sums_ref, out_ref, head_ref, tail_ref):
    mean, scale = row_statistics((even_ref, odd_ref))
    cells = jnp.concatenate([even_ref[...], odd_ref[...]], axis=1)
    for j in range(out_ref.shape[1] // PAIR):
        both = norm_product(cells, mean, scale, folded_ref, sums_ref, j * 2 * PAIR, 2 * PAIR)
        out_ref[:, j * PAIR : (j + 1) * PAIR] = (
            both[:, :PAIR] / (1.0 + jnp.exp(-both[:, PAIR:]))
        ).astype(BF16)
    frames = out_ref.shape[0]
    head_ref[...] = out_ref[:HALO, :]
    tail_ref[...] = out_ref[frames - HALO :, :]


def conv_kernel(gated_ref, left_ref, right_ref, taps_ref, bn_ref, w_ref, keep_ref, send_ref, padded, activated):
    total, width = gated_ref.shape
    half = keep_ref.shape[1]
    piece = 32
    padded[0:HALO, :] = left_ref[...].astype(F32)
    padded[HALO : HALO + total, :] = gated_ref[...].astype(F32)
    padded[HALO + total :, :] = right_ref[...].astype(F32)
    for col in range(0, width, PAIR):
        cols = slice(col, col + PAIR)
        taps = [taps_ref[j : j + 1, cols] for j in range(KERNEL)]
        scale, shift = bn_ref[0:1, cols], bn_ref[1:2, cols]

        def block(index, carry):
            start = pl.multiple_of(index * piece, piece)
            window = padded[pl.ds(start, piece + 2 * HALO), cols]
            convolved = None
            for residue in range(8):
                part = None
                for offset in range(residue, KERNEL + 1, 8):
                    if offset == 0:
                        continue
                    base = offset - residue
                    term = taps[offset - 1] * window[base : base + piece + 8]
                    part = term if part is None else part + term
                part = part[residue : residue + piece]
                convolved = part if convolved is None else convolved + part
            value = convolved * scale + shift
            activated[pl.ds(start, piece), cols] = (value / (1.0 + jnp.exp(-value))).astype(BF16)
            return carry

        lax.fori_loop(0, total // piece, block, 0, unroll=2)
    share = activated[...]
    keep_ref[...] = jnp.dot(share, w_ref[:, :half], preferred_element_type=F32).astype(BF16)
    send_ref[...] = jnp.dot(share, w_ref[:, half:], preferred_element_type=F32).astype(BF16)


def pad_columns(weight, width):
    if weight.shape[1] == width:
        return weight
    return jnp.pad(weight, ((0, 0), (0, width - weight.shape[1])))


def on_device(
    frames_in,
    norm1_gain,
    norm1_bias,
    w_query,
    w_key,
    w_value,
    w_out,
    norm2_gain,
    norm2_bias,
    w_glu_value,
    w_glu_gate,
    depth_kernel,
    bn_scale,
    bn_shift,
    w_proj,
):
    frames, width = frames_in.shape
    grid, ctx = lax.axis_size("grid"), lax.axis_size("ctx")
    me = lax.axis_index("grid")
    place = me.astype(jnp.int32).reshape(1)
    order = list(range(0, grid, CORES)) + list(range(1, grid, CORES))
    padded = -(-width // PAIR) * PAIR
    query_rows = math.gcd(frames, 256)

    def by_distance(cells):
        return jnp.concatenate(
            [lax.dynamic_slice_in_dim(cells, (me ^ r) * width, width, 1) for r in order], axis=1
        )

    def over_chips(block):
        return [exchange(block, "grid", CORES * a) for a in range(1, grid // CORES)]

    def other_core(blocks):
        return [exchange(block, "grid", 1) for block in blocks]

    steps = [1 << k for k in range(ctx.bit_length() - 1)]
    raw = {0: frames_in}
    chips = {0: over_chips(frames_in)}
    for distance in steps:
        raw[distance] = exchange(frames_in, "ctx", distance)
    gains = pl.pallas_call(
        stack_kernel,
        out_shape=jax.ShapeDtypeStruct((8, width), F32),
        compiler_params=pltpu.CompilerParams(vmem_limit_bytes=1024 * 1024),
        cost_estimate=pl.CostEstimate(flops=1000, bytes_accessed=1000, transcendentals=0),
    )(norm1_gain, norm1_bias, norm2_gain, norm2_bias)
    gains = [gains] + over_chips(gains)
    gains = gains + other_core(gains)

    w_query, w_key, w_value, w_glu_value, w_glu_gate = (
        pad_columns(weight, padded) for weight in (w_query, w_key, w_value, w_glu_value, w_glu_gate)
    )
    if width % PAIR:
        row_pad = ((0, padded - width), (0, 0))
        w_o, w_p = (jnp.pad(by_distance(weight), row_pad) for weight in (w_out, w_proj))
    else:
        w_o, w_p = kernel_call(
            functools.partial(reorder_kernel, order),
            [(w_out.shape, BF16), (w_proj.shape, BF16)],
            [place, w_out, w_proj],
            spaces={0: pltpu.SMEM},
        )
    taps = pad_columns(depth_kernel, padded)
    bn = pad_columns(jnp.stack([bn_scale, bn_shift]), padded)
    qkv, qkv_sums = folded(place, order, 0, gains, (w_key, w_value, w_query))
    chips[0] = [after(block, qkv_sums) for block in chips[0]]
    glu, glu_sums = folded(place, order, 2, gains, (w_glu_value, w_glu_gate))

    raw.update({s: after(block, glu_sums) for s, block in raw.items() if s})
    state_shape = ((frames, 4 * padded), F32)
    token_shape = ((8, 128), F32)
    queries = state = own = token = None
    for s in range(ctx):
        if s == 1:
            chips[1] = over_chips(raw[1])
        mine = [raw[s]] + (chips[s] if s == 0 else [after(block, token) for block in chips[s]])
        blocks = mine + other_core(mine)
        ahead = s + 2
        if ahead < ctx:
            low = ahead & -ahead
            if ahead != low:
                raw[ahead] = exchange(raw[ahead ^ low], "ctx", low)
            chips[ahead] = over_chips(raw[ahead])
        behind = raw.get(ahead, raw[0])
        if s == 0:
            own = mine
            n = len(blocks)
            early = [raw[s] for s in steps]
            queries, keys, values = kernel_call(
                functools.partial(project_kernel, n),
                [((frames, 2 * padded), BF16), ((frames, padded), BF16), ((frames, 2 * padded), BF16)],
                [*blocks, qkv, qkv_sums, *early],
                spaces={n + 2 + i: pl.ANY for i in range(len(early))},
            )
            state, token = kernel_call(
                functools.partial(first_kernel, query_rows),
                [state_shape, token_shape],
                [queries, keys, values, behind],
                spaces={3: pl.ANY},
            )
        elif s < ctx - 1:
            state, token = kernel_call(
                functools.partial(slot_kernel, n, False, query_rows),
                [state_shape, token_shape],
                [*blocks, qkv, qkv_sums, queries, state, behind],
                spaces={n + 4: pl.ANY},
                aliases={n + 3: 0},
                scratch=[pltpu.VMEM(*state_shape)],
            )
        else:
            keep, send = kernel_call(
                functools.partial(slot_kernel, n, True, query_rows),
                [((frames, grid // CORES * width), BF16)] * 2,
                [*blocks, qkv, qkv_sums, queries, state, w_o],
                scratch=[pltpu.VMEM(*state_shape), pltpu.VMEM((frames, padded), BF16)],
            )
    pair_sum = (keep.astype(F32) + exchange(send, "grid", 1).astype(F32)).astype(BF16)
    middle = jnp.concatenate(own, axis=1).astype(F32) + pair_sum.astype(F32)
    for a in range(1, grid // CORES):
        theirs = exchange(pair_sum, "grid", CORES * a).astype(F32)
        middle = middle + jnp.concatenate(
            [theirs[:, (k ^ a) * width : (k ^ a) * width + width] for k in range(grid // CORES)], axis=1
        )
    middle = middle.astype(BF16)
    gated, head, tail = kernel_call(
        glu_kernel,
        [((frames, padded), BF16), ((HALO, padded), BF16), ((HALO, padded), BF16)],
        [middle, exchange(middle, "grid", 1), glu, glu_sums],
    )
    left = lax.ppermute(tail, "ctx", [(i, i + 1) for i in range(ctx - 1)])
    right = lax.ppermute(head, "ctx", [(i + 1, i) for i in range(ctx - 1)])
    keep, send = kernel_call(
        conv_kernel,
        [((frames, grid // CORES * width), BF16)] * 2,
        [gated, left, right, taps, bn, w_p],
        scratch=[pltpu.VMEM((frames + 2 * HALO, padded), F32), pltpu.VMEM((frames, padded), BF16)],
    )
    pair_sum = keep.astype(F32) + exchange(send, "grid", 1).astype(F32)
    result = middle[:, :width].astype(F32) + pair_sum[:, :width]
    for a in range(1, grid // CORES):
        share = pair_sum[:, a * width : (a + 1) * width].astype(BF16)
        result = result + exchange(share, "grid", CORES * a).astype(F32)
    return result.astype(BF16)


def solution(mesh):
    return jax.shard_map(
        on_device,
        mesh=mesh,
        in_specs=(
            P(("parts", "ctx"), "grid"),
            P("grid"),
            P("grid"),
            P(None, "grid"),
            P(None, "grid"),
            P(None, "grid"),
            P("grid", None),
            P("grid"),
            P("grid"),
            P(None, "grid"),
            P(None, "grid"),
            P(None, "grid"),
            P("grid"),
            P("grid"),
            P("grid", None),
        ),
        out_specs=P(("parts", "ctx"), "grid"),
        check_vma=False,
    )
```

```python
import functools
import math

import jax
import jax.numpy as jnp
from jax import lax
from jax.experimental import pallas as pl
from jax.experimental.pallas import tpu as pltpu
from jax.sharding import PartitionSpec as P

HEAD_DIM = 64
PAIR = 2 * HEAD_DIM
KERNEL = 31
HALF = 15
HALO = 16
EPSILON = 1e-05
CORES = 2
VMEM_BYTES = 16 * 1024 * 1024
BF16 = jnp.bfloat16
F32 = jnp.float32
SCORE_SCALE = math.log2(math.e) / math.sqrt(HEAD_DIM)


def exchange(cells, axis, distance):
    count = lax.axis_size(axis)
    return lax.ppermute(cells, axis, [(i, i ^ distance) for i in range(count)])


def kernel_call(body, outs, operands, spaces=None, scratch=(), aliases=None):
    spaces = spaces or {}
    operands = [
        pltpu.with_memory_space_constraint(cells, pltpu.HBM) if spaces.get(i) == pltpu.HBM else cells
        for i, cells in enumerate(operands)
    ]
    in_specs = [
        pl.BlockSpec(memory_space=spaces.get(i, pltpu.VMEM)) for i in range(len(operands))
    ]
    return pl.pallas_call(
        body,
        in_specs=in_specs,
        out_specs=tuple(pl.BlockSpec(memory_space=pltpu.VMEM) for _ in outs),
        out_shape=tuple(jax.ShapeDtypeStruct(shape, dtype) for shape, dtype in outs),
        scratch_shapes=list(scratch),
        input_output_aliases=aliases or {},
        compiler_params=pltpu.CompilerParams(vmem_limit_bytes=VMEM_BYTES),
        cost_estimate=pl.CostEstimate(flops=1000, bytes_accessed=1000, transcendentals=0),
    )(*operands)


def after(cells, *done):
    def body(*refs):
        pass

    anywhere = pl.BlockSpec(memory_space=pl.ANY)
    return pl.pallas_call(
        body,
        in_specs=[anywhere] * (1 + len(done)),
        out_specs=anywhere,
        out_shape=jax.ShapeDtypeStruct(cells.shape, cells.dtype),
        input_output_aliases={0: 0},
        compiler_params=pltpu.CompilerParams(vmem_limit_bytes=64 * 1024),
        cost_estimate=pl.CostEstimate(flops=0, bytes_accessed=0, transcendentals=0),
    )(cells, *done)


def fold_kernel(order, which, count, me_ref, *refs):
    gains, refs = refs[: len(order)], refs[len(order) :]
    sources, (folded_ref, sums_ref), weights, done = refs[:count], refs[count : count + 2], refs[count + 2 : -1], refs[-1]
    copies = [pltpu.make_async_copy(sources[n], weights[n], done.at[n]) for n in range(count)]
    for copy in copies:
        copy.start()
    width = gains[0].shape[1]
    columns = weights[0].shape[1]
    factors = []
    for k in range(len(order)):
        gain = jnp.transpose(jnp.broadcast_to(gains[k][which : which + 1, :], (PAIR, width)))
        bias = jnp.broadcast_to(gains[k][which + 1 : which + 2, :], (8, width)).astype(BF16)
        factors.append((gain, bias))
    for n, ref in enumerate(weights):
        copies[n].wait()
        total = jnp.zeros((8, columns), F32)
        for k, r in enumerate(order):
            gain, bias = factors[k]
            start = pl.multiple_of((me_ref[0] ^ r) * width, width)
            block = ref[pl.ds(start, width), :]
            total = total + jnp.dot(bias, block, preferred_element_type=F32)
            for j in range(columns // PAIR):
                target = (j * count + n) * PAIR
                folded_ref[k * width : (k + 1) * width, target : target + PAIR] = (
                    block[:, j * PAIR : (j + 1) * PAIR].astype(F32) * gain
                ).astype(BF16)
        for j in range(columns // PAIR):
            target = (j * count + n) * PAIR
            sums_ref[1:2, target : target + PAIR] = total[0:1, j * PAIR : (j + 1) * PAIR]
    sums = jnp.dot(jnp.ones((8, folded_ref.shape[0]), BF16), folded_ref[...], preferred_element_type=F32)
    sums_ref[0:1, :] = sums[0:1]


def folded(me, order, which, gains, weights):
    rows, columns = weights[0].shape
    total = columns * len(weights)
    first = 1 + len(gains)
    spaces = {first + n: pltpu.HBM for n in range(len(weights))}
    return kernel_call(
        functools.partial(fold_kernel, order, which, len(weights)),
        [((rows, total), BF16), ((2, total), F32)],
        [me, *gains, *weights],
        spaces={0: pltpu.SMEM, **spaces},
        scratch=[pltpu.VMEM((rows, columns), BF16)] * len(weights) + [pltpu.SemaphoreType.DMA((len(weights),))],
    )


def stack_kernel(*refs):
    count = (len(refs) - 2) // 2
    sources, out_ref, rows, done = refs[:count], refs[count], refs[count + 1 : -1], refs[-1]
    copies = [pltpu.make_async_copy(sources[i], rows[i], done.at[i]) for i in range(count)]
    for copy in copies:
        copy.start()
    out_ref[...] = jnp.zeros_like(out_ref)
    for i, copy in enumerate(copies):
        copy.wait()
        out_ref[i : i + 1, :] = rows[i][...].astype(F32).reshape(1, out_ref.shape[1])


def reorder_kernel(order, me_ref, source_ref, out_ref, done):
    width = source_ref.shape[1] // len(order)
    copies = []
    for k, r in enumerate(order):
        cols = pl.ds(pl.multiple_of((me_ref[0] ^ r) * width, PAIR), width)
        copies.append(
            pltpu.make_async_copy(source_ref.at[:, cols], out_ref.at[:, k * width : (k + 1) * width], done.at[k])
        )
        copies[-1].start()
    for copy in copies:
        copy.wait()


def half_kernel(part_ref, source_ref, half_ref, done):
    rows = half_ref.shape[0]
    copy = pltpu.make_async_copy(
        source_ref.at[pl.ds(pl.multiple_of(part_ref[0] * rows, rows), rows), :], half_ref, done.at[0]
    )
    copy.start()
    copy.wait()


def row_statistics(refs):
    rows, width = refs[0].shape
    full = width * len(refs)
    means, scales = [], []
    step = math.gcd(rows, 64)
    for start in range(0, rows, step):
        parts = [ref[start : start + step, :].astype(F32) for ref in refs]
        mean = sum(jnp.sum(part, axis=1, keepdims=True) for part in parts) / full
        variance = sum(jnp.sum(jnp.square(part - mean), axis=1, keepdims=True) for part in parts) / full
        means.append(mean)
        scales.append(lax.rsqrt(variance + EPSILON))
    return jnp.concatenate(means, axis=0), jnp.concatenate(scales, axis=0)


def norm_product(cells, mean, scale, folded_ref, sums_ref, start, columns):
    cols = slice(start, start + columns)
    product = jnp.dot(cells, folded_ref[:, cols], preferred_element_type=F32)
    return (product - mean * sums_ref[0:1, cols]) * scale + sums_ref[1:2, cols]


def lane_masks():
    lanes = lax.broadcasted_iota(jnp.int32, (1, PAIR), 1)
    return lanes < HEAD_DIM


def keys_values(projected):
    low = lane_masks()
    values = projected[:, PAIR : 2 * PAIR]
    return (
        projected[:, :PAIR].astype(BF16),
        jnp.where(low, values, 1.0).astype(BF16),
        jnp.where(low, 1.0, values).astype(BF16),
    )


def project_kernel(count, *refs):
    blocks, (folded_ref, sums_ref), (query_ref, key_ref, value_ref) = refs[:count], refs[count : count + 2], refs[-4:-1]
    sent_ref = refs[-1]
    mean, scale = row_statistics(blocks)
    cells = jnp.concatenate([ref[...] for ref in blocks], axis=1)
    low = lane_masks()
    for j in range(key_ref.shape[1] // PAIR):
        projected = norm_product(cells, mean, scale, folded_ref, sums_ref, j * 3 * PAIR, 3 * PAIR)
        keys, low_values, high_values = keys_values(projected)
        queries = projected[:, 2 * PAIR :] * SCORE_SCALE
        base = 2 * j * PAIR
        sent_ref[:, base : base + 2 * PAIR] = projected[:, : 2 * PAIR].astype(BF16)
        key_ref[:, j * PAIR : (j + 1) * PAIR] = keys
        value_ref[:, base : base + PAIR] = low_values
        value_ref[:, base + PAIR : base + 2 * PAIR] = high_values
        query_ref[:, base : base + PAIR] = jnp.where(low, queries, 0.0).astype(BF16)
        query_ref[:, base + PAIR : base + 2 * PAIR] = jnp.where(low, 0.0, queries).astype(BF16)


def attend_pair(pair, query_rows, query_ref, keys, values, state_ref):
    total = query_ref.shape[0]
    for start in range(0, total, query_rows):
        rows = slice(start, start + query_rows)
        for head in range(2):
            index = 2 * pair + head
            queries = query_ref[rows, index * PAIR : (index + 1) * PAIR]
            scores = lax.dot_general(
                queries, keys, (((1,), (1,)), ((), ())), preferred_element_type=F32
            )
            peak = jnp.max(scores, axis=1, keepdims=True)
            soft = jnp.exp2(scores - peak).astype(BF16)
            sums = jnp.dot(soft, values[head], preferred_element_type=F32)
            state_ref[rows, 2 * index * PAIR : (2 * index + 1) * PAIR] = sums
            state_ref[rows, (2 * index + 1) * PAIR : (2 * index + 2) * PAIR] = jnp.broadcast_to(
                peak, (query_rows, PAIR)
            )


def merge_head(old_ref, part_ref, rows, index):
    sums = slice(2 * index * PAIR, (2 * index + 1) * PAIR)
    peaks = slice((2 * index + 1) * PAIR, (2 * index + 2) * PAIR)
    old_peak, part_peak = old_ref[rows, peaks], part_ref[rows, peaks]
    peak = jnp.maximum(old_peak, part_peak)
    total = old_ref[rows, sums] * jnp.exp2(old_peak - peak) + part_ref[rows, sums] * jnp.exp2(part_peak - peak)
    return total, peak


def first_kernel(query_rows, query_ref, key_ref, value_ref, _, state_ref, token_ref):
    token_ref[...] = jnp.zeros_like(token_ref)
    for j in range(key_ref.shape[1] // PAIR):
        values = [value_ref[:, n * PAIR : (n + 1) * PAIR] for n in (2 * j, 2 * j + 1)]
        attend_pair(j, query_rows, query_ref, key_ref[:, j * PAIR : (j + 1) * PAIR], values, state_ref)


def slot_kernel(count, last, query_rows, *refs):
    query_ref, old_ref, *refs = refs
    if count:
        blocks, (folded_ref, sums_ref) = refs[:count], refs[count : count + 2]
        mean, scale = row_statistics(blocks)
        cells = jnp.concatenate([ref[...] for ref in blocks], axis=1)
    else:
        sent_ref = refs[0]
    if last:
        attended, part = refs[-2:]
    else:
        state_ref, token_ref, part = refs[-3:]
        token_ref[...] = jnp.zeros_like(token_ref)
    pairs = query_ref.shape[1] // (2 * PAIR)
    for j in range(pairs):
        if count:
            projected = norm_product(cells, mean, scale, folded_ref, sums_ref, j * 3 * PAIR, 2 * PAIR)
        else:
            projected = sent_ref[:, 2 * j * PAIR : 2 * (j + 1) * PAIR].astype(F32)
        keys, *values = keys_values(projected)
        attend_pair(j, query_rows, query_ref, keys, values, part)
    total = query_ref.shape[0]
    low = lane_masks()
    for start in range(0, total, query_rows):
        rows = slice(start, start + query_rows)
        for j in range(pairs):
            heads = [merge_head(old_ref, part, rows, 2 * j + head) for head in range(2)]
            if last:
                (one, _), (two, _) = heads
                both = jnp.where(low, one, two)
                weight = pltpu.roll(jnp.where(low, two, one), HEAD_DIM, 1)
                attended[rows, j * PAIR : (j + 1) * PAIR] = (both / weight).astype(BF16)
            else:
                for head, (sums, peak) in enumerate(heads):
                    at = 2 * (2 * j + head) * PAIR
                    state_ref[rows, at : at + PAIR] = sums
                    state_ref[rows, at + PAIR : at + 2 * PAIR] = peak


def middle_kernel(count, order, me_ref, part_ref, *refs):
    attended, frames_refs, refs = refs[:count], refs[count : 2 * count], refs[2 * count :]
    *pieces, folded_ref, sums_ref, own_ref, out_ref, head_ref, tail_ref, middle = refs
    width = frames_refs[0].shape[1]
    cells = jnp.concatenate([ref[:, :width] for ref in attended], axis=1)
    swap = part_ref[0] != 0

    def weights(k):
        if width % PAIR:
            cols = slice(k * width, (k + 1) * width)
        else:
            cols = pl.ds(pl.multiple_of((me_ref[0] ^ order[k]) * width, PAIR), width)
        rows, index = [], 0
        while index < len(pieces):
            mine = pieces[index][:, cols]
            index += 1
            if mine.shape[0] < width:
                other = pieces[index][:, cols]
                index += 1
                mine = jnp.concatenate([jnp.where(swap, other, mine), jnp.where(swap, mine, other)], axis=0)
            rows.append(mine)
        return jnp.concatenate(rows, axis=0)

    for k in range(0, count, 2):
        both = jnp.concatenate([weights(k), weights(k + 1)], axis=1)
        share = jnp.dot(cells, both, preferred_element_type=F32)
        for n in range(2):
            cols = slice((k + n) * width, (k + n + 1) * width)
            middle[:, cols] = (
                frames_refs[k + n][...].astype(F32) + share[:, n * width : (n + 1) * width]
            ).astype(BF16)
    own_ref[...] = middle[:, :width]
    mean, scale = row_statistics((middle,))
    cells = middle[...]
    for j in range(out_ref.shape[1] // PAIR):
        both = norm_product(cells, mean, scale, folded_ref, sums_ref, j * 2 * PAIR, 2 * PAIR)
        out_ref[:, j * PAIR : (j + 1) * PAIR] = (
            both[:, :PAIR] / (1.0 + jnp.exp(-both[:, PAIR:]))
        ).astype(BF16)
    total = out_ref.shape[0]
    head_ref[...] = out_ref[:HALO, :]
    tail_ref[...] = out_ref[total - HALO :, :]


def conv_rows(padded, start, piece, cols, taps, scale, shift):
    window = padded[pl.ds(start, piece + 2 * HALO), cols]
    convolved = None
    for residue in range(8):
        part = None
        for offset in range(residue, KERNEL + 1, 8):
            if offset == 0:
                continue
            base = offset - residue
            term = taps[offset - 1] * window[base : base + piece + 8]
            part = term if part is None else part + term
        part = part[residue : residue + piece]
        convolved = part if convolved is None else convolved + part
    value = convolved * scale + shift
    return (value / (1.0 + jnp.exp(-value))).astype(BF16)


def conv_inner_kernel(gated_ref, taps_ref, bn_ref, activated_ref, padded):
    total, width = gated_ref.shape
    piece = 32
    padded[HALO : HALO + total, :] = gated_ref[...].astype(F32)
    for col in range(0, width, PAIR):
        cols = slice(col, col + PAIR)
        taps = [taps_ref[j : j + 1, cols] for j in range(KERNEL)]
        scale, shift = bn_ref[0:1, cols], bn_ref[1:2, cols]

        def block(index, carry):
            start = pl.multiple_of(HALO + index * piece, HALO)
            activated_ref[pl.ds(start, piece), cols] = conv_rows(padded, start, piece, cols, taps, scale, shift)
            return carry

        lax.fori_loop(0, total // piece - 1, block, 0, unroll=3)


def conv_outer_kernel(gated_ref, left_ref, right_ref, taps_ref, bn_ref, activated_ref, w_ref, keep_ref, send_ref, padded):
    total, width = gated_ref.shape
    half = keep_ref.shape[1]
    ends = []
    for first, rows in (
        (True, (left_ref[...], gated_ref[: 2 * HALO, :])),
        (False, (gated_ref[total - 2 * HALO :, :], right_ref[...])),
    ):
        padded[...] = jnp.concatenate([part.astype(F32) for part in rows], axis=0)
        parts = []
        for col in range(0, width, PAIR):
            cols = slice(col, col + PAIR)
            taps = [taps_ref[j : j + 1, cols] for j in range(KERNEL)]
            parts.append(conv_rows(padded, 0, HALO, cols, taps, bn_ref[0:1, cols], bn_ref[1:2, cols]))
        ends.append(jnp.concatenate(parts, axis=1))
    share = jnp.concatenate([ends[0], activated_ref[HALO : total - HALO, :], ends[1]], axis=0)
    keep_ref[...] = jnp.dot(share, w_ref[:, :half], preferred_element_type=F32).astype(BF16)
    send_ref[...] = jnp.dot(share, w_ref[:, half:], preferred_element_type=F32).astype(BF16)


def pad_columns(weight, width):
    if weight.shape[1] == width:
        return weight
    return jnp.pad(weight, ((0, 0), (0, width - weight.shape[1])))


def on_device(
    frames_in,
    norm1_gain,
    norm1_bias,
    w_query,
    w_key,
    w_value,
    w_out,
    norm2_gain,
    norm2_bias,
    w_glu_value,
    w_glu_gate,
    depth_kernel,
    bn_scale,
    bn_shift,
    w_proj,
):
    frames, width = frames_in.shape
    grid, ctx = lax.axis_size("grid"), lax.axis_size("ctx")
    me = lax.axis_index("grid")
    place = me.astype(jnp.int32).reshape(1)
    order = list(range(0, grid, CORES)) + list(range(1, grid, CORES))
    padded = -(-width // PAIR) * PAIR
    query_rows = math.gcd(frames, 256)

    def by_distance(cells):
        return jnp.concatenate(
            [lax.dynamic_slice_in_dim(cells, (me ^ r) * width, width, 1) for r in order], axis=1
        )

    def over_chips(block):
        return [exchange(block, "grid", CORES * a) for a in range(1, grid // CORES)]

    def other_core(blocks):
        return [exchange(block, "grid", 1) for block in blocks]

    steps = [1 << k for k in range(1, ctx.bit_length() - 1)]
    raw = {0: frames_in}
    chips = {0: over_chips(frames_in)}
    for distance in steps:
        raw[distance] = exchange(frames_in, "ctx", distance)
    vectors = [norm1_gain, norm1_bias, norm2_gain, norm2_bias]
    (gains,) = kernel_call(
        stack_kernel,
        [((8, width), F32)],
        vectors,
        spaces={i: pltpu.HBM for i in range(len(vectors))},
        scratch=[pltpu.VMEM((width,), BF16)] * len(vectors) + [pltpu.SemaphoreType.DMA((len(vectors),))],
    )
    gains = [gains] + over_chips(gains)
    gains = gains + other_core(gains)

    w_query, w_key, w_value, w_glu_value, w_glu_gate = (
        pad_columns(weight, padded) for weight in (w_query, w_key, w_value, w_glu_value, w_glu_gate)
    )
    if width % PAIR:
        row_pad = ((0, padded - width), (0, 0))
        w_p = jnp.pad(by_distance(w_proj), row_pad)
    else:
        (w_p,) = kernel_call(
            functools.partial(reorder_kernel, order),
            [(w_proj.shape, BF16)],
            [place, w_proj],
            spaces={0: pltpu.SMEM, 1: pltpu.HBM},
            scratch=[pltpu.SemaphoreType.DMA((grid,))],
        )
    taps = pad_columns(depth_kernel, padded)
    bn = pad_columns(jnp.stack([bn_scale, bn_shift]), padded)
    qkv, qkv_sums = folded(place, order, 0, gains, (w_key, w_value, w_query))
    chips[0] = [after(block, qkv_sums) for block in chips[0]]
    glu, glu_sums = folded(place, order, 2, gains, (w_glu_value, w_glu_gate))
    raw.update({s: after(block, qkv_sums) for s, block in raw.items() if s})

    parts = lax.axis_size("parts")
    part = lax.axis_index("parts").astype(jnp.int32).reshape(1)
    if parts == 2:
        (half,) = kernel_call(
            half_kernel,
            [((width // 2, w_out.shape[1]), BF16)],
            [part, w_out],
            spaces={0: pltpu.SMEM, 1: pltpu.HBM},
            scratch=[pltpu.SemaphoreType.DMA((1,))],
        )
    else:
        half = w_out
    crossed = over_chips(after(half, *chips[0]))
    state_shape = ((frames, 4 * padded), F32)
    token_shape = ((8, 128), F32)
    own = [frames_in] + chips[0]
    blocks = own + other_core(own)
    own_blocks = blocks
    n = len(blocks)
    queries, keys, values, sent = kernel_call(
        functools.partial(project_kernel, n),
        [
            ((frames, 2 * padded), BF16),
            ((frames, padded), BF16),
            ((frames, 2 * padded), BF16),
            ((frames, 2 * padded), BF16),
        ],
        [*blocks, qkv, qkv_sums],
    )
    sent = exchange(sent, "ctx", 1)
    sequence = [2, 1, *range(3, ctx)] if ctx > 2 else [1]

    def prepare(s):
        if s > 1:
            low = s & -s
            if s != low:
                raw[s] = exchange(raw[s ^ low], "ctx", low)
            chips[s] = over_chips(raw[s])

    for s in sequence[:1]:
        prepare(s)
    state, token = kernel_call(
        functools.partial(first_kernel, query_rows),
        [state_shape, token_shape],
        [queries, keys, values, raw.get(2, frames_in)],
        spaces={3: pl.ANY},
    )
    crossed = [after(block, token) for block in crossed]
    swapped = [exchange(block, "parts", 1) for block in crossed] if parts == 2 else []
    pieces = [w_out]
    for a, block in enumerate(crossed):
        pieces += [block, swapped[a]] if swapped else [block]
    pieces = pieces + other_core(pieces)
    late = [crossed, swapped]
    for index, s in enumerate(sequence):
        last = index == len(sequence) - 1
        for ahead in sequence[index + 1 : index + 3]:
            if ahead not in chips:
                prepare(ahead)
        if s == 1:
            operands = [queries, state, sent]
            count = 0
        else:
            mine = [raw[s]] + [after(block, token) for block in chips[s]]
            operands = [queries, state, *mine, *other_core(mine), qkv, qkv_sums]
            count = n
        behind = late.pop(0) if late else []
        if index == 0:
            behind = [*behind, *[raw[ahead] for ahead in sequence[1:3] if ahead > 1]]
        outs = [((frames, padded), BF16)] if last else [state_shape, token_shape]
        results = kernel_call(
            functools.partial(slot_kernel, count, last, query_rows),
            outs,
            operands + behind,
            spaces={len(operands) + i: pl.ANY for i in range(len(behind))},
            aliases={} if last else {1: 0},
            scratch=[pltpu.VMEM(*state_shape)],
        )
        if last:
            (attended,) = results
        else:
            state, token = results
    attended = [attended] + over_chips(attended)
    attended = attended + other_core(attended)
    if width % PAIR:
        pieces = [by_distance(piece) for piece in pieces]
    middle, gated, head, tail = kernel_call(
        functools.partial(middle_kernel, n, order),
        [
            ((frames, width), BF16),
            ((frames, padded), BF16),
            ((HALO, padded), BF16),
            ((HALO, padded), BF16),
        ],
        [place, part, *attended, *own_blocks, *pieces, glu, glu_sums],
        spaces={0: pltpu.SMEM, 1: pltpu.SMEM},
        scratch=[pltpu.VMEM((frames, grid * width), BF16)],
    )
    left = lax.ppermute(tail, "ctx", [(i, i + 1) for i in range(ctx - 1)])
    right = lax.ppermute(head, "ctx", [(i + 1, i) for i in range(ctx - 1)])
    (activated,) = kernel_call(
        conv_inner_kernel,
        [((frames, padded), BF16)],
        [gated, taps, bn],
        scratch=[pltpu.VMEM((frames + 2 * HALO, padded), F32)],
    )
    keep, send = kernel_call(
        conv_outer_kernel,
        [((frames, grid // CORES * width), BF16)] * 2,
        [gated, left, right, taps, bn, activated, w_p],
        scratch=[pltpu.VMEM((3 * HALO, padded), F32)],
    )
    pair_sum = keep.astype(F32) + exchange(send, "grid", 1).astype(F32)
    result = middle.astype(F32) + pair_sum[:, :width]
    for a in range(1, grid // CORES):
        share = pair_sum[:, a * width : (a + 1) * width].astype(BF16)
        result = result + exchange(share, "grid", CORES * a).astype(F32)
    return result.astype(BF16)


def solution(mesh):
    return jax.shard_map(
        on_device,
        mesh=mesh,
        in_specs=(
            P(("parts", "ctx"), "grid"),
            P("grid"),
            P("grid"),
            P(None, "grid"),
            P(None, "grid"),
            P(None, "grid"),
            P("grid", None),
            P("grid"),
            P("grid"),
            P(None, "grid"),
            P(None, "grid"),
            P(None, "grid"),
            P("grid"),
            P("grid"),
            P("grid", None),
        ),
        out_specs=P(("parts", "ctx"), "grid"),
        check_vma=False,
    )
```

```python
import functools
import math

import jax
import jax.numpy as jnp
from jax import lax
from jax.experimental import pallas as pl
from jax.experimental.pallas import tpu as pltpu
from jax.sharding import PartitionSpec as P

HEAD_DIM = 64
PAIR = 2 * HEAD_DIM
KERNEL = 31
HALF = 15
HALO = 16
EPSILON = 1e-05
CORES = 2
VMEM_BYTES = 16 * 1024 * 1024
BF16 = jnp.bfloat16
F32 = jnp.float32
SCORE_SCALE = math.log2(math.e) / math.sqrt(HEAD_DIM)


def exchange(cells, axis, distance):
    count = lax.axis_size(axis)
    return lax.ppermute(cells, axis, [(i, i ^ distance) for i in range(count)])


def kernel_call(body, outs, operands, spaces=None, scratch=(), aliases=None):
    spaces = spaces or {}
    operands = [
        pltpu.with_memory_space_constraint(cells, pltpu.HBM) if spaces.get(i) == pltpu.HBM else cells
        for i, cells in enumerate(operands)
    ]
    in_specs = [
        pl.BlockSpec(memory_space=spaces.get(i, pltpu.VMEM)) for i in range(len(operands))
    ]
    return pl.pallas_call(
        body,
        in_specs=in_specs,
        out_specs=tuple(pl.BlockSpec(memory_space=pltpu.VMEM) for _ in outs),
        out_shape=tuple(jax.ShapeDtypeStruct(shape, dtype) for shape, dtype in outs),
        scratch_shapes=list(scratch),
        input_output_aliases=aliases or {},
        compiler_params=pltpu.CompilerParams(vmem_limit_bytes=VMEM_BYTES),
        cost_estimate=pl.CostEstimate(flops=1000, bytes_accessed=1000, transcendentals=0),
    )(*operands)


def after(cells, *done):
    def body(*refs):
        pass

    anywhere = pl.BlockSpec(memory_space=pl.ANY)
    return pl.pallas_call(
        body,
        in_specs=[anywhere] * (1 + len(done)),
        out_specs=anywhere,
        out_shape=jax.ShapeDtypeStruct(cells.shape, cells.dtype),
        input_output_aliases={0: 0},
        compiler_params=pltpu.CompilerParams(vmem_limit_bytes=64 * 1024),
        cost_estimate=pl.CostEstimate(flops=0, bytes_accessed=0, transcendentals=0),
    )(cells, *done)


def fold_kernel(order, which, count, me_ref, gains_ref, *refs):
    sources, (folded_ref, sums_ref), weights, done = refs[:count], refs[count : count + 2], refs[count + 2 : -1], refs[-1]
    copies = [pltpu.make_async_copy(sources[n], weights[n], done.at[n]) for n in range(count)]
    for copy in copies:
        copy.start()
    width = gains_ref.shape[1]
    columns = weights[0].shape[1]
    factors = []
    for r in order:
        gains = gains_ref[pl.ds(pl.multiple_of((me_ref[0] ^ r) * 8, 8), 8), :]
        gain = jnp.transpose(jnp.broadcast_to(gains[which : which + 1, :], (PAIR, width)))
        bias = jnp.broadcast_to(gains[which + 1 : which + 2, :], (8, width)).astype(BF16)
        factors.append((gain, bias))
    for n, ref in enumerate(weights):
        copies[n].wait()
        total = jnp.zeros((8, columns), F32)
        for k, r in enumerate(order):
            gain, bias = factors[k]
            start = pl.multiple_of((me_ref[0] ^ r) * width, width)
            block = ref[pl.ds(start, width), :]
            total = total + jnp.dot(bias, block, preferred_element_type=F32)
            for j in range(columns // PAIR):
                target = (j * count + n) * PAIR
                folded_ref[k * width : (k + 1) * width, target : target + PAIR] = (
                    block[:, j * PAIR : (j + 1) * PAIR].astype(F32) * gain
                ).astype(BF16)
        for j in range(columns // PAIR):
            target = (j * count + n) * PAIR
            sums_ref[1:2, target : target + PAIR] = total[0:1, j * PAIR : (j + 1) * PAIR]
    sums = jnp.dot(jnp.ones((8, folded_ref.shape[0]), BF16), folded_ref[...], preferred_element_type=F32)
    sums_ref[0:1, :] = sums[0:1]


def folded(me, order, which, gains, weights):
    rows, columns = weights[0].shape
    total = columns * len(weights)
    spaces = {2 + n: pltpu.HBM for n in range(len(weights))}
    return kernel_call(
        functools.partial(fold_kernel, order, which, len(weights)),
        [((rows, total), BF16), ((2, total), F32)],
        [me, gains, *weights],
        spaces={0: pltpu.SMEM, **spaces},
        scratch=[pltpu.VMEM((rows, columns), BF16)] * len(weights) + [pltpu.SemaphoreType.DMA((len(weights),))],
    )


def stack_kernel(*refs):
    count = (len(refs) - 2) // 2
    sources, out_ref, rows, done = refs[:count], refs[count], refs[count + 1 : -1], refs[-1]
    copies = [pltpu.make_async_copy(sources[i], rows[i], done.at[i]) for i in range(count)]
    for copy in copies:
        copy.start()
    out_ref[...] = jnp.zeros_like(out_ref)
    for i, copy in enumerate(copies):
        copy.wait()
        out_ref[i : i + 1, :] = rows[i][...].astype(F32).reshape(1, out_ref.shape[1])


def reorder_kernel(order, me_ref, source_ref, out_ref, done):
    width = source_ref.shape[1] // len(order)
    copies = []
    for k, r in enumerate(order):
        cols = pl.ds(pl.multiple_of((me_ref[0] ^ r) * width, PAIR), width)
        copies.append(
            pltpu.make_async_copy(source_ref.at[:, cols], out_ref.at[:, k * width : (k + 1) * width], done.at[k])
        )
        copies[-1].start()
    for copy in copies:
        copy.wait()


def half_kernel(part_ref, source_ref, half_ref, done):
    rows = half_ref.shape[0]
    copy = pltpu.make_async_copy(
        source_ref.at[pl.ds(pl.multiple_of(part_ref[0] * rows, rows), rows), :], half_ref, done.at[0]
    )
    copy.start()
    copy.wait()


def row_statistics(refs):
    rows, width = refs[0].shape
    full = width * len(refs)
    means, scales = [], []
    step = math.gcd(rows, 64)
    for start in range(0, rows, step):
        parts = [ref[start : start + step, :].astype(F32) for ref in refs]
        mean = sum(jnp.sum(part, axis=1, keepdims=True) for part in parts) / full
        variance = sum(jnp.sum(jnp.square(part - mean), axis=1, keepdims=True) for part in parts) / full
        means.append(mean)
        scales.append(lax.rsqrt(variance + EPSILON))
    return jnp.concatenate(means, axis=0), jnp.concatenate(scales, axis=0)


def norm_product(cells, mean, scale, folded_ref, sums_ref, start, columns):
    cols = slice(start, start + columns)
    product = jnp.dot(cells, folded_ref[:, cols], preferred_element_type=F32)
    return (product - mean * sums_ref[0:1, cols]) * scale + sums_ref[1:2, cols]


def lane_masks():
    lanes = lax.broadcasted_iota(jnp.int32, (1, PAIR), 1)
    return lanes < HEAD_DIM


def keys_values(projected):
    low = lane_masks()
    values = projected[:, PAIR : 2 * PAIR]
    return (
        projected[:, :PAIR].astype(BF16),
        jnp.where(low, values, 1.0).astype(BF16),
        jnp.where(low, 1.0, values).astype(BF16),
    )


def project_kernel(count, *refs):
    blocks, (folded_ref, sums_ref), (query_ref, key_ref, value_ref) = refs[:count], refs[count : count + 2], refs[-3:]
    mean, scale = row_statistics(blocks)
    cells = jnp.concatenate([ref[...] for ref in blocks], axis=1)
    low = lane_masks()
    for j in range(key_ref.shape[1] // PAIR):
        projected = norm_product(cells, mean, scale, folded_ref, sums_ref, j * 3 * PAIR, 3 * PAIR)
        keys, low_values, high_values = keys_values(projected)
        queries = projected[:, 2 * PAIR :] * SCORE_SCALE
        base = 2 * j * PAIR
        key_ref[:, j * PAIR : (j + 1) * PAIR] = keys
        value_ref[:, base : base + PAIR] = low_values
        value_ref[:, base + PAIR : base + 2 * PAIR] = high_values
        query_ref[:, base : base + PAIR] = jnp.where(low, queries, 0.0).astype(BF16)
        query_ref[:, base + PAIR : base + 2 * PAIR] = jnp.where(low, 0.0, queries).astype(BF16)


def attend_pair(pair, query_rows, query_ref, keys, values, state_ref):
    total = query_ref.shape[0]
    for start in range(0, total, query_rows):
        rows = slice(start, start + query_rows)
        for head in range(2):
            index = 2 * pair + head
            queries = query_ref[rows, index * PAIR : (index + 1) * PAIR]
            scores = lax.dot_general(
                queries, keys, (((1,), (1,)), ((), ())), preferred_element_type=F32
            )
            peak = jnp.max(scores, axis=1, keepdims=True)
            soft = jnp.exp2(scores - peak).astype(BF16)
            sums = jnp.dot(soft, values[head], preferred_element_type=F32)
            state_ref[rows, 2 * index * PAIR : (2 * index + 1) * PAIR] = sums
            state_ref[rows, (2 * index + 1) * PAIR : (2 * index + 2) * PAIR] = jnp.broadcast_to(
                peak, (query_rows, PAIR)
            )


def merge_head(old_ref, part_ref, rows, index):
    sums = slice(2 * index * PAIR, (2 * index + 1) * PAIR)
    peaks = slice((2 * index + 1) * PAIR, (2 * index + 2) * PAIR)
    old_peak, part_peak = old_ref[rows, peaks], part_ref[rows, peaks]
    peak = jnp.maximum(old_peak, part_peak)
    total = old_ref[rows, sums] * jnp.exp2(old_peak - peak) + part_ref[rows, sums] * jnp.exp2(part_peak - peak)
    return total, peak


def first_kernel(query_rows, query_ref, key_ref, value_ref, _, state_ref, token_ref):
    token_ref[...] = jnp.zeros_like(token_ref)
    for j in range(key_ref.shape[1] // PAIR):
        values = [value_ref[:, n * PAIR : (n + 1) * PAIR] for n in (2 * j, 2 * j + 1)]
        attend_pair(j, query_rows, query_ref, key_ref[:, j * PAIR : (j + 1) * PAIR], values, state_ref)


def slot_kernel(count, last, query_rows, *refs):
    query_ref, old_ref, *refs = refs
    blocks, (folded_ref, sums_ref) = refs[:count], refs[count : count + 2]
    part, key_ref, value_ref = refs[-3:]
    if last:
        attended = refs[-4]
    else:
        state_ref, token_ref = refs[-5:-3]
        token_ref[...] = jnp.zeros_like(token_ref)
    mean, scale = row_statistics(blocks)
    cells = jnp.concatenate([ref[...] for ref in blocks], axis=1)
    pairs = query_ref.shape[1] // (2 * PAIR)
    for j in range(pairs):
        projected = norm_product(cells, mean, scale, folded_ref, sums_ref, j * 3 * PAIR, 2 * PAIR)
        base = 2 * j * PAIR
        (
            key_ref[:, j * PAIR : (j + 1) * PAIR],
            value_ref[:, base : base + PAIR],
            value_ref[:, base + PAIR : base + 2 * PAIR],
        ) = keys_values(projected)
    for j in range(pairs):
        values = [value_ref[:, n * PAIR : (n + 1) * PAIR] for n in (2 * j, 2 * j + 1)]
        attend_pair(j, query_rows, query_ref, key_ref[:, j * PAIR : (j + 1) * PAIR], values, part)
    total = query_ref.shape[0]
    low = lane_masks()
    for start in range(0, total, query_rows):
        rows = slice(start, start + query_rows)
        for j in range(pairs):
            heads = [merge_head(old_ref, part, rows, 2 * j + head) for head in range(2)]
            if last:
                (one, _), (two, _) = heads
                both = jnp.where(low, one, two)
                weight = pltpu.roll(jnp.where(low, two, one), HEAD_DIM, 1)
                attended[rows, j * PAIR : (j + 1) * PAIR] = (both / weight).astype(BF16)
            else:
                for head, (sums, peak) in enumerate(heads):
                    at = 2 * (2 * j + head) * PAIR
                    state_ref[rows, at : at + PAIR] = sums
                    state_ref[rows, at + PAIR : at + 2 * PAIR] = peak


def middle_kernel(count, order, me_ref, part_ref, *refs):
    attended, frames_refs, refs = refs[:count], refs[count : 2 * count], refs[2 * count :]
    *pieces, folded_ref, sums_ref, own_ref, out_ref, head_ref, tail_ref, middle = refs
    width = frames_refs[0].shape[1]
    cells = jnp.concatenate([ref[:, :width] for ref in attended], axis=1)
    swap = part_ref[0] != 0

    def weights(k):
        if width % PAIR:
            cols = slice(k * width, (k + 1) * width)
        else:
            cols = pl.ds(pl.multiple_of((me_ref[0] ^ order[k]) * width, PAIR), width)
        rows, index = [], 0
        while index < len(pieces):
            mine = pieces[index][:, cols]
            index += 1
            if mine.shape[0] < width:
                other = pieces[index][:, cols]
                index += 1
                mine = jnp.concatenate([jnp.where(swap, other, mine), jnp.where(swap, mine, other)], axis=0)
            rows.append(mine)
        return jnp.concatenate(rows, axis=0)

    for k in range(0, count, 2):
        both = jnp.concatenate([weights(k), weights(k + 1)], axis=1)
        share = jnp.dot(cells, both, preferred_element_type=F32)
        for n in range(2):
            cols = slice((k + n) * width, (k + n + 1) * width)
            middle[:, cols] = (
                frames_refs[k + n][...].astype(F32) + share[:, n * width : (n + 1) * width]
            ).astype(BF16)
    own_ref[...] = middle[:, :width]
    mean, scale = row_statistics((middle,))
    cells = middle[...]
    for j in range(out_ref.shape[1] // PAIR):
        both = norm_product(cells, mean, scale, folded_ref, sums_ref, j * 2 * PAIR, 2 * PAIR)
        out_ref[:, j * PAIR : (j + 1) * PAIR] = (
            both[:, :PAIR] / (1.0 + jnp.exp(-both[:, PAIR:]))
        ).astype(BF16)
    total = out_ref.shape[0]
    head_ref[...] = out_ref[:HALO, :]
    tail_ref[...] = out_ref[total - HALO :, :]


def conv_rows(padded, start, piece, cols, taps, scale, shift):
    window = padded[pl.ds(start, piece + 2 * HALO), cols]
    convolved = None
    for residue in range(8):
        part = None
        for offset in range(residue, KERNEL + 1, 8):
            if offset == 0:
                continue
            base = offset - residue
            term = taps[offset - 1] * window[base : base + piece + 8]
            part = term if part is None else part + term
        part = part[residue : residue + piece]
        convolved = part if convolved is None else convolved + part
    value = convolved * scale + shift
    return (value / (1.0 + jnp.exp(-value))).astype(BF16)


def conv_inner_kernel(gated_ref, taps_ref, bn_ref, activated_ref, padded):
    total, width = gated_ref.shape
    piece = 32
    padded[HALO : HALO + total, :] = gated_ref[...].astype(F32)
    for col in range(0, width, PAIR):
        cols = slice(col, col + PAIR)
        taps = [taps_ref[j : j + 1, cols] for j in range(KERNEL)]
        scale, shift = bn_ref[0:1, cols], bn_ref[1:2, cols]

        def block(index, carry):
            start = pl.multiple_of(HALO + index * piece, HALO)
            activated_ref[pl.ds(start, piece), cols] = conv_rows(padded, start, piece, cols, taps, scale, shift)
            return carry

        lax.fori_loop(0, total // piece - 1, block, 0, unroll=3)


def conv_outer_kernel(gated_ref, left_ref, right_ref, taps_ref, bn_ref, activated_ref, w_ref, keep_ref, send_ref, padded):
    total, width = gated_ref.shape
    half = keep_ref.shape[1]
    ends = []
    for first, rows in (
        (True, (left_ref[...], gated_ref[: 2 * HALO, :])),
        (False, (gated_ref[total - 2 * HALO :, :], right_ref[...])),
    ):
        padded[...] = jnp.concatenate([part.astype(F32) for part in rows], axis=0)
        parts = []
        for col in range(0, width, PAIR):
            cols = slice(col, col + PAIR)
            taps = [taps_ref[j : j + 1, cols] for j in range(KERNEL)]
            parts.append(conv_rows(padded, 0, HALO, cols, taps, bn_ref[0:1, cols], bn_ref[1:2, cols]))
        ends.append(jnp.concatenate(parts, axis=1))
    share = jnp.concatenate([ends[0], activated_ref[HALO : total - HALO, :], ends[1]], axis=0)
    keep_ref[...] = jnp.dot(share, w_ref[:, :half], preferred_element_type=F32).astype(BF16)
    send_ref[...] = jnp.dot(share, w_ref[:, half:], preferred_element_type=F32).astype(BF16)


def pad_columns(weight, width):
    if weight.shape[1] == width:
        return weight
    return jnp.pad(weight, ((0, 0), (0, width - weight.shape[1])))


def on_device(
    frames_in,
    norm1_gain,
    norm1_bias,
    w_query,
    w_key,
    w_value,
    w_out,
    norm2_gain,
    norm2_bias,
    w_glu_value,
    w_glu_gate,
    depth_kernel,
    bn_scale,
    bn_shift,
    w_proj,
):
    frames, width = frames_in.shape
    grid, ctx = lax.axis_size("grid"), lax.axis_size("ctx")
    me = lax.axis_index("grid")
    place = me.astype(jnp.int32).reshape(1)
    order = list(range(0, grid, CORES)) + list(range(1, grid, CORES))
    padded = -(-width // PAIR) * PAIR
    query_rows = math.gcd(frames, 256)

    def by_distance(cells):
        return jnp.concatenate(
            [lax.dynamic_slice_in_dim(cells, (me ^ r) * width, width, 1) for r in order], axis=1
        )

    def over_chips(block):
        return [exchange(block, "grid", CORES * a) for a in range(1, grid // CORES)]

    def other_core(blocks):
        return [exchange(block, "grid", 1) for block in blocks]

    vectors = [norm1_gain, norm1_bias, norm2_gain, norm2_bias]
    (gains,) = kernel_call(
        stack_kernel,
        [((8, width), F32)],
        vectors,
        spaces={i: pltpu.HBM for i in range(len(vectors))},
        scratch=[pltpu.VMEM((width,), BF16)] * len(vectors) + [pltpu.SemaphoreType.DMA((len(vectors),))],
    )
    gains = lax.all_gather(gains, "grid", axis=0, tiled=True)
    raw = {0: frames_in}
    chips = {0: over_chips(frames_in)}
    for k in reversed(range(ctx.bit_length() - 1)):
        raw[1 << k] = exchange(frames_in, "ctx", 1 << k)

    w_query, w_key, w_value, w_glu_value, w_glu_gate = (
        pad_columns(weight, padded) for weight in (w_query, w_key, w_value, w_glu_value, w_glu_gate)
    )
    if width % PAIR:
        row_pad = ((0, padded - width), (0, 0))
        w_p = jnp.pad(by_distance(w_proj), row_pad)
    else:
        (w_p,) = kernel_call(
            functools.partial(reorder_kernel, order),
            [(w_proj.shape, BF16)],
            [place, w_proj],
            spaces={0: pltpu.SMEM, 1: pltpu.HBM},
            scratch=[pltpu.SemaphoreType.DMA((grid,))],
        )
    taps = pad_columns(depth_kernel, padded)
    bn = pad_columns(jnp.stack([bn_scale, bn_shift]), padded)
    qkv, qkv_sums = folded(place, order, 0, gains, (w_key, w_value, w_query))
    chips[0] = [after(block, qkv_sums) for block in chips[0]]
    glu, glu_sums = folded(place, order, 2, gains, (w_glu_value, w_glu_gate))

    parts = lax.axis_size("parts")
    part = lax.axis_index("parts").astype(jnp.int32).reshape(1)
    if parts == 2:
        (half,) = kernel_call(
            half_kernel,
            [((width // 2, w_out.shape[1]), BF16)],
            [part, w_out],
            spaces={0: pltpu.SMEM, 1: pltpu.HBM},
            scratch=[pltpu.SemaphoreType.DMA((1,))],
        )
    else:
        half = w_out
    crossed = over_chips(after(half, *chips[0]))
    state_shape = ((frames, 4 * padded), F32)
    token_shape = ((8, 128), F32)
    wide, narrow = ((frames, 2 * padded), BF16), ((frames, padded), BF16)
    chips[1] = [exchange(block, "ctx", 1) for block in chips[0]]
    own = [frames_in] + chips[0]
    own_blocks = own + other_core(own)
    n = len(own_blocks)
    early = [raw[s] for s in raw if s]
    queries, keys, values = kernel_call(
        functools.partial(project_kernel, n),
        [wide, narrow, wide],
        [*own_blocks, qkv, qkv_sums, *early],
        spaces={n + 2 + i: pl.ANY for i in range(len(early))},
    )

    def prepare(s):
        low = s & -s
        if s != low:
            raw[s] = exchange(raw[s ^ low], "ctx", low)
        chips[s] = over_chips(raw[s])

    for s in range(2, min(ctx, 4)):
        prepare(s)
    state, token = kernel_call(
        functools.partial(first_kernel, query_rows),
        [state_shape, token_shape],
        [queries, keys, values, frames_in],
        spaces={3: pl.ANY},
    )
    crossed = [after(block, token) for block in crossed]
    swapped = [exchange(block, "parts", 1) for block in crossed] if parts == 2 else []
    pieces = [w_out]
    for a, block in enumerate(crossed):
        pieces += [block, swapped[a]] if swapped else [block]
    pieces = pieces + other_core(pieces)
    late = {1: [*crossed, *[raw[s] for s in (3,) if s < ctx]], 2: swapped}
    for s in range(1, ctx):
        last = s == ctx - 1
        if s + 2 < ctx and s + 2 not in chips:
            prepare(s + 2)
        mine = [raw[s]] + [after(block, token) for block in chips[s]]
        operands = [queries, state, *mine, *other_core(mine), qkv, qkv_sums]
        behind = late.get(s, [])
        results = kernel_call(
            functools.partial(slot_kernel, n, last, query_rows),
            [narrow] if last else [state_shape, token_shape],
            operands + behind,
            spaces={len(operands) + i: pl.ANY for i in range(len(behind))},
            aliases={} if last else {1: 0},
            scratch=[pltpu.VMEM(*shape) for shape in (state_shape, narrow, wide)],
        )
        if last:
            (attended,) = results
        else:
            state, token = results
    attended = [attended] + [after(block, glu_sums, w_p) for block in over_chips(attended)]
    attended = attended + other_core(attended)
    if width % PAIR:
        pieces = [by_distance(piece) for piece in pieces]
    middle, gated, head, tail = kernel_call(
        functools.partial(middle_kernel, n, order),
        [
            ((frames, width), BF16),
            ((frames, padded), BF16),
            ((HALO, padded), BF16),
            ((HALO, padded), BF16),
        ],
        [place, part, *attended, *own_blocks, *pieces, glu, glu_sums],
        spaces={0: pltpu.SMEM, 1: pltpu.SMEM},
        scratch=[pltpu.VMEM((frames, grid * width), BF16)],
    )
    left = lax.ppermute(tail, "ctx", [(i, i + 1) for i in range(ctx - 1)])
    right = lax.ppermute(head, "ctx", [(i + 1, i) for i in range(ctx - 1)])
    (activated,) = kernel_call(
        conv_inner_kernel,
        [((frames, padded), BF16)],
        [gated, taps, bn],
        scratch=[pltpu.VMEM((frames + 2 * HALO, padded), F32)],
    )
    keep, send = kernel_call(
        conv_outer_kernel,
        [((frames, grid // CORES * width), BF16)] * 2,
        [gated, left, right, taps, bn, activated, w_p],
        scratch=[pltpu.VMEM((3 * HALO, padded), F32)],
    )
    pair_sum = keep.astype(F32) + exchange(send, "grid", 1).astype(F32)
    result = middle.astype(F32) + pair_sum[:, :width]
    for a in range(1, grid // CORES):
        share = pair_sum[:, a * width : (a + 1) * width].astype(BF16)
        result = result + exchange(share, "grid", CORES * a).astype(F32)
    return result.astype(BF16)


def solution(mesh):
    return jax.shard_map(
        on_device,
        mesh=mesh,
        in_specs=(
            P(("parts", "ctx"), "grid"),
            P("grid"),
            P("grid"),
            P(None, "grid"),
            P(None, "grid"),
            P(None, "grid"),
            P("grid", None),
            P("grid"),
            P("grid"),
            P(None, "grid"),
            P(None, "grid"),
            P(None, "grid"),
            P("grid"),
            P("grid"),
            P("grid", None),
        ),
        out_specs=P(("parts", "ctx"), "grid"),
        check_vma=False,
    )
```

```python
import functools
import math

import jax
import jax.numpy as jnp
from jax import lax
from jax.experimental import pallas as pl
from jax.experimental.pallas import tpu as pltpu
from jax.sharding import PartitionSpec as P

HEAD_DIM = 64
PAIR = 2 * HEAD_DIM
KERNEL = 31
HALF = 15
HALO = 16
EPSILON = 1e-05
CORES = 2
VMEM_BYTES = 16 * 1024 * 1024
BF16 = jnp.bfloat16
F32 = jnp.float32
SCORE_SCALE = math.log2(math.e) / math.sqrt(HEAD_DIM)


def exchange(cells, axis, distance):
    count = lax.axis_size(axis)
    return lax.ppermute(cells, axis, [(i, i ^ distance) for i in range(count)])


def kernel_call(body, outs, operands, spaces=None, scratch=(), aliases=None):
    spaces = spaces or {}
    operands = [
        pltpu.with_memory_space_constraint(cells, pltpu.HBM) if spaces.get(i) == pltpu.HBM else cells
        for i, cells in enumerate(operands)
    ]
    in_specs = [
        pl.BlockSpec(memory_space=spaces.get(i, pltpu.VMEM)) for i in range(len(operands))
    ]
    return pl.pallas_call(
        body,
        in_specs=in_specs,
        out_specs=tuple(pl.BlockSpec(memory_space=pltpu.VMEM) for _ in outs),
        out_shape=tuple(jax.ShapeDtypeStruct(shape, dtype) for shape, dtype in outs),
        scratch_shapes=list(scratch),
        input_output_aliases=aliases or {},
        compiler_params=pltpu.CompilerParams(vmem_limit_bytes=VMEM_BYTES),
        cost_estimate=pl.CostEstimate(flops=1000, bytes_accessed=1000, transcendentals=0),
    )(*operands)


def after(cells, *done):
    def body(*refs):
        pass

    anywhere = pl.BlockSpec(memory_space=pl.ANY)
    return pl.pallas_call(
        body,
        in_specs=[anywhere] * (1 + len(done)),
        out_specs=anywhere,
        out_shape=jax.ShapeDtypeStruct(cells.shape, cells.dtype),
        input_output_aliases={0: 0},
        compiler_params=pltpu.CompilerParams(vmem_limit_bytes=64 * 1024),
        cost_estimate=pl.CostEstimate(flops=0, bytes_accessed=0, transcendentals=0),
    )(cells, *done)


def fold_kernel(order, which, count, me_ref, gains_ref, *refs):
    sources, (folded_ref, sums_ref), weights, done = refs[:count], refs[count : count + 2], refs[count + 2 : -1], refs[-1]
    copies = [pltpu.make_async_copy(sources[n], weights[n], done.at[n]) for n in range(count)]
    for copy in copies:
        copy.start()
    width = gains_ref.shape[1]
    columns = weights[0].shape[1]
    factors = []
    for r in order:
        gains = gains_ref[pl.ds(pl.multiple_of((me_ref[0] ^ r) * 8, 8), 8), :]
        gain = jnp.transpose(jnp.broadcast_to(gains[which : which + 1, :], (PAIR, width)))
        bias = jnp.broadcast_to(gains[which + 1 : which + 2, :], (8, width)).astype(BF16)
        factors.append((gain, bias))
    for n, ref in enumerate(weights):
        copies[n].wait()
        total = jnp.zeros((8, columns), F32)
        for k, r in enumerate(order):
            gain, bias = factors[k]
            start = pl.multiple_of((me_ref[0] ^ r) * width, width)
            block = ref[pl.ds(start, width), :]
            total = total + jnp.dot(bias, block, preferred_element_type=F32)
            for j in range(columns // PAIR):
                target = (j * count + n) * PAIR
                folded_ref[k * width : (k + 1) * width, target : target + PAIR] = (
                    block[:, j * PAIR : (j + 1) * PAIR].astype(F32) * gain
                ).astype(BF16)
        for j in range(columns // PAIR):
            target = (j * count + n) * PAIR
            sums_ref[1:2, target : target + PAIR] = total[0:1, j * PAIR : (j + 1) * PAIR]
    sums = jnp.dot(jnp.ones((8, folded_ref.shape[0]), BF16), folded_ref[...], preferred_element_type=F32)
    sums_ref[0:1, :] = sums[0:1]


def folded(me, order, which, gains, weights):
    rows, columns = weights[0].shape
    total = columns * len(weights)
    spaces = {2 + n: pltpu.HBM for n in range(len(weights))}
    return kernel_call(
        functools.partial(fold_kernel, order, which, len(weights)),
        [((rows, total), BF16), ((2, total), F32)],
        [me, gains, *weights],
        spaces={0: pltpu.SMEM, **spaces},
        scratch=[pltpu.VMEM((rows, columns), BF16)] * len(weights) + [pltpu.SemaphoreType.DMA((len(weights),))],
    )


def stack_kernel(*refs):
    count = (len(refs) - 2) // 2
    sources, out_ref, rows, done = refs[:count], refs[count], refs[count + 1 : -1], refs[-1]
    copies = [pltpu.make_async_copy(sources[i], rows[i], done.at[i]) for i in range(count)]
    for copy in copies:
        copy.start()
    out_ref[...] = jnp.zeros_like(out_ref)
    for i, copy in enumerate(copies):
        copy.wait()
        out_ref[i : i + 1, :] = rows[i][...].astype(F32).reshape(1, out_ref.shape[1])


def reorder_kernel(order, me_ref, source_ref, out_ref, done):
    width = source_ref.shape[1] // len(order)
    copies = []
    for k, r in enumerate(order):
        cols = pl.ds(pl.multiple_of((me_ref[0] ^ r) * width, PAIR), width)
        copies.append(
            pltpu.make_async_copy(source_ref.at[:, cols], out_ref.at[:, k * width : (k + 1) * width], done.at[k])
        )
        copies[-1].start()
    for copy in copies:
        copy.wait()


def half_kernel(part_ref, source_ref, half_ref, done):
    rows = half_ref.shape[0]
    copy = pltpu.make_async_copy(
        source_ref.at[pl.ds(pl.multiple_of(part_ref[0] * rows, rows), rows), :], half_ref, done.at[0]
    )
    copy.start()
    copy.wait()


def row_statistics(refs):
    rows, width = refs[0].shape
    full = width * len(refs)
    means, scales = [], []
    step = math.gcd(rows, 64)
    for start in range(0, rows, step):
        parts = [ref[start : start + step, :].astype(F32) for ref in refs]
        mean = sum(jnp.sum(part, axis=1, keepdims=True) for part in parts) / full
        variance = sum(jnp.sum(jnp.square(part - mean), axis=1, keepdims=True) for part in parts) / full
        means.append(mean)
        scales.append(lax.rsqrt(variance + EPSILON))
    return jnp.concatenate(means, axis=0), jnp.concatenate(scales, axis=0)


def norm_product(cells, mean, scale, folded_ref, sums_ref, start, columns):
    cols = slice(start, start + columns)
    product = jnp.dot(cells, folded_ref[:, cols], preferred_element_type=F32)
    return (product - mean * sums_ref[0:1, cols]) * scale + sums_ref[1:2, cols]


def lane_masks():
    lanes = lax.broadcasted_iota(jnp.int32, (1, PAIR), 1)
    return lanes < HEAD_DIM


def keys_values(projected):
    low = lane_masks()
    values = projected[:, PAIR : 2 * PAIR]
    return (
        projected[:, :PAIR].astype(BF16),
        jnp.where(low, values, 1.0).astype(BF16),
        jnp.where(low, 1.0, values).astype(BF16),
    )


def project_kernel(count, first, *refs):
    blocks, (folded_ref, sums_ref, *refs) = refs[:count], refs[count:]
    key_ref, value_ref = refs[-2:]
    query_ref = refs[-3] if first else None
    mean, scale = row_statistics(blocks)
    cells = jnp.concatenate([ref[...] for ref in blocks], axis=1)
    low = lane_masks()
    for j in range(key_ref.shape[1] // PAIR):
        columns = (3 if first else 2) * PAIR
        projected = norm_product(cells, mean, scale, folded_ref, sums_ref, j * 3 * PAIR, columns)
        base = 2 * j * PAIR
        (
            key_ref[:, j * PAIR : (j + 1) * PAIR],
            value_ref[:, base : base + PAIR],
            value_ref[:, base + PAIR : base + 2 * PAIR],
        ) = keys_values(projected)
        if first:
            queries = projected[:, 2 * PAIR :] * SCORE_SCALE
            query_ref[:, base : base + PAIR] = jnp.where(low, queries, 0.0).astype(BF16)
            query_ref[:, base + PAIR : base + 2 * PAIR] = jnp.where(low, 0.0, queries).astype(BF16)


def attend_pair(pair, query_rows, query_ref, keys, values, state_ref):
    total = query_ref.shape[0]
    for start in range(0, total, query_rows):
        rows = slice(start, start + query_rows)
        for head in range(2):
            index = 2 * pair + head
            queries = query_ref[rows, index * PAIR : (index + 1) * PAIR]
            scores = lax.dot_general(
                queries, keys, (((1,), (1,)), ((), ())), preferred_element_type=F32
            )
            peak = jnp.max(scores, axis=1, keepdims=True)
            soft = jnp.exp2(scores - peak).astype(BF16)
            sums = jnp.dot(soft, values[head], preferred_element_type=F32)
            state_ref[rows, 2 * index * PAIR : (2 * index + 1) * PAIR] = sums
            state_ref[rows, (2 * index + 1) * PAIR : (2 * index + 2) * PAIR] = jnp.broadcast_to(
                peak, (query_rows, PAIR)
            )


def merge_head(old_ref, part_ref, rows, index):
    sums = slice(2 * index * PAIR, (2 * index + 1) * PAIR)
    peaks = slice((2 * index + 1) * PAIR, (2 * index + 2) * PAIR)
    old_peak, part_peak = old_ref[rows, peaks], part_ref[rows, peaks]
    peak = jnp.maximum(old_peak, part_peak)
    total = old_ref[rows, sums] * jnp.exp2(old_peak - peak) + part_ref[rows, sums] * jnp.exp2(part_peak - peak)
    return total, peak


def attend_kernel(first, last, query_rows, query_ref, key_ref, value_ref, *refs):
    if last:
        old_ref, attended, part = refs[0], refs[-2], refs[-1]
    elif first:
        part, token_ref = refs[-2:]
    else:
        old_ref, (state_ref, token_ref, part) = refs[0], refs[-3:]
    if not last:
        token_ref[...] = jnp.zeros_like(token_ref)
    pairs = query_ref.shape[1] // (2 * PAIR)
    for j in range(pairs):
        values = [value_ref[:, n * PAIR : (n + 1) * PAIR] for n in (2 * j, 2 * j + 1)]
        attend_pair(j, query_rows, query_ref, key_ref[:, j * PAIR : (j + 1) * PAIR], values, part)
    if first:
        return
    total = query_ref.shape[0]
    low = lane_masks()
    for start in range(0, total, query_rows):
        rows = slice(start, start + query_rows)
        for j in range(pairs):
            heads = [merge_head(old_ref, part, rows, 2 * j + head) for head in range(2)]
            if last:
                (one, _), (two, _) = heads
                both = jnp.where(low, one, two)
                weight = pltpu.roll(jnp.where(low, two, one), HEAD_DIM, 1)
                attended[rows, j * PAIR : (j + 1) * PAIR] = (both / weight).astype(BF16)
            else:
                for head, (sums, peak) in enumerate(heads):
                    at = 2 * (2 * j + head) * PAIR
                    state_ref[rows, at : at + PAIR] = sums
                    state_ref[rows, at + PAIR : at + 2 * PAIR] = peak


def middle_kernel(count, order, me_ref, part_ref, *refs):
    attended, frames_refs, refs = refs[:count], refs[count : 2 * count], refs[2 * count :]
    *pieces, folded_ref, sums_ref, own_ref, out_ref, head_ref, tail_ref, middle = refs
    width = frames_refs[0].shape[1]
    cells = jnp.concatenate([ref[:, :width] for ref in attended], axis=1)
    swap = part_ref[0] != 0

    def weights(k):
        if width % PAIR:
            cols = slice(k * width, (k + 1) * width)
        else:
            cols = pl.ds(pl.multiple_of((me_ref[0] ^ order[k]) * width, PAIR), width)
        rows, index = [], 0
        while index < len(pieces):
            mine = pieces[index][:, cols]
            index += 1
            if mine.shape[0] < width:
                other = pieces[index][:, cols]
                index += 1
                mine = jnp.concatenate([jnp.where(swap, other, mine), jnp.where(swap, mine, other)], axis=0)
            rows.append(mine)
        return jnp.concatenate(rows, axis=0)

    for k in range(0, count, 2):
        both = jnp.concatenate([weights(k), weights(k + 1)], axis=1)
        share = jnp.dot(cells, both, preferred_element_type=F32)
        for n in range(2):
            cols = slice((k + n) * width, (k + n + 1) * width)
            middle[:, cols] = (
                frames_refs[k + n][...].astype(F32) + share[:, n * width : (n + 1) * width]
            ).astype(BF16)
    own_ref[...] = middle[:, :width]
    mean, scale = row_statistics((middle,))
    cells = middle[...]
    for j in range(out_ref.shape[1] // PAIR):
        both = norm_product(cells, mean, scale, folded_ref, sums_ref, j * 2 * PAIR, 2 * PAIR)
        out_ref[:, j * PAIR : (j + 1) * PAIR] = (
            both[:, :PAIR] / (1.0 + jnp.exp(-both[:, PAIR:]))
        ).astype(BF16)
    total = out_ref.shape[0]
    head_ref[...] = out_ref[:HALO, :]
    tail_ref[...] = out_ref[total - HALO :, :]


def conv_rows(padded, start, piece, cols, taps, scale, shift):
    window = padded[pl.ds(start, piece + 2 * HALO), cols]
    convolved = None
    for residue in range(8):
        part = None
        for offset in range(residue, KERNEL + 1, 8):
            if offset == 0:
                continue
            base = offset - residue
            term = taps[offset - 1] * window[base : base + piece + 8]
            part = term if part is None else part + term
        part = part[residue : residue + piece]
        convolved = part if convolved is None else convolved + part
    value = convolved * scale + shift
    return (value / (1.0 + jnp.exp(-value))).astype(BF16)


def conv_inner_kernel(gated_ref, taps_ref, bn_ref, activated_ref, padded):
    total, width = gated_ref.shape
    piece = 32
    padded[HALO : HALO + total, :] = gated_ref[...].astype(F32)
    for col in range(0, width, PAIR):
        cols = slice(col, col + PAIR)
        taps = [taps_ref[j : j + 1, cols] for j in range(KERNEL)]
        scale, shift = bn_ref[0:1, cols], bn_ref[1:2, cols]

        def block(index, carry):
            start = pl.multiple_of(HALO + index * piece, HALO)
            activated_ref[pl.ds(start, piece), cols] = conv_rows(padded, start, piece, cols, taps, scale, shift)
            return carry

        lax.fori_loop(0, total // piece - 1, block, 0, unroll=3)


def conv_outer_kernel(gated_ref, left_ref, right_ref, taps_ref, bn_ref, activated_ref, w_ref, keep_ref, send_ref, padded):
    total, width = gated_ref.shape
    half = keep_ref.shape[1]
    ends = []
    for first, rows in (
        (True, (left_ref[...], gated_ref[: 2 * HALO, :])),
        (False, (gated_ref[total - 2 * HALO :, :], right_ref[...])),
    ):
        padded[...] = jnp.concatenate([part.astype(F32) for part in rows], axis=0)
        parts = []
        for col in range(0, width, PAIR):
            cols = slice(col, col + PAIR)
            taps = [taps_ref[j : j + 1, cols] for j in range(KERNEL)]
            parts.append(conv_rows(padded, 0, HALO, cols, taps, bn_ref[0:1, cols], bn_ref[1:2, cols]))
        ends.append(jnp.concatenate(parts, axis=1))
    share = jnp.concatenate([ends[0], activated_ref[HALO : total - HALO, :], ends[1]], axis=0)
    keep_ref[...] = jnp.dot(share, w_ref[:, :half], preferred_element_type=F32).astype(BF16)
    send_ref[...] = jnp.dot(share, w_ref[:, half:], preferred_element_type=F32).astype(BF16)


def pad_columns(weight, width):
    if weight.shape[1] == width:
        return weight
    return jnp.pad(weight, ((0, 0), (0, width - weight.shape[1])))


def on_device(
    frames_in,
    norm1_gain,
    norm1_bias,
    w_query,
    w_key,
    w_value,
    w_out,
    norm2_gain,
    norm2_bias,
    w_glu_value,
    w_glu_gate,
    depth_kernel,
    bn_scale,
    bn_shift,
    w_proj,
):
    frames, width = frames_in.shape
    grid, ctx = lax.axis_size("grid"), lax.axis_size("ctx")
    me = lax.axis_index("grid")
    place = me.astype(jnp.int32).reshape(1)
    order = list(range(0, grid, CORES)) + list(range(1, grid, CORES))
    padded = -(-width // PAIR) * PAIR
    query_rows = math.gcd(frames, 256)

    def by_distance(cells):
        return jnp.concatenate(
            [lax.dynamic_slice_in_dim(cells, (me ^ r) * width, width, 1) for r in order], axis=1
        )

    def over_chips(block):
        return [exchange(block, "grid", CORES * a) for a in range(1, grid // CORES)]

    def other_core(blocks):
        return [exchange(block, "grid", 1) for block in blocks]

    vectors = [norm1_gain, norm1_bias, norm2_gain, norm2_bias]
    (gains,) = kernel_call(
        stack_kernel,
        [((8, width), F32)],
        vectors,
        spaces={i: pltpu.HBM for i in range(len(vectors))},
        scratch=[pltpu.VMEM((width,), BF16)] * len(vectors) + [pltpu.SemaphoreType.DMA((len(vectors),))],
    )
    gains = lax.all_gather(gains, "grid", axis=0, tiled=True)
    raw = {0: frames_in}
    chips = {0: over_chips(frames_in)}
    for k in reversed(range(ctx.bit_length() - 1)):
        raw[1 << k] = exchange(frames_in, "ctx", 1 << k)

    w_query, w_key, w_value, w_glu_value, w_glu_gate = (
        pad_columns(weight, padded) for weight in (w_query, w_key, w_value, w_glu_value, w_glu_gate)
    )
    if width % PAIR:
        row_pad = ((0, padded - width), (0, 0))
        w_p = jnp.pad(by_distance(w_proj), row_pad)
    else:
        (w_p,) = kernel_call(
            functools.partial(reorder_kernel, order),
            [(w_proj.shape, BF16)],
            [place, w_proj],
            spaces={0: pltpu.SMEM, 1: pltpu.HBM},
            scratch=[pltpu.SemaphoreType.DMA((grid,))],
        )
    taps = pad_columns(depth_kernel, padded)
    bn = pad_columns(jnp.stack([bn_scale, bn_shift]), padded)
    qkv, qkv_sums = folded(place, order, 0, gains, (w_key, w_value, w_query))
    chips[0] = [after(block, qkv_sums) for block in chips[0]]
    glu, glu_sums = folded(place, order, 2, gains, (w_glu_value, w_glu_gate))

    parts = lax.axis_size("parts")
    part = lax.axis_index("parts").astype(jnp.int32).reshape(1)
    if parts == 2:
        (half,) = kernel_call(
            half_kernel,
            [((width // 2, w_out.shape[1]), BF16)],
            [part, w_out],
            spaces={0: pltpu.SMEM, 1: pltpu.HBM},
            scratch=[pltpu.SemaphoreType.DMA((1,))],
        )
    else:
        half = w_out
    crossed = over_chips(half)
    state_shape = ((frames, 4 * padded), F32)
    token_shape = ((8, 128), F32)
    wide, narrow = ((frames, 2 * padded), BF16), ((frames, padded), BF16)
    chips[1] = [exchange(block, "ctx", 1) for block in chips[0]]
    own = [frames_in] + chips[0]
    own_blocks = own + other_core(own)
    n = len(own_blocks)
    early = [*[raw[s] for s in raw if s], *crossed]
    queries, keys, values = kernel_call(
        functools.partial(project_kernel, n, True),
        [wide, narrow, wide],
        [*own_blocks, qkv, qkv_sums, *early],
        spaces={n + 2 + i: pl.ANY for i in range(len(early))},
    )
    swapped = [exchange(block, "parts", 1) for block in crossed] if parts == 2 else []
    pieces = [w_out]
    for a, block in enumerate(crossed):
        pieces += [block, swapped[a]] if swapped else [block]
    pieces = pieces + other_core(pieces)

    def prepare(s):
        if 2 <= s < ctx:
            low = s & -s
            if s != low:
                raw[s] = after(exchange(raw[s ^ low], "ctx", low), token)
            chips[s] = over_chips(raw[s])

    prepare(2)
    state, token = kernel_call(
        functools.partial(attend_kernel, True, False, query_rows),
        [state_shape, token_shape],
        [queries, keys, values],
    )
    moved = {1: [after(block, keys) for block in chips[1]]}
    for s in range(1, ctx):
        last = s == ctx - 1
        prepare(s + 2)
        if not last:
            moved[s + 1] = [after(block, token) for block in chips[s + 1]]
        mine = [raw[s]] + moved[s]
        keys, values = kernel_call(
            functools.partial(project_kernel, n, False),
            [narrow, wide],
            [*mine, *other_core(mine), qkv, qkv_sums],
        )
        behind = [raw[s + 2]] if s + 2 < ctx else swapped
        if s > 1 and not last:
            behind = behind + moved[s + 1]
        results = kernel_call(
            functools.partial(attend_kernel, False, last, query_rows),
            [narrow] if last else [state_shape, token_shape],
            [queries, keys, values, state, *behind],
            spaces={4 + i: pl.ANY for i in range(len(behind))},
            aliases={} if last else {3: 0},
            scratch=[pltpu.VMEM(*state_shape)],
        )
        if last:
            (attended,) = results
        else:
            state, token = results
    attended = [attended] + [after(block, glu_sums, w_p) for block in over_chips(attended)]
    attended = attended + other_core(attended)
    if width % PAIR:
        pieces = [by_distance(piece) for piece in pieces]
    middle, gated, head, tail = kernel_call(
        functools.partial(middle_kernel, n, order),
        [
            ((frames, width), BF16),
            ((frames, padded), BF16),
            ((HALO, padded), BF16),
            ((HALO, padded), BF16),
        ],
        [place, part, *attended, *own_blocks, *pieces, glu, glu_sums],
        spaces={0: pltpu.SMEM, 1: pltpu.SMEM},
        scratch=[pltpu.VMEM((frames, grid * width), BF16)],
    )
    left = lax.ppermute(tail, "ctx", [(i, i + 1) for i in range(ctx - 1)])
    right = lax.ppermute(head, "ctx", [(i + 1, i) for i in range(ctx - 1)])
    (activated,) = kernel_call(
        conv_inner_kernel,
        [((frames, padded), BF16)],
        [gated, taps, bn],
        scratch=[pltpu.VMEM((frames + 2 * HALO, padded), F32)],
    )
    keep, send = kernel_call(
        conv_outer_kernel,
        [((frames, grid // CORES * width), BF16)] * 2,
        [gated, left, right, taps, bn, activated, w_p],
        scratch=[pltpu.VMEM((3 * HALO, padded), F32)],
    )
    pair_sum = keep.astype(F32) + exchange(send, "grid", 1).astype(F32)
    result = middle.astype(F32) + pair_sum[:, :width]
    for a in range(1, grid // CORES):
        share = pair_sum[:, a * width : (a + 1) * width].astype(BF16)
        result = result + exchange(share, "grid", CORES * a).astype(F32)
    return result.astype(BF16)


def solution(mesh):
    return jax.shard_map(
        on_device,
        mesh=mesh,
        in_specs=(
            P(("parts", "ctx"), "grid"),
            P("grid"),
            P("grid"),
            P(None, "grid"),
            P(None, "grid"),
            P(None, "grid"),
            P("grid", None),
            P("grid"),
            P("grid"),
            P(None, "grid"),
            P(None, "grid"),
            P(None, "grid"),
            P("grid"),
            P("grid"),
            P("grid", None),
        ),
        out_specs=P(("parts", "ctx"), "grid"),
        check_vma=False,
    )
```

```python
import functools
import math

import jax
import jax.numpy as jnp
from jax import lax
from jax.experimental import pallas as pl
from jax.experimental.pallas import tpu as pltpu
from jax.sharding import PartitionSpec as P

HEAD_DIM = 64
PAIR = 2 * HEAD_DIM
KERNEL = 31
HALF = 15
HALO = 16
EPSILON = 1e-05
CORES = 2
VMEM_BYTES = 16 * 1024 * 1024
BF16 = jnp.bfloat16
F32 = jnp.float32
SCORE_SCALE = math.log2(math.e) / math.sqrt(HEAD_DIM)


def exchange(cells, axis, distance):
    count = lax.axis_size(axis)
    return lax.ppermute(cells, axis, [(i, i ^ distance) for i in range(count)])


def kernel_call(body, outs, operands, spaces=None, scratch=(), aliases=None):
    spaces = spaces or {}
    operands = [
        pltpu.with_memory_space_constraint(cells, pltpu.HBM) if spaces.get(i) == pltpu.HBM else cells
        for i, cells in enumerate(operands)
    ]
    in_specs = [
        pl.BlockSpec(memory_space=spaces.get(i, pltpu.VMEM)) for i in range(len(operands))
    ]
    return pl.pallas_call(
        body,
        in_specs=in_specs,
        out_specs=tuple(pl.BlockSpec(memory_space=pltpu.VMEM) for _ in outs),
        out_shape=tuple(jax.ShapeDtypeStruct(shape, dtype) for shape, dtype in outs),
        scratch_shapes=list(scratch),
        input_output_aliases=aliases or {},
        compiler_params=pltpu.CompilerParams(vmem_limit_bytes=VMEM_BYTES),
        cost_estimate=pl.CostEstimate(flops=1000, bytes_accessed=1000, transcendentals=0),
    )(*operands)


def after(cells, *done):
    def body(*refs):
        pass

    anywhere = pl.BlockSpec(memory_space=pl.ANY)
    return pl.pallas_call(
        body,
        in_specs=[anywhere] * (1 + len(done)),
        out_specs=anywhere,
        out_shape=jax.ShapeDtypeStruct(cells.shape, cells.dtype),
        input_output_aliases={0: 0},
        compiler_params=pltpu.CompilerParams(vmem_limit_bytes=64 * 1024),
        cost_estimate=pl.CostEstimate(flops=0, bytes_accessed=0, transcendentals=0),
    )(cells, *done)


def fold_kernel(order, which, count, me_ref, gains_ref, *refs):
    sources, (folded_ref, sums_ref), weights, done = refs[:count], refs[count : count + 2], refs[count + 2 : -1], refs[-1]
    copies = [pltpu.make_async_copy(sources[n], weights[n], done.at[n]) for n in range(count)]
    for copy in copies:
        copy.start()
    width = gains_ref.shape[1]
    columns = weights[0].shape[1]
    factors = []
    for r in order:
        gains = gains_ref[pl.ds(pl.multiple_of((me_ref[0] ^ r) * 8, 8), 8), :]
        gain = jnp.transpose(jnp.broadcast_to(gains[which : which + 1, :], (PAIR, width)))
        bias = jnp.broadcast_to(gains[which + 1 : which + 2, :], (8, width)).astype(BF16)
        factors.append((gain, bias))
    for n, ref in enumerate(weights):
        copies[n].wait()
        total = jnp.zeros((8, columns), F32)
        for k, r in enumerate(order):
            gain, bias = factors[k]
            start = pl.multiple_of((me_ref[0] ^ r) * width, width)
            block = ref[pl.ds(start, width), :]
            total = total + jnp.dot(bias, block, preferred_element_type=F32)
            for j in range(columns // PAIR):
                target = (j * count + n) * PAIR
                folded_ref[k * width : (k + 1) * width, target : target + PAIR] = (
                    block[:, j * PAIR : (j + 1) * PAIR].astype(F32) * gain
                ).astype(BF16)
        for j in range(columns // PAIR):
            target = (j * count + n) * PAIR
            sums_ref[1:2, target : target + PAIR] = total[0:1, j * PAIR : (j + 1) * PAIR]
    sums = jnp.dot(jnp.ones((8, folded_ref.shape[0]), BF16), folded_ref[...], preferred_element_type=F32)
    sums_ref[0:1, :] = sums[0:1]


def folded(me, order, which, gains, weights):
    rows, columns = weights[0].shape
    total = columns * len(weights)
    spaces = {2 + n: pltpu.HBM for n in range(len(weights))}
    return kernel_call(
        functools.partial(fold_kernel, order, which, len(weights)),
        [((rows, total), BF16), ((2, total), F32)],
        [me, gains, *weights],
        spaces={0: pltpu.SMEM, **spaces},
        scratch=[pltpu.VMEM((rows, columns), BF16)] * len(weights) + [pltpu.SemaphoreType.DMA((len(weights),))],
    )


def stack_kernel(*refs):
    count = (len(refs) - 2) // 2
    sources, out_ref, rows, done = refs[:count], refs[count], refs[count + 1 : -1], refs[-1]
    copies = [pltpu.make_async_copy(sources[i], rows[i], done.at[i]) for i in range(count)]
    for copy in copies:
        copy.start()
    out_ref[...] = jnp.zeros_like(out_ref)
    for i, copy in enumerate(copies):
        copy.wait()
        out_ref[i : i + 1, :] = rows[i][...].astype(F32).reshape(1, out_ref.shape[1])


def reorder_kernel(order, me_ref, source_ref, out_ref, done):
    width = source_ref.shape[1] // len(order)
    copies = []
    for k, r in enumerate(order):
        cols = pl.ds(pl.multiple_of((me_ref[0] ^ r) * width, PAIR), width)
        copies.append(
            pltpu.make_async_copy(source_ref.at[:, cols], out_ref.at[:, k * width : (k + 1) * width], done.at[k])
        )
        copies[-1].start()
    for copy in copies:
        copy.wait()


def half_kernel(part_ref, source_ref, half_ref, done):
    rows = half_ref.shape[0]
    copy = pltpu.make_async_copy(
        source_ref.at[pl.ds(pl.multiple_of(part_ref[0] * rows, rows), rows), :], half_ref, done.at[0]
    )
    copy.start()
    copy.wait()


def row_statistics(refs):
    rows, width = refs[0].shape
    full = width * len(refs)
    means, scales = [], []
    step = math.gcd(rows, 64)
    for start in range(0, rows, step):
        parts = [ref[start : start + step, :].astype(F32) for ref in refs]
        mean = sum(jnp.sum(part, axis=1, keepdims=True) for part in parts) / full
        variance = sum(jnp.sum(jnp.square(part - mean), axis=1, keepdims=True) for part in parts) / full
        means.append(mean)
        scales.append(lax.rsqrt(variance + EPSILON))
    return jnp.concatenate(means, axis=0), jnp.concatenate(scales, axis=0)


def norm_product(cells, mean, scale, folded_ref, sums_ref, start, columns):
    cols = slice(start, start + columns)
    product = jnp.dot(cells, folded_ref[:, cols], preferred_element_type=F32)
    return (product - mean * sums_ref[0:1, cols]) * scale + sums_ref[1:2, cols]


def lane_masks():
    lanes = lax.broadcasted_iota(jnp.int32, (1, PAIR), 1)
    return lanes < HEAD_DIM


def keys_values(projected):
    low = lane_masks()
    values = projected[:, PAIR : 2 * PAIR]
    return (
        projected[:, :PAIR].astype(BF16),
        jnp.where(low, values, 1.0).astype(BF16),
        jnp.where(low, 1.0, values).astype(BF16),
    )


def project_kernel(count, first, *refs):
    blocks, (folded_ref, sums_ref, *refs) = refs[:count], refs[count:]
    key_ref, value_ref = refs[-2:]
    query_ref = refs[-3] if first else None
    mean, scale = row_statistics(blocks)
    cells = jnp.concatenate([ref[...] for ref in blocks], axis=1)
    low = lane_masks()
    for j in range(key_ref.shape[1] // PAIR):
        columns = (3 if first else 2) * PAIR
        projected = norm_product(cells, mean, scale, folded_ref, sums_ref, j * 3 * PAIR, columns)
        base = 2 * j * PAIR
        (
            key_ref[:, j * PAIR : (j + 1) * PAIR],
            value_ref[:, base : base + PAIR],
            value_ref[:, base + PAIR : base + 2 * PAIR],
        ) = keys_values(projected)
        if first:
            queries = projected[:, 2 * PAIR :] * SCORE_SCALE
            query_ref[:, base : base + PAIR] = jnp.where(low, queries, 0.0).astype(BF16)
            query_ref[:, base + PAIR : base + 2 * PAIR] = jnp.where(low, 0.0, queries).astype(BF16)


def chunks_of(spans, rows):
    pieces, local = [], 0
    for start, size in spans:
        step = math.gcd(size, rows)
        for offset in range(0, size, step):
            pieces.append((slice(start + offset, start + offset + step), slice(local, local + step)))
            local += step
    return pieces


def attend_pair(pair, chunks, query_ref, keys, values, state_ref):
    for source, rows in chunks:
        for head in range(2):
            index = 2 * pair + head
            queries = query_ref[source, index * PAIR : (index + 1) * PAIR]
            scores = lax.dot_general(
                queries, keys, (((1,), (1,)), ((), ())), preferred_element_type=F32
            )
            peak = jnp.max(scores, axis=1, keepdims=True)
            soft = jnp.exp2(scores - peak).astype(BF16)
            sums = jnp.dot(soft, values[head], preferred_element_type=F32)
            state_ref[rows, 2 * index * PAIR : (2 * index + 1) * PAIR] = sums
            state_ref[rows, (2 * index + 1) * PAIR : (2 * index + 2) * PAIR] = jnp.broadcast_to(
                peak, (peak.shape[0], PAIR)
            )


def merge_head(old_ref, part_ref, source, rows, index):
    sums = slice(2 * index * PAIR, (2 * index + 1) * PAIR)
    peaks = slice((2 * index + 1) * PAIR, (2 * index + 2) * PAIR)
    old_peak, part_peak = old_ref[source, peaks], part_ref[rows, peaks]
    peak = jnp.maximum(old_peak, part_peak)
    total = old_ref[source, sums] * jnp.exp2(old_peak - peak) + part_ref[rows, sums] * jnp.exp2(part_peak - peak)
    return total, peak


def attend_kernel(first, last, chunks, query_ref, key_ref, value_ref, *refs):
    if last:
        old_ref, attended, part = refs[0], refs[-2], refs[-1]
    elif first:
        part, token_ref = refs[-2:]
    else:
        old_ref, (state_ref, token_ref, part) = refs[0], refs[-3:]
    if not last:
        token_ref[...] = jnp.zeros_like(token_ref)
    pairs = query_ref.shape[1] // (2 * PAIR)
    for j in range(pairs):
        values = [value_ref[:, n * PAIR : (n + 1) * PAIR] for n in (2 * j, 2 * j + 1)]
        attend_pair(j, chunks, query_ref, key_ref[:, j * PAIR : (j + 1) * PAIR], values, part)
    if first:
        return
    low = lane_masks()
    for source, rows in chunks:
        for j in range(pairs):
            heads = [merge_head(old_ref, part, source, rows, 2 * j + head) for head in range(2)]
            if last:
                (one, _), (two, _) = heads
                both = jnp.where(low, one, two)
                weight = pltpu.roll(jnp.where(low, two, one), HEAD_DIM, 1)
                attended[rows, j * PAIR : (j + 1) * PAIR] = (both / weight).astype(BF16)
            else:
                for head, (sums, peak) in enumerate(heads):
                    at = 2 * (2 * j + head) * PAIR
                    state_ref[rows, at : at + PAIR] = sums
                    state_ref[rows, at + PAIR : at + 2 * PAIR] = peak


def middle_kernel(count, order, spans, me_ref, part_ref, *refs):
    attended, frames_refs, refs = refs[:count], refs[count : 2 * count], refs[2 * count :]
    *pieces, folded_ref, sums_ref, own_ref, out_ref, head_ref, tail_ref, middle = refs
    total = out_ref.shape[0]
    width = frames_refs[0].shape[1]
    cells = jnp.concatenate([ref[:, :width] for ref in attended], axis=1)
    swap = part_ref[0] != 0

    def weights(k):
        if width % PAIR:
            cols = slice(k * width, (k + 1) * width)
        else:
            cols = pl.ds(pl.multiple_of((me_ref[0] ^ order[k]) * width, PAIR), width)
        rows, index = [], 0
        while index < len(pieces):
            mine = pieces[index][:, cols]
            index += 1
            if mine.shape[0] < width:
                other = pieces[index][:, cols]
                index += 1
                mine = jnp.concatenate([jnp.where(swap, other, mine), jnp.where(swap, mine, other)], axis=0)
            rows.append(mine)
        return jnp.concatenate(rows, axis=0)

    for k in range(0, count, 2):
        both = jnp.concatenate([weights(k), weights(k + 1)], axis=1)
        share = jnp.dot(cells, both, preferred_element_type=F32)
        for n in range(2):
            cols = slice((k + n) * width, (k + n + 1) * width)
            own = jnp.concatenate([frames_refs[k + n][start : start + size, :] for start, size in spans], axis=0)
            middle[:, cols] = (own.astype(F32) + share[:, n * width : (n + 1) * width]).astype(BF16)
    own_ref[...] = middle[:, :width]
    mean, scale = row_statistics((middle,))
    cells = middle[...]
    for j in range(out_ref.shape[1] // PAIR):
        both = norm_product(cells, mean, scale, folded_ref, sums_ref, j * 2 * PAIR, 2 * PAIR)
        out_ref[:, j * PAIR : (j + 1) * PAIR] = (
            both[:, :PAIR] / (1.0 + jnp.exp(-both[:, PAIR:]))
        ).astype(BF16)
    head_ref[...] = out_ref[:HALO, :]
    tail_ref[...] = out_ref[total - HALO :, :]


def conv_rows(padded, start, piece, cols, taps, scale, shift):
    window = padded[pl.ds(start, piece + 2 * HALO), cols]
    convolved = None
    for residue in range(8):
        part = None
        for offset in range(residue, KERNEL + 1, 8):
            if offset == 0:
                continue
            base = offset - residue
            term = taps[offset - 1] * window[base : base + piece + 8]
            part = term if part is None else part + term
        part = part[residue : residue + piece]
        convolved = part if convolved is None else convolved + part
    value = convolved * scale + shift
    return (value / (1.0 + jnp.exp(-value))).astype(BF16)


def conv_kernel(outer, first_ref, second_ref, *refs):
    if outer:
        left_ref, right_ref, *refs = refs
    taps_ref, bn_ref, w_ref, keep_ref, send_ref, padded, activated = refs
    total, width = first_ref.shape
    half = keep_ref.shape[1]
    piece, quarter = 32, total // 2
    if outer:
        runs = (
            (left_ref[...], first_ref[:quarter, :], second_ref[:HALO, :]),
            (second_ref[total - HALO :, :], first_ref[quarter:, :], right_ref[...]),
        )
    else:
        runs = ((first_ref[quarter - HALO : quarter, :], second_ref[...], first_ref[quarter : quarter + HALO, :]),)
    at = 0
    for before, rows, behind in runs:
        count = rows.shape[0]
        padded[0:HALO, :] = before.astype(F32)
        padded[HALO : HALO + count, :] = rows.astype(F32)
        padded[HALO + count : 2 * HALO + count, :] = behind.astype(F32)
        for col in range(0, width, PAIR):
            cols = slice(col, col + PAIR)
            taps = [taps_ref[j : j + 1, cols] for j in range(KERNEL)]
            scale, shift = bn_ref[0:1, cols], bn_ref[1:2, cols]

            def block(index, carry, at=at):
                start = pl.multiple_of(index * piece, piece)
                target = pl.multiple_of(at + index * piece, piece)
                activated[pl.ds(target, piece), cols] = conv_rows(padded, start, piece, cols, taps, scale, shift)
                return carry

            lax.fori_loop(0, count // piece, block, 0, unroll=4)
        at += count
    share = activated[...]
    send_ref[...] = jnp.dot(share, w_ref[:, half:], preferred_element_type=F32).astype(BF16)
    keep_ref[...] = jnp.dot(share, w_ref[:, :half], preferred_element_type=F32).astype(BF16)


def pad_columns(weight, width):
    if weight.shape[1] == width:
        return weight
    return jnp.pad(weight, ((0, 0), (0, width - weight.shape[1])))


def on_device(
    frames_in,
    norm1_gain,
    norm1_bias,
    w_query,
    w_key,
    w_value,
    w_out,
    norm2_gain,
    norm2_bias,
    w_glu_value,
    w_glu_gate,
    depth_kernel,
    bn_scale,
    bn_shift,
    w_proj,
):
    frames, width = frames_in.shape
    grid, ctx = lax.axis_size("grid"), lax.axis_size("ctx")
    me = lax.axis_index("grid")
    place = me.astype(jnp.int32).reshape(1)
    order = list(range(0, grid, CORES)) + list(range(1, grid, CORES))
    padded = -(-width // PAIR) * PAIR
    query_rows, every = 256, ((0, frames),)

    def by_distance(cells):
        return jnp.concatenate(
            [lax.dynamic_slice_in_dim(cells, (me ^ r) * width, width, 1) for r in order], axis=1
        )

    def over_chips(block):
        return [exchange(block, "grid", CORES * a) for a in range(1, grid // CORES)]

    def other_core(blocks):
        return [exchange(block, "grid", 1) for block in blocks]

    vectors = [norm1_gain, norm1_bias, norm2_gain, norm2_bias]
    (gains,) = kernel_call(
        stack_kernel,
        [((8, width), F32)],
        vectors,
        spaces={i: pltpu.HBM for i in range(len(vectors))},
        scratch=[pltpu.VMEM((width,), BF16)] * len(vectors) + [pltpu.SemaphoreType.DMA((len(vectors),))],
    )
    gains = lax.all_gather(gains, "grid", axis=0, tiled=True)
    raw = {0: frames_in}
    chips = {0: over_chips(frames_in)}
    for k in reversed(range(ctx.bit_length() - 1)):
        raw[1 << k] = exchange(frames_in, "ctx", 1 << k)

    w_query, w_key, w_value, w_glu_value, w_glu_gate = (
        pad_columns(weight, padded) for weight in (w_query, w_key, w_value, w_glu_value, w_glu_gate)
    )
    if width % PAIR:
        row_pad = ((0, padded - width), (0, 0))
        w_p = jnp.pad(by_distance(w_proj), row_pad)
    else:
        (w_p,) = kernel_call(
            functools.partial(reorder_kernel, order),
            [(w_proj.shape, BF16)],
            [place, w_proj],
            spaces={0: pltpu.SMEM, 1: pltpu.HBM},
            scratch=[pltpu.SemaphoreType.DMA((grid,))],
        )
    taps = pad_columns(depth_kernel, padded)
    bn = pad_columns(jnp.stack([bn_scale, bn_shift]), padded)
    qkv, qkv_sums = folded(place, order, 0, gains, (w_key, w_value, w_query))
    chips[0] = [after(block, qkv_sums) for block in chips[0]]
    glu, glu_sums = folded(place, order, 2, gains, (w_glu_value, w_glu_gate))

    parts = lax.axis_size("parts")
    part = lax.axis_index("parts").astype(jnp.int32).reshape(1)
    if parts == 2:
        (half,) = kernel_call(
            half_kernel,
            [((width // 2, w_out.shape[1]), BF16)],
            [part, w_out],
            spaces={0: pltpu.SMEM, 1: pltpu.HBM},
            scratch=[pltpu.SemaphoreType.DMA((1,))],
        )
    else:
        half = w_out
    crossed = over_chips(after(half, gains))
    state_shape = ((frames, 4 * padded), F32)
    token_shape = ((8, 128), F32)
    wide, narrow = ((frames, 2 * padded), BF16), ((frames, padded), BF16)
    chips[1] = [exchange(block, "ctx", 1) for block in chips[0]]
    own = [frames_in] + chips[0]
    own_blocks = own + other_core(own)
    n = len(own_blocks)
    raw.update({s: after(block, glu_sums, w_p) for s, block in raw.items() if s > 1})
    early = [*[raw[s] for s in raw if s], *crossed]
    queries, keys, values = kernel_call(
        functools.partial(project_kernel, n, True),
        [wide, narrow, wide],
        [*own_blocks, qkv, qkv_sums, *early],
        spaces={n + 2 + i: pl.ANY for i in range(len(early))},
    )
    swapped = [exchange(block, "parts", 1) for block in crossed] if parts == 2 else []
    pieces = [w_out]
    for a, block in enumerate(crossed):
        pieces += [block, swapped[a]] if swapped else [block]
    pieces = pieces + other_core(pieces)

    def prepare(s):
        if 2 <= s < ctx:
            low = s & -s
            if s != low:
                raw[s] = after(exchange(raw[s ^ low], "ctx", low), token)
            chips[s] = over_chips(raw[s])

    prepare(2)
    state, token = kernel_call(
        functools.partial(attend_kernel, True, False, chunks_of(every, query_rows)),
        [state_shape, token_shape],
        [queries, keys, values],
    )
    moved = {1: [after(block, keys) for block in chips[1]]}
    for s in range(1, ctx):
        last = s == ctx - 1
        prepare(s + 2)
        if not last:
            moved[s + 1] = [after(block, token) for block in chips[s + 1]]
        mine = [raw[s]] + moved[s]
        keys, values = kernel_call(
            functools.partial(project_kernel, n, False),
            [narrow, wide],
            [*mine, *other_core(mine), qkv, qkv_sums],
        )
        if last:
            break
        behind = [raw[s + 2]] if s + 2 < ctx else []
        if s > 1:
            behind = behind + moved[s + 1]
        state, token = kernel_call(
            functools.partial(attend_kernel, False, False, chunks_of(every, query_rows)),
            [state_shape, token_shape],
            [queries, keys, values, state, *behind],
            spaces={4 + i: pl.ANY for i in range(len(behind))},
            aliases={3: 0},
            scratch=[pltpu.VMEM(*state_shape)],
        )
    rows, quarter = frames // 2, frames // 4
    spans = (((0, quarter), (3 * quarter, quarter)), ((quarter, rows),))
    attended = []
    for h in range(2):
        (mine,) = kernel_call(
            functools.partial(attend_kernel, False, True, chunks_of(spans[h], query_rows)),
            [((rows, padded), BF16)],
            [queries, keys, values, state, *swapped],
            spaces={4 + i: pl.ANY for i in range(len(swapped))},
            scratch=[pltpu.VMEM((rows, 4 * padded), F32)],
        )
        attended.append([mine] + over_chips(mine))
    if width % PAIR:
        pieces = [by_distance(piece) for piece in pieces]
    middle, gated = [], []
    for h in range(2):
        mine = attended[h]
        done = gated[0] if h else attended[1][0]
        mine = mine[:1] + [after(block, done) for block in mine[1:]]
        results = kernel_call(
            functools.partial(middle_kernel, n, order, spans[h]),
            [((rows, width), BF16), ((rows, padded), BF16), ((HALO, padded), BF16), ((HALO, padded), BF16)],
            [place, part, *mine, *other_core(mine), *own_blocks, *pieces, glu, glu_sums],
            spaces={0: pltpu.SMEM, 1: pltpu.SMEM},
            scratch=[pltpu.VMEM((rows, grid * width), BF16)],
        )
        middle.append(results[0])
        gated.append(results[1])
        if h == 0:
            left = lax.ppermute(results[3], "ctx", [(i, i + 1) for i in range(ctx - 1)])
            right = lax.ppermute(results[2], "ctx", [(i + 1, i) for i in range(ctx - 1)])
    outs = [None, None]
    for h, around in ((1, []), (0, [left, right])):
        keep, send = kernel_call(
            functools.partial(conv_kernel, h == 0),
            [((rows, grid // CORES * width), BF16)] * 2,
            [*gated, *around, taps, bn, w_p],
            scratch=[pltpu.VMEM((rows + 2 * HALO, padded), F32), pltpu.VMEM((rows, padded), BF16)],
        )
        theirs = exchange(send, "grid", 1)

        def pair_sum(a):
            cols = slice(a * width, (a + 1) * width)
            return keep[:, cols].astype(F32) + theirs[:, cols].astype(F32)

        result = middle[h].astype(F32) + pair_sum(0)
        for a in range(1, grid // CORES):
            result = result + exchange(pair_sum(a).astype(BF16), "grid", CORES * a).astype(F32)
        outs[h] = result.astype(BF16)
    return jnp.concatenate([outs[0][:quarter], outs[1], outs[0][quarter:]], axis=0)


def solution(mesh):
    return jax.shard_map(
        on_device,
        mesh=mesh,
        in_specs=(
            P(("parts", "ctx"), "grid"),
            P("grid"),
            P("grid"),
            P(None, "grid"),
            P(None, "grid"),
            P(None, "grid"),
            P("grid", None),
            P("grid"),
            P("grid"),
            P(None, "grid"),
            P(None, "grid"),
            P(None, "grid"),
            P("grid"),
            P("grid"),
            P("grid", None),
        ),
        out_specs=P(("parts", "ctx"), "grid"),
        check_vma=False,
    )
```

```python
import functools
import math

import jax
import jax.numpy as jnp
from jax import lax
from jax.experimental import pallas as pl
from jax.experimental.pallas import tpu as pltpu
from jax.sharding import PartitionSpec as P

HEAD_DIM = 64
PAIR = 2 * HEAD_DIM
KERNEL = 31
HALF = 15
HALO = 16
EPSILON = 1e-05
CORES = 2
VMEM_BYTES = 16 * 1024 * 1024
BF16 = jnp.bfloat16
F32 = jnp.float32
SCORE_SCALE = math.log2(math.e) / math.sqrt(HEAD_DIM)


def exchange(cells, axis, distance):
    count = lax.axis_size(axis)
    return lax.ppermute(cells, axis, [(i, i ^ distance) for i in range(count)])


def kernel_call(body, outs, operands, spaces=None, scratch=(), aliases=None):
    spaces = spaces or {}
    operands = [
        pltpu.with_memory_space_constraint(cells, pltpu.HBM) if spaces.get(i) == pltpu.HBM else cells
        for i, cells in enumerate(operands)
    ]
    in_specs = [
        pl.BlockSpec(memory_space=spaces.get(i, pltpu.VMEM)) for i in range(len(operands))
    ]
    return pl.pallas_call(
        body,
        in_specs=in_specs,
        out_specs=tuple(pl.BlockSpec(memory_space=pltpu.VMEM) for _ in outs),
        out_shape=tuple(jax.ShapeDtypeStruct(shape, dtype) for shape, dtype in outs),
        scratch_shapes=list(scratch),
        input_output_aliases=aliases or {},
        compiler_params=pltpu.CompilerParams(vmem_limit_bytes=VMEM_BYTES),
        cost_estimate=pl.CostEstimate(flops=1000, bytes_accessed=1000, transcendentals=0),
    )(*operands)


def after(cells, *done):
    def body(*refs):
        pass

    anywhere = pl.BlockSpec(memory_space=pl.ANY)
    return pl.pallas_call(
        body,
        in_specs=[anywhere] * (1 + len(done)),
        out_specs=anywhere,
        out_shape=jax.ShapeDtypeStruct(cells.shape, cells.dtype),
        input_output_aliases={0: 0},
        compiler_params=pltpu.CompilerParams(vmem_limit_bytes=64 * 1024),
        cost_estimate=pl.CostEstimate(flops=0, bytes_accessed=0, transcendentals=0),
    )(cells, *done)


def fold_kernel(order, which, count, me_ref, gains_ref, *refs):
    sources, (folded_ref, sums_ref), weights, done = refs[:count], refs[count : count + 2], refs[count + 2 : -1], refs[-1]
    copies = [pltpu.make_async_copy(sources[n], weights[n], done.at[n]) for n in range(count)]
    for copy in copies:
        copy.start()
    width = gains_ref.shape[1]
    columns = weights[0].shape[1]
    factors = []
    for r in order:
        gains = gains_ref[pl.ds(pl.multiple_of((me_ref[0] ^ r) * 8, 8), 8), :]
        gain = jnp.transpose(jnp.broadcast_to(gains[which : which + 1, :], (PAIR, width)))
        bias = jnp.broadcast_to(gains[which + 1 : which + 2, :], (8, width)).astype(BF16)
        factors.append((gain, bias))
    for n, ref in enumerate(weights):
        copies[n].wait()
        total = jnp.zeros((8, columns), F32)
        for k, r in enumerate(order):
            gain, bias = factors[k]
            start = pl.multiple_of((me_ref[0] ^ r) * width, width)
            block = ref[pl.ds(start, width), :]
            total = total + jnp.dot(bias, block, preferred_element_type=F32)
            for j in range(columns // PAIR):
                target = (j * count + n) * PAIR
                folded_ref[k * width : (k + 1) * width, target : target + PAIR] = (
                    block[:, j * PAIR : (j + 1) * PAIR].astype(F32) * gain
                ).astype(BF16)
        for j in range(columns // PAIR):
            target = (j * count + n) * PAIR
            sums_ref[1:2, target : target + PAIR] = total[0:1, j * PAIR : (j + 1) * PAIR]
    sums = jnp.dot(jnp.ones((8, folded_ref.shape[0]), BF16), folded_ref[...], preferred_element_type=F32)
    sums_ref[0:1, :] = sums[0:1]


def folded(me, order, which, gains, weights):
    rows, columns = weights[0].shape
    total = columns * len(weights)
    spaces = {2 + n: pltpu.HBM for n in range(len(weights))}
    return kernel_call(
        functools.partial(fold_kernel, order, which, len(weights)),
        [((rows, total), BF16), ((2, total), F32)],
        [me, gains, *weights],
        spaces={0: pltpu.SMEM, **spaces},
        scratch=[pltpu.VMEM((rows, columns), BF16)] * len(weights) + [pltpu.SemaphoreType.DMA((len(weights),))],
    )


def stack_kernel(*refs):
    count = (len(refs) - 2) // 2
    sources, out_ref, rows, done = refs[:count], refs[count], refs[count + 1 : -1], refs[-1]
    copies = [pltpu.make_async_copy(sources[i], rows[i], done.at[i]) for i in range(count)]
    for copy in copies:
        copy.start()
    out_ref[...] = jnp.zeros_like(out_ref)
    for i, copy in enumerate(copies):
        copy.wait()
        out_ref[i : i + 1, :] = rows[i][...].astype(F32).reshape(1, out_ref.shape[1])


def reorder_kernel(order, me_ref, source_ref, out_ref, done):
    width = source_ref.shape[1] // len(order)
    copies = []
    for k, r in enumerate(order):
        cols = pl.ds(pl.multiple_of((me_ref[0] ^ r) * width, PAIR), width)
        copies.append(
            pltpu.make_async_copy(source_ref.at[:, cols], out_ref.at[:, k * width : (k + 1) * width], done.at[k])
        )
        copies[-1].start()
    for copy in copies:
        copy.wait()


def half_kernel(part_ref, source_ref, half_ref, done):
    rows = half_ref.shape[0]
    copy = pltpu.make_async_copy(
        source_ref.at[pl.ds(pl.multiple_of(part_ref[0] * rows, rows), rows), :], half_ref, done.at[0]
    )
    copy.start()
    copy.wait()


def row_statistics(refs):
    rows, width = refs[0].shape
    full = width * len(refs)
    means, scales = [], []
    step = math.gcd(rows, 64)
    for start in range(0, rows, step):
        parts = [ref[start : start + step, :].astype(F32) for ref in refs]
        mean = sum(jnp.sum(part, axis=1, keepdims=True) for part in parts) / full
        variance = sum(jnp.sum(jnp.square(part - mean), axis=1, keepdims=True) for part in parts) / full
        means.append(mean)
        scales.append(lax.rsqrt(variance + EPSILON))
    return jnp.concatenate(means, axis=0), jnp.concatenate(scales, axis=0)


def norm_product(cells, mean, scale, folded_ref, sums_ref, start, columns):
    cols = slice(start, start + columns)
    product = jnp.dot(cells, folded_ref[:, cols], preferred_element_type=F32)
    return (product - mean * sums_ref[0:1, cols]) * scale + sums_ref[1:2, cols]


def lane_masks():
    lanes = lax.broadcasted_iota(jnp.int32, (1, PAIR), 1)
    return lanes < HEAD_DIM


def keys_values(projected):
    low = lane_masks()
    values = projected[:, PAIR : 2 * PAIR]
    return (
        projected[:, :PAIR].astype(BF16),
        jnp.where(low, values, 1.0).astype(BF16),
        jnp.where(low, 1.0, values).astype(BF16),
    )


def project_kernel(count, first, *refs):
    blocks, (folded_ref, sums_ref, *refs) = refs[:count], refs[count:]
    key_ref, value_ref = refs[-2:]
    query_ref = refs[-3] if first else None
    mean, scale = row_statistics(blocks)
    cells = jnp.concatenate([ref[...] for ref in blocks], axis=1)
    low = lane_masks()
    for j in range(key_ref.shape[1] // PAIR):
        columns = (3 if first else 2) * PAIR
        projected = norm_product(cells, mean, scale, folded_ref, sums_ref, j * 3 * PAIR, columns)
        base = 2 * j * PAIR
        (
            key_ref[:, j * PAIR : (j + 1) * PAIR],
            value_ref[:, base : base + PAIR],
            value_ref[:, base + PAIR : base + 2 * PAIR],
        ) = keys_values(projected)
        if first:
            queries = projected[:, 2 * PAIR :] * SCORE_SCALE
            query_ref[:, base : base + PAIR] = jnp.where(low, queries, 0.0).astype(BF16)
            query_ref[:, base + PAIR : base + 2 * PAIR] = jnp.where(low, 0.0, queries).astype(BF16)


def chunks_of(spans, rows):
    pieces, local = [], 0
    for start, size in spans:
        step = math.gcd(size, rows)
        for offset in range(0, size, step):
            pieces.append((slice(start + offset, start + offset + step), slice(local, local + step)))
            local += step
    return pieces


def attend_pair(pair, chunks, query_ref, keys, values, state_ref):
    for source, rows in chunks:
        for head in range(2):
            index = 2 * pair + head
            queries = query_ref[source, index * PAIR : (index + 1) * PAIR]
            scores = lax.dot_general(
                queries, keys, (((1,), (1,)), ((), ())), preferred_element_type=F32
            )
            peak = jnp.max(scores, axis=1, keepdims=True)
            soft = jnp.exp2(scores - peak).astype(BF16)
            sums = jnp.dot(soft, values[head], preferred_element_type=F32)
            state_ref[rows, 2 * index * PAIR : (2 * index + 1) * PAIR] = sums
            state_ref[rows, (2 * index + 1) * PAIR : (2 * index + 2) * PAIR] = jnp.broadcast_to(
                peak, (peak.shape[0], PAIR)
            )


def merge_head(old_ref, part_ref, source, rows, index):
    sums = slice(2 * index * PAIR, (2 * index + 1) * PAIR)
    peaks = slice((2 * index + 1) * PAIR, (2 * index + 2) * PAIR)
    old_peak, part_peak = old_ref[source, peaks], part_ref[rows, peaks]
    peak = jnp.maximum(old_peak, part_peak)
    total = old_ref[source, sums] * jnp.exp2(old_peak - peak) + part_ref[rows, sums] * jnp.exp2(part_peak - peak)
    return total, peak


def attend_kernel(first, last, chunks, query_ref, key_ref, value_ref, *refs):
    if last:
        old_ref, attended, part = refs[0], refs[-2], refs[-1]
    elif first:
        part, token_ref = refs[-2:]
    else:
        old_ref, (state_ref, token_ref, part) = refs[0], refs[-3:]
    if not last:
        token_ref[...] = jnp.zeros_like(token_ref)
    pairs = query_ref.shape[1] // (2 * PAIR)
    for j in range(pairs):
        values = [value_ref[:, n * PAIR : (n + 1) * PAIR] for n in (2 * j, 2 * j + 1)]
        attend_pair(j, chunks, query_ref, key_ref[:, j * PAIR : (j + 1) * PAIR], values, part)
    if first:
        return
    low = lane_masks()
    for source, rows in chunks:
        for j in range(pairs):
            heads = [merge_head(old_ref, part, source, rows, 2 * j + head) for head in range(2)]
            if last:
                (one, _), (two, _) = heads
                both = jnp.where(low, one, two)
                weight = pltpu.roll(jnp.where(low, two, one), HEAD_DIM, 1)
                attended[rows, j * PAIR : (j + 1) * PAIR] = (both / weight).astype(BF16)
            else:
                for head, (sums, peak) in enumerate(heads):
                    at = 2 * (2 * j + head) * PAIR
                    state_ref[rows, at : at + PAIR] = sums
                    state_ref[rows, at + PAIR : at + 2 * PAIR] = peak


def middle_kernel(count, order, spans, me_ref, part_ref, *refs):
    attended, frames_refs, refs = refs[:count], refs[count : 2 * count], refs[2 * count :]
    *pieces, folded_ref, sums_ref, own_ref, out_ref, head_ref, tail_ref, middle = refs
    total = out_ref.shape[0]
    width = frames_refs[0].shape[1]
    cells = jnp.concatenate([ref[:, :width] for ref in attended], axis=1)
    swap = part_ref[0] != 0

    def weights(k):
        if width % PAIR:
            cols = slice(k * width, (k + 1) * width)
        else:
            cols = pl.ds(pl.multiple_of((me_ref[0] ^ order[k]) * width, PAIR), width)
        rows, index = [], 0
        while index < len(pieces):
            mine = pieces[index][:, cols]
            index += 1
            if mine.shape[0] < width:
                other = pieces[index][:, cols]
                index += 1
                mine = jnp.concatenate([jnp.where(swap, other, mine), jnp.where(swap, mine, other)], axis=0)
            rows.append(mine)
        return jnp.concatenate(rows, axis=0)

    for k in range(0, count, 2):
        both = jnp.concatenate([weights(k), weights(k + 1)], axis=1)
        share = jnp.dot(cells, both, preferred_element_type=F32)
        for n in range(2):
            cols = slice((k + n) * width, (k + n + 1) * width)
            own = jnp.concatenate([frames_refs[k + n][start : start + size, :] for start, size in spans], axis=0)
            middle[:, cols] = (own.astype(F32) + share[:, n * width : (n + 1) * width]).astype(BF16)
    own_ref[...] = middle[:, :width]
    mean, scale = row_statistics((middle,))
    cells = middle[...]
    for j in range(out_ref.shape[1] // PAIR):
        both = norm_product(cells, mean, scale, folded_ref, sums_ref, j * 2 * PAIR, 2 * PAIR)
        out_ref[:, j * PAIR : (j + 1) * PAIR] = (
            both[:, :PAIR] / (1.0 + jnp.exp(-both[:, PAIR:]))
        ).astype(BF16)
    head_ref[...] = out_ref[:HALO, :]
    tail_ref[...] = out_ref[total - HALO :, :]


def conv_rows(padded, start, piece, cols, taps, scale, shift):
    window = padded[pl.ds(start, piece + 2 * HALO), cols]
    convolved = None
    for residue in range(8):
        part = None
        for offset in range(residue, KERNEL + 1, 8):
            if offset == 0:
                continue
            base = offset - residue
            term = taps[offset - 1] * window[base : base + piece + 8]
            part = term if part is None else part + term
        part = part[residue : residue + piece]
        convolved = part if convolved is None else convolved + part
    value = convolved * scale + shift
    return (value / (1.0 + jnp.exp(-value))).astype(BF16)


def conv_kernel(outer, first_ref, second_ref, *refs):
    if outer:
        left_ref, right_ref, *refs = refs
    taps_ref, bn_ref, w_ref, keep_ref, send_ref, padded, activated = refs
    total, width = first_ref.shape
    half = keep_ref.shape[1]
    piece, quarter = 32, total // 2
    if outer:
        runs = (
            (left_ref[...], first_ref[:quarter, :], second_ref[:HALO, :]),
            (second_ref[total - HALO :, :], first_ref[quarter:, :], right_ref[...]),
        )
    else:
        runs = ((first_ref[quarter - HALO : quarter, :], second_ref[...], first_ref[quarter : quarter + HALO, :]),)
    at = 0
    for before, rows, behind in runs:
        count = rows.shape[0]
        padded[0:HALO, :] = before.astype(F32)
        padded[HALO : HALO + count, :] = rows.astype(F32)
        padded[HALO + count : 2 * HALO + count, :] = behind.astype(F32)
        for col in range(0, width, PAIR):
            cols = slice(col, col + PAIR)
            taps = [taps_ref[j : j + 1, cols] for j in range(KERNEL)]
            scale, shift = bn_ref[0:1, cols], bn_ref[1:2, cols]

            def block(index, carry, at=at):
                start = pl.multiple_of(index * piece, piece)
                target = pl.multiple_of(at + index * piece, piece)
                activated[pl.ds(target, piece), cols] = conv_rows(padded, start, piece, cols, taps, scale, shift)
                return carry

            lax.fori_loop(0, count // piece, block, 0, unroll=4)
        at += count
    share = activated[...]
    send_ref[...] = jnp.dot(share, w_ref[:, half:], preferred_element_type=F32).astype(BF16)
    keep_ref[...] = jnp.dot(share, w_ref[:, :half], preferred_element_type=F32).astype(BF16)


def pad_columns(weight, width):
    if weight.shape[1] == width:
        return weight
    return jnp.pad(weight, ((0, 0), (0, width - weight.shape[1])))


def on_device(
    frames_in,
    norm1_gain,
    norm1_bias,
    w_query,
    w_key,
    w_value,
    w_out,
    norm2_gain,
    norm2_bias,
    w_glu_value,
    w_glu_gate,
    depth_kernel,
    bn_scale,
    bn_shift,
    w_proj,
):
    frames, width = frames_in.shape
    grid, ctx = lax.axis_size("grid"), lax.axis_size("ctx")
    me = lax.axis_index("grid")
    place = me.astype(jnp.int32).reshape(1)
    order = list(range(0, grid, CORES)) + list(range(1, grid, CORES))
    padded = -(-width // PAIR) * PAIR
    query_rows, every = 256, ((0, frames),)

    def by_distance(cells):
        return jnp.concatenate(
            [lax.dynamic_slice_in_dim(cells, (me ^ r) * width, width, 1) for r in order], axis=1
        )

    def over_chips(block):
        return [exchange(block, "grid", CORES * a) for a in range(1, grid // CORES)]

    def other_core(blocks):
        return [exchange(block, "grid", 1) for block in blocks]

    vectors = [norm1_gain, norm1_bias, norm2_gain, norm2_bias]
    (gains,) = kernel_call(
        stack_kernel,
        [((8, width), F32)],
        vectors,
        spaces={i: pltpu.HBM for i in range(len(vectors))},
        scratch=[pltpu.VMEM((width,), BF16)] * len(vectors) + [pltpu.SemaphoreType.DMA((len(vectors),))],
    )
    gains = lax.all_gather(gains, "grid", axis=0, tiled=True)
    raw = {0: frames_in}
    chips = {0: over_chips(frames_in)}
    for k in reversed(range(ctx.bit_length() - 1)):
        raw[1 << k] = exchange(frames_in, "ctx", 1 << k)

    w_query, w_key, w_value, w_glu_value, w_glu_gate = (
        pad_columns(weight, padded) for weight in (w_query, w_key, w_value, w_glu_value, w_glu_gate)
    )
    if width % PAIR:
        row_pad = ((0, padded - width), (0, 0))
        w_p = jnp.pad(by_distance(w_proj), row_pad)
    else:
        (w_p,) = kernel_call(
            functools.partial(reorder_kernel, order),
            [(w_proj.shape, BF16)],
            [place, w_proj],
            spaces={0: pltpu.SMEM, 1: pltpu.HBM},
            scratch=[pltpu.SemaphoreType.DMA((grid,))],
        )
    taps = pad_columns(depth_kernel, padded)
    bn = pad_columns(jnp.stack([bn_scale, bn_shift]), padded)
    qkv, qkv_sums = folded(place, order, 0, gains, (w_key, w_value, w_query))
    chips[0] = [after(block, gains) for block in chips[0]]
    glu, glu_sums = folded(place, order, 2, gains, (w_glu_value, w_glu_gate))

    parts = lax.axis_size("parts")
    part = lax.axis_index("parts").astype(jnp.int32).reshape(1)
    if parts == 2:
        (half,) = kernel_call(
            half_kernel,
            [((width // 2, w_out.shape[1]), BF16)],
            [part, w_out],
            spaces={0: pltpu.SMEM, 1: pltpu.HBM},
            scratch=[pltpu.SemaphoreType.DMA((1,))],
        )
    else:
        half = w_out
    crossed = over_chips(after(half, *chips[0]))
    state_shape = ((frames, 4 * padded), F32)
    token_shape = ((8, 128), F32)
    wide, narrow = ((frames, 2 * padded), BF16), ((frames, padded), BF16)
    chips[1] = [exchange(block, "ctx", 1) for block in chips[0]]
    own = [frames_in] + chips[0]
    own_blocks = own + other_core(own)
    n = len(own_blocks)
    early = [*[raw[s] for s in raw if s], *crossed, *chips[1]]
    queries, keys, values = kernel_call(
        functools.partial(project_kernel, n, True),
        [wide, narrow, wide],
        [*own_blocks, qkv, qkv_sums, *early],
        spaces={n + 2 + i: pl.ANY for i in range(len(early))},
    )
    def prepare(s, done):
        if 2 <= s < ctx:
            low = s & -s
            if s != low:
                raw[s] = after(exchange(raw[s ^ low], "ctx", low), done)
            chips[s] = over_chips(raw[s])

    prepare(2, None)
    state, token = kernel_call(
        functools.partial(attend_kernel, True, False, chunks_of(every, query_rows)),
        [state_shape, token_shape],
        [queries, keys, values],
    )
    crossed = [after(block, token) for block in crossed]
    swapped = [exchange(block, "parts", 1) for block in crossed] if parts == 2 else []
    moved = {1: chips[1]}
    for s in range(1, ctx):
        last = s == ctx - 1
        mine = [raw[s]] + moved[s]
        keys, values = kernel_call(
            functools.partial(project_kernel, n, False),
            [narrow, wide],
            [*mine, *other_core(mine), qkv, qkv_sums],
        )
        if last:
            break
        prepare(s + 2, token)
        moved[s + 1] = [after(block, token) for block in chips[s + 1]]
        behind = [raw[s + 2]] if s + 2 < ctx else []
        behind += moved[s + 1] + ([glu_sums, w_p] if s == 1 else [])
        state, token = kernel_call(
            functools.partial(attend_kernel, False, False, chunks_of(every, query_rows)),
            [state_shape, token_shape],
            [queries, keys, values, state, *behind],
            spaces={4 + i: pl.ANY for i in range(len(behind))},
            aliases={3: 0},
            scratch=[pltpu.VMEM(*state_shape)],
        )
    rows, quarter = frames // 2, frames // 4
    spans = (((0, quarter), (3 * quarter, quarter)), ((quarter, rows),))
    attended = []
    for h in range(2):
        (mine,) = kernel_call(
            functools.partial(attend_kernel, False, True, chunks_of(spans[h], query_rows)),
            [((rows, padded), BF16)],
            [queries, keys, values, state],
            scratch=[pltpu.VMEM((rows, 4 * padded), F32)],
        )
        attended.append([mine] + over_chips(mine))
    swapped = [after(block, attended[0][0]) for block in swapped]
    pieces = [w_out]
    for a, block in enumerate(crossed):
        pieces += [block, swapped[a]] if swapped else [block]
    pieces = pieces + other_core(pieces)
    if width % PAIR:
        pieces = [by_distance(piece) for piece in pieces]
    middle, gated = [], []
    for h in range(2):
        mine = attended[h]
        done = gated[0] if h else attended[1][0]
        mine = mine[:1] + [after(block, done) for block in mine[1:]]
        results = kernel_call(
            functools.partial(middle_kernel, n, order, spans[h]),
            [((rows, width), BF16), ((rows, padded), BF16), ((HALO, padded), BF16), ((HALO, padded), BF16)],
            [place, part, *mine, *other_core(mine), *own_blocks, *pieces, glu, glu_sums],
            spaces={0: pltpu.SMEM, 1: pltpu.SMEM},
            scratch=[pltpu.VMEM((rows, grid * width), BF16)],
        )
        middle.append(results[0])
        gated.append(results[1])
        if h == 0:
            left = lax.ppermute(results[3], "ctx", [(i, i + 1) for i in range(ctx - 1)])
            right = lax.ppermute(results[2], "ctx", [(i + 1, i) for i in range(ctx - 1)])
    outs = [None, None]
    for h, around in ((1, []), (0, [left, right])):
        keep, send = kernel_call(
            functools.partial(conv_kernel, h == 0),
            [((rows, grid // CORES * width), BF16)] * 2,
            [*gated, *around, taps, bn, w_p],
            scratch=[pltpu.VMEM((rows + 2 * HALO, padded), F32), pltpu.VMEM((rows, padded), BF16)],
        )
        theirs = exchange(send, "grid", 1)

        def pair_sum(a):
            cols = slice(a * width, (a + 1) * width)
            return keep[:, cols].astype(F32) + theirs[:, cols].astype(F32)

        result = middle[h].astype(F32) + pair_sum(0)
        for a in range(1, grid // CORES):
            result = result + exchange(pair_sum(a).astype(BF16), "grid", CORES * a).astype(F32)
        outs[h] = result.astype(BF16)
    return jnp.concatenate([outs[0][:quarter], outs[1], outs[0][quarter:]], axis=0)


def solution(mesh):
    return jax.shard_map(
        on_device,
        mesh=mesh,
        in_specs=(
            P(("parts", "ctx"), "grid"),
            P("grid"),
            P("grid"),
            P(None, "grid"),
            P(None, "grid"),
            P(None, "grid"),
            P("grid", None),
            P("grid"),
            P("grid"),
            P(None, "grid"),
            P(None, "grid"),
            P(None, "grid"),
            P("grid"),
            P("grid"),
            P("grid", None),
        ),
        out_specs=P(("parts", "ctx"), "grid"),
        check_vma=False,
    )
```

```python
import functools
import math

import jax
import jax.numpy as jnp
from jax import lax
from jax.experimental import pallas as pl
from jax.experimental.pallas import tpu as pltpu
from jax.sharding import PartitionSpec as P

HEAD_DIM = 64
PAIR = 2 * HEAD_DIM
KERNEL = 31
HALF = 15
HALO = 16
EPSILON = 1e-05
CORES = 2
VMEM_BYTES = 16 * 1024 * 1024
BF16 = jnp.bfloat16
F32 = jnp.float32
SCORE_SCALE = math.log2(math.e) / math.sqrt(HEAD_DIM)


def exchange(cells, axis, distance):
    count = lax.axis_size(axis)
    return lax.ppermute(cells, axis, [(i, i ^ distance) for i in range(count)])


def kernel_call(body, outs, operands, spaces=None, scratch=(), aliases=None):
    spaces = spaces or {}
    operands = [
        pltpu.with_memory_space_constraint(cells, pltpu.HBM) if spaces.get(i) == pltpu.HBM else cells
        for i, cells in enumerate(operands)
    ]
    in_specs = [
        pl.BlockSpec(memory_space=spaces.get(i, pltpu.VMEM)) for i in range(len(operands))
    ]
    return pl.pallas_call(
        body,
        in_specs=in_specs,
        out_specs=tuple(pl.BlockSpec(memory_space=pltpu.VMEM) for _ in outs),
        out_shape=tuple(jax.ShapeDtypeStruct(shape, dtype) for shape, dtype in outs),
        scratch_shapes=list(scratch),
        input_output_aliases=aliases or {},
        compiler_params=pltpu.CompilerParams(vmem_limit_bytes=VMEM_BYTES),
        cost_estimate=pl.CostEstimate(flops=1000, bytes_accessed=1000, transcendentals=0),
    )(*operands)


def after(cells, *done):
    def body(*refs):
        pass

    anywhere = pl.BlockSpec(memory_space=pl.ANY)
    return pl.pallas_call(
        body,
        in_specs=[anywhere] * (1 + len(done)),
        out_specs=anywhere,
        out_shape=jax.ShapeDtypeStruct(cells.shape, cells.dtype),
        input_output_aliases={0: 0},
        compiler_params=pltpu.CompilerParams(vmem_limit_bytes=64 * 1024),
        cost_estimate=pl.CostEstimate(flops=0, bytes_accessed=0, transcendentals=0),
    )(cells, *done)


def fold_kernel(order, which, count, me_ref, gains_ref, *refs):
    sources, (folded_ref, sums_ref), weights, done = refs[:count], refs[count : count + 2], refs[count + 2 : -1], refs[-1]
    copies = [pltpu.make_async_copy(sources[n], weights[n], done.at[n]) for n in range(count)]
    for copy in copies:
        copy.start()
    width = gains_ref.shape[1]
    columns = weights[0].shape[1]
    factors = []
    for r in order:
        gains = gains_ref[pl.ds(pl.multiple_of((me_ref[0] ^ r) * 8, 8), 8), :]
        gain = jnp.transpose(jnp.broadcast_to(gains[which : which + 1, :], (PAIR, width)))
        bias = jnp.broadcast_to(gains[which + 1 : which + 2, :], (8, width)).astype(BF16)
        factors.append((gain, bias))
    for n, ref in enumerate(weights):
        copies[n].wait()
        total = jnp.zeros((8, columns), F32)
        for k, r in enumerate(order):
            gain, bias = factors[k]
            start = pl.multiple_of((me_ref[0] ^ r) * width, width)
            block = ref[pl.ds(start, width), :]
            total = total + jnp.dot(bias, block, preferred_element_type=F32)
            for j in range(columns // PAIR):
                target = (j * count + n) * PAIR
                folded_ref[k * width : (k + 1) * width, target : target + PAIR] = (
                    block[:, j * PAIR : (j + 1) * PAIR].astype(F32) * gain
                ).astype(BF16)
        for j in range(columns // PAIR):
            target = (j * count + n) * PAIR
            sums_ref[1:2, target : target + PAIR] = total[0:1, j * PAIR : (j + 1) * PAIR]
    sums = jnp.dot(jnp.ones((8, folded_ref.shape[0]), BF16), folded_ref[...], preferred_element_type=F32)
    sums_ref[0:1, :] = sums[0:1]


def folded(me, order, which, gains, weights):
    rows, columns = weights[0].shape
    total = columns * len(weights)
    spaces = {2 + n: pltpu.HBM for n in range(len(weights))}
    return kernel_call(
        functools.partial(fold_kernel, order, which, len(weights)),
        [((rows, total), BF16), ((2, total), F32)],
        [me, gains, *weights],
        spaces={0: pltpu.SMEM, **spaces},
        scratch=[pltpu.VMEM((rows, columns), BF16)] * len(weights) + [pltpu.SemaphoreType.DMA((len(weights),))],
    )


def stack_kernel(*refs):
    count = (len(refs) - 2) // 2
    sources, out_ref, rows, done = refs[:count], refs[count], refs[count + 1 : -1], refs[-1]
    copies = [pltpu.make_async_copy(sources[i], rows[i], done.at[i]) for i in range(count)]
    for copy in copies:
        copy.start()
    out_ref[...] = jnp.zeros_like(out_ref)
    for i, copy in enumerate(copies):
        copy.wait()
        out_ref[i : i + 1, :] = rows[i][...].astype(F32).reshape(1, out_ref.shape[1])


def reorder_kernel(order, me_ref, source_ref, out_ref, done):
    width = source_ref.shape[1] // len(order)
    copies = []
    for k, r in enumerate(order):
        cols = pl.ds(pl.multiple_of((me_ref[0] ^ r) * width, PAIR), width)
        copies.append(
            pltpu.make_async_copy(source_ref.at[:, cols], out_ref.at[:, k * width : (k + 1) * width], done.at[k])
        )
        copies[-1].start()
    for copy in copies:
        copy.wait()


def half_kernel(part_ref, source_ref, half_ref, done):
    rows = half_ref.shape[0]
    copy = pltpu.make_async_copy(
        source_ref.at[pl.ds(pl.multiple_of(part_ref[0] * rows, rows), rows), :], half_ref, done.at[0]
    )
    copy.start()
    copy.wait()


def row_statistics(refs):
    rows, width = refs[0].shape
    full = width * len(refs)
    means, scales = [], []
    step = math.gcd(rows, 64)
    for start in range(0, rows, step):
        parts = [ref[start : start + step, :].astype(F32) for ref in refs]
        mean = sum(jnp.sum(part, axis=1, keepdims=True) for part in parts) / full
        variance = sum(jnp.sum(jnp.square(part - mean), axis=1, keepdims=True) for part in parts) / full
        means.append(mean)
        scales.append(lax.rsqrt(variance + EPSILON))
    return jnp.concatenate(means, axis=0), jnp.concatenate(scales, axis=0)


def norm_product(cells, mean, scale, folded_ref, sums_ref, start, columns):
    cols = slice(start, start + columns)
    product = jnp.dot(cells, folded_ref[:, cols], preferred_element_type=F32)
    return (product - mean * sums_ref[0:1, cols]) * scale + sums_ref[1:2, cols]


def lane_masks():
    lanes = lax.broadcasted_iota(jnp.int32, (1, PAIR), 1)
    return lanes < HEAD_DIM


def keys_values(projected):
    low = lane_masks()
    values = projected[:, PAIR : 2 * PAIR]
    return (
        projected[:, :PAIR].astype(BF16),
        jnp.where(low, values, 1.0).astype(BF16),
        jnp.where(low, 1.0, values).astype(BF16),
    )


def project_kernel(count, first, *refs):
    blocks, (folded_ref, sums_ref, *refs) = refs[:count], refs[count:]
    key_ref, value_ref = refs[-2:]
    query_ref = refs[-3] if first else None
    mean, scale = row_statistics(blocks)
    cells = jnp.concatenate([ref[...] for ref in blocks], axis=1)
    low = lane_masks()
    for j in range(key_ref.shape[1] // PAIR):
        columns = (3 if first else 2) * PAIR
        projected = norm_product(cells, mean, scale, folded_ref, sums_ref, j * 3 * PAIR, columns)
        base = 2 * j * PAIR
        (
            key_ref[:, j * PAIR : (j + 1) * PAIR],
            value_ref[:, base : base + PAIR],
            value_ref[:, base + PAIR : base + 2 * PAIR],
        ) = keys_values(projected)
        if first:
            queries = projected[:, 2 * PAIR :] * SCORE_SCALE
            query_ref[:, base : base + PAIR] = jnp.where(low, queries, 0.0).astype(BF16)
            query_ref[:, base + PAIR : base + 2 * PAIR] = jnp.where(low, 0.0, queries).astype(BF16)


def rows_of(ref, spans, cols):
    return jnp.concatenate([ref[start : start + size, cols] for start, size in spans], axis=0)


def attend_pair(pair, spans, query_ref, keys, values, state_ref):
    for head in range(2):
        index = 2 * pair + head
        queries = rows_of(query_ref, spans, slice(index * PAIR, (index + 1) * PAIR))
        scores = lax.dot_general(queries, keys, (((1,), (1,)), ((), ())), preferred_element_type=F32)
        peak = jnp.max(scores, axis=1, keepdims=True)
        soft = jnp.exp2(scores - peak).astype(BF16)
        sums = jnp.dot(soft, values[head], preferred_element_type=F32)
        state_ref[:, 2 * index * PAIR : (2 * index + 1) * PAIR] = sums
        state_ref[:, (2 * index + 1) * PAIR : (2 * index + 2) * PAIR] = jnp.broadcast_to(peak, (peak.shape[0], PAIR))


def merge_head(old_ref, part_ref, spans, index):
    sums = slice(2 * index * PAIR, (2 * index + 1) * PAIR)
    peaks = slice((2 * index + 1) * PAIR, (2 * index + 2) * PAIR)
    old_peak, part_peak = rows_of(old_ref, spans, peaks), part_ref[:, peaks]
    peak = jnp.maximum(old_peak, part_peak)
    total = rows_of(old_ref, spans, sums) * jnp.exp2(old_peak - peak) + part_ref[:, sums] * jnp.exp2(part_peak - peak)
    return total, peak


def attend_kernel(first, last, spans, query_ref, key_ref, value_ref, *refs):
    if last:
        old_ref, attended, part = refs[0], refs[-2], refs[-1]
    elif first:
        part, token_ref = refs[-2:]
    else:
        old_ref, (state_ref, token_ref, part) = refs[0], refs[-3:]
    if not last:
        token_ref[...] = jnp.zeros_like(token_ref)
    pairs = query_ref.shape[1] // (2 * PAIR)
    for j in range(pairs):
        values = [value_ref[:, n * PAIR : (n + 1) * PAIR] for n in (2 * j, 2 * j + 1)]
        attend_pair(j, spans, query_ref, key_ref[:, j * PAIR : (j + 1) * PAIR], values, part)
    if first:
        return
    low = lane_masks()
    for j in range(pairs):
        heads = [merge_head(old_ref, part, spans, 2 * j + head) for head in range(2)]
        if last:
            (one, _), (two, _) = heads
            both = jnp.where(low, one, two)
            weight = pltpu.roll(jnp.where(low, two, one), HEAD_DIM, 1)
            attended[:, j * PAIR : (j + 1) * PAIR] = (both / weight).astype(BF16)
        else:
            for head, (sums, peak) in enumerate(heads):
                at = 2 * (2 * j + head) * PAIR
                state_ref[:, at : at + PAIR] = sums
                state_ref[:, at + PAIR : at + 2 * PAIR] = peak


def middle_kernel(count, order, spans, me_ref, part_ref, *refs):
    attended, frames_refs, refs = refs[:count], refs[count : 2 * count], refs[2 * count :]
    *pieces, folded_ref, sums_ref, own_ref, out_ref, head_ref, tail_ref, middle = refs
    total = out_ref.shape[0]
    width = frames_refs[0].shape[1]
    cells = jnp.concatenate([ref[:, :width] for ref in attended], axis=1)
    swap = part_ref[0] != 0

    def weights(k):
        if width % PAIR:
            cols = slice(k * width, (k + 1) * width)
        else:
            cols = pl.ds(pl.multiple_of((me_ref[0] ^ order[k]) * width, PAIR), width)
        rows, index = [], 0
        while index < len(pieces):
            mine = pieces[index][:, cols]
            index += 1
            if mine.shape[0] < width:
                other = pieces[index][:, cols]
                index += 1
                mine = jnp.concatenate([jnp.where(swap, other, mine), jnp.where(swap, mine, other)], axis=0)
            rows.append(mine)
        return jnp.concatenate(rows, axis=0)

    for k in range(0, count, 2):
        both = jnp.concatenate([weights(k), weights(k + 1)], axis=1)
        share = jnp.dot(cells, both, preferred_element_type=F32)
        for n in range(2):
            cols = slice((k + n) * width, (k + n + 1) * width)
            own = jnp.concatenate([frames_refs[k + n][start : start + size, :] for start, size in spans], axis=0)
            middle[:, cols] = (own.astype(F32) + share[:, n * width : (n + 1) * width]).astype(BF16)
    own_ref[...] = middle[:, :width]
    mean, scale = row_statistics((middle,))
    cells = middle[...]
    for j in range(out_ref.shape[1] // PAIR):
        both = norm_product(cells, mean, scale, folded_ref, sums_ref, j * 2 * PAIR, 2 * PAIR)
        out_ref[:, j * PAIR : (j + 1) * PAIR] = (
            both[:, :PAIR] / (1.0 + jnp.exp(-both[:, PAIR:]))
        ).astype(BF16)
    head_ref[...] = out_ref[:HALO, :]
    tail_ref[...] = out_ref[total - HALO :, :]


def conv_rows(padded, start, piece, cols, taps, scale, shift):
    window = padded[pl.ds(start, piece + 2 * HALO), cols]
    convolved = None
    for residue in range(8):
        part = None
        for offset in range(residue, KERNEL + 1, 8):
            if offset == 0:
                continue
            base = offset - residue
            term = taps[offset - 1] * window[base : base + piece + 8]
            part = term if part is None else part + term
        part = part[residue : residue + piece]
        convolved = part if convolved is None else convolved + part
    value = convolved * scale + shift
    return (value / (1.0 + jnp.exp(-value))).astype(BF16)


def conv_kernel(outer, first_ref, second_ref, *refs):
    if outer:
        left_ref, right_ref, *refs = refs
    taps_ref, bn_ref, w_ref, keep_ref, send_ref, padded, activated = refs
    total, width = first_ref.shape
    half = keep_ref.shape[1]
    piece, quarter = 32, total // 2
    if outer:
        runs = (
            (left_ref[...], first_ref[:quarter, :], second_ref[:HALO, :]),
            (second_ref[total - HALO :, :], first_ref[quarter:, :], right_ref[...]),
        )
    else:
        runs = ((first_ref[quarter - HALO : quarter, :], second_ref[...], first_ref[quarter : quarter + HALO, :]),)
    at = 0
    for before, rows, behind in runs:
        count = rows.shape[0]
        padded[0:HALO, :] = before.astype(F32)
        padded[HALO : HALO + count, :] = rows.astype(F32)
        padded[HALO + count : 2 * HALO + count, :] = behind.astype(F32)
        for col in range(0, width, PAIR):
            cols = slice(col, col + PAIR)
            taps = [taps_ref[j : j + 1, cols] for j in range(KERNEL)]
            scale, shift = bn_ref[0:1, cols], bn_ref[1:2, cols]

            def block(index, carry, at=at):
                start = pl.multiple_of(index * piece, piece)
                target = pl.multiple_of(at + index * piece, piece)
                activated[pl.ds(target, piece), cols] = conv_rows(padded, start, piece, cols, taps, scale, shift)
                return carry

            lax.fori_loop(0, count // piece, block, 0, unroll=4)
        at += count
    share = activated[...]
    send_ref[...] = jnp.dot(share, w_ref[:, half:], preferred_element_type=F32).astype(BF16)
    keep_ref[...] = jnp.dot(share, w_ref[:, :half], preferred_element_type=F32).astype(BF16)


def pad_columns(weight, width):
    if weight.shape[1] == width:
        return weight
    return jnp.pad(weight, ((0, 0), (0, width - weight.shape[1])))


def on_device(
    frames_in,
    norm1_gain,
    norm1_bias,
    w_query,
    w_key,
    w_value,
    w_out,
    norm2_gain,
    norm2_bias,
    w_glu_value,
    w_glu_gate,
    depth_kernel,
    bn_scale,
    bn_shift,
    w_proj,
):
    frames, width = frames_in.shape
    grid, ctx = lax.axis_size("grid"), lax.axis_size("ctx")
    me = lax.axis_index("grid")
    place = me.astype(jnp.int32).reshape(1)
    order = list(range(0, grid, CORES)) + list(range(1, grid, CORES))
    padded = -(-width // PAIR) * PAIR
    every = ((0, frames),)

    def by_distance(cells):
        return jnp.concatenate(
            [lax.dynamic_slice_in_dim(cells, (me ^ r) * width, width, 1) for r in order], axis=1
        )

    def over_chips(block):
        return [exchange(block, "grid", CORES * a) for a in range(1, grid // CORES)]

    def other_core(blocks):
        return [exchange(block, "grid", 1) for block in blocks]

    vectors = [norm1_gain, norm1_bias, norm2_gain, norm2_bias]
    (gains,) = kernel_call(
        stack_kernel,
        [((8, width), F32)],
        vectors,
        spaces={i: pltpu.HBM for i in range(len(vectors))},
        scratch=[pltpu.VMEM((width,), BF16)] * len(vectors) + [pltpu.SemaphoreType.DMA((len(vectors),))],
    )
    gains = lax.all_gather(gains, "grid", axis=0, tiled=True)
    raw = {0: frames_in}
    chips = {0: over_chips(frames_in)}
    for k in reversed(range(ctx.bit_length() - 1)):
        raw[1 << k] = exchange(frames_in, "ctx", 1 << k)

    w_query, w_key, w_value, w_glu_value, w_glu_gate = (
        pad_columns(weight, padded) for weight in (w_query, w_key, w_value, w_glu_value, w_glu_gate)
    )
    if width % PAIR:
        row_pad = ((0, padded - width), (0, 0))
        w_p = jnp.pad(by_distance(w_proj), row_pad)
    else:
        (w_p,) = kernel_call(
            functools.partial(reorder_kernel, order),
            [(w_proj.shape, BF16)],
            [place, w_proj],
            spaces={0: pltpu.SMEM, 1: pltpu.HBM},
            scratch=[pltpu.SemaphoreType.DMA((grid,))],
        )
    taps = pad_columns(depth_kernel, padded)
    bn = pad_columns(jnp.stack([bn_scale, bn_shift]), padded)
    qkv, qkv_sums = folded(place, order, 0, gains, (w_key, w_value, w_query))
    chips[0] = [after(block, qkv_sums) for block in chips[0]]
    glu, glu_sums = folded(place, order, 2, gains, (w_glu_value, w_glu_gate))

    parts = lax.axis_size("parts")
    part = lax.axis_index("parts").astype(jnp.int32).reshape(1)
    if parts == 2:
        (half,) = kernel_call(
            half_kernel,
            [((width // 2, w_out.shape[1]), BF16)],
            [part, w_out],
            spaces={0: pltpu.SMEM, 1: pltpu.HBM},
            scratch=[pltpu.SemaphoreType.DMA((1,))],
        )
    else:
        half = w_out
    crossed = over_chips(after(half, *chips[0]))
    state_shape = ((frames, 4 * padded), F32)
    token_shape = ((8, 128), F32)
    wide, narrow = ((frames, 2 * padded), BF16), ((frames, padded), BF16)
    chips[1] = [exchange(block, "ctx", 1) for block in chips[0]]
    own = [frames_in] + chips[0]
    own_blocks = own + other_core(own)
    n = len(own_blocks)
    early = [*[raw[s] for s in raw if s], glu_sums, w_p]
    queries, keys, values = kernel_call(
        functools.partial(project_kernel, n, True),
        [wide, narrow, wide],
        [*own_blocks, qkv, qkv_sums, *early],
        spaces={n + 2 + i: pl.ANY for i in range(len(early))},
    )
    def prepare(s, done):
        if 2 <= s < ctx:
            low = s & -s
            if s != low:
                raw[s] = after(exchange(raw[s ^ low], "ctx", low), done)
            chips[s] = over_chips(raw[s])

    prepare(2, None)
    state, token = kernel_call(
        functools.partial(attend_kernel, True, False, every),
        [state_shape, token_shape],
        [queries, keys, values, *crossed],
        spaces={3 + i: pl.ANY for i in range(len(crossed))},
    )
    crossed = [after(block, token) for block in crossed]
    swapped = [exchange(block, "parts", 1) for block in crossed] if parts == 2 else []
    moved = {1: [after(block, token) for block in chips[1]]}
    for s in range(1, ctx):
        last = s == ctx - 1
        mine = [raw[s]] + moved[s]
        keys, values = kernel_call(
            functools.partial(project_kernel, n, False),
            [narrow, wide],
            [*mine, *other_core(mine), qkv, qkv_sums],
        )
        if last:
            break
        prepare(s + 2, token)
        moved[s + 1] = [after(block, token) for block in chips[s + 1]]
        behind = [raw[s + 2]] if s + 2 < ctx else []
        behind += moved[s + 1]
        state, token = kernel_call(
            functools.partial(attend_kernel, False, False, every),
            [state_shape, token_shape],
            [queries, keys, values, state, *behind],
            spaces={4 + i: pl.ANY for i in range(len(behind))},
            aliases={3: 0},
            scratch=[pltpu.VMEM(*state_shape)],
        )
    rows, quarter = frames // 2, frames // 4
    spans = (((0, quarter), (3 * quarter, quarter)), ((quarter, rows),))
    attended = []
    for h in range(2):
        (mine,) = kernel_call(
            functools.partial(attend_kernel, False, True, spans[h]),
            [((rows, padded), BF16)],
            [queries, keys, values, state],
            scratch=[pltpu.VMEM((rows, 4 * padded), F32)],
        )
        attended.append([mine] + over_chips(mine))
    swapped = [after(block, attended[0][0]) for block in swapped]
    pieces = [w_out]
    for a, block in enumerate(crossed):
        pieces += [block, swapped[a]] if swapped else [block]
    pieces = pieces + other_core(pieces)
    if width % PAIR:
        pieces = [by_distance(piece) for piece in pieces]
    middle, gated = [], []
    for h in range(2):
        mine = attended[h]
        done = gated[0] if h else attended[1][0]
        mine = mine[:1] + [after(block, done) for block in mine[1:]]
        results = kernel_call(
            functools.partial(middle_kernel, n, order, spans[h]),
            [((rows, width), BF16), ((rows, padded), BF16), ((HALO, padded), BF16), ((HALO, padded), BF16)],
            [place, part, *mine, *other_core(mine), *own_blocks, *pieces, glu, glu_sums],
            spaces={0: pltpu.SMEM, 1: pltpu.SMEM},
            scratch=[pltpu.VMEM((rows, grid * width), BF16)],
        )
        middle.append(results[0])
        gated.append(results[1])
        if h == 0:
            left = lax.ppermute(results[3], "ctx", [(i, i + 1) for i in range(ctx - 1)])
            right = lax.ppermute(results[2], "ctx", [(i + 1, i) for i in range(ctx - 1)])
    outs = [None, None]
    for h, around in ((1, []), (0, [left, right])):
        keep, send = kernel_call(
            functools.partial(conv_kernel, h == 0),
            [((rows, grid // CORES * width), BF16)] * 2,
            [*gated, *around, taps, bn, w_p],
            scratch=[pltpu.VMEM((rows + 2 * HALO, padded), F32), pltpu.VMEM((rows, padded), BF16)],
        )
        theirs = exchange(send, "grid", 1)

        def pair_sum(a):
            cols = slice(a * width, (a + 1) * width)
            return keep[:, cols].astype(F32) + theirs[:, cols].astype(F32)

        result = middle[h].astype(F32) + pair_sum(0)
        for a in range(1, grid // CORES):
            result = result + exchange(pair_sum(a).astype(BF16), "grid", CORES * a).astype(F32)
        outs[h] = result.astype(BF16)
    return jnp.concatenate([outs[0][:quarter], outs[1], outs[0][quarter:]], axis=0)


def solution(mesh):
    return jax.shard_map(
        on_device,
        mesh=mesh,
        in_specs=(
            P(("parts", "ctx"), "grid"),
            P("grid"),
            P("grid"),
            P(None, "grid"),
            P(None, "grid"),
            P(None, "grid"),
            P("grid", None),
            P("grid"),
            P("grid"),
            P(None, "grid"),
            P(None, "grid"),
            P(None, "grid"),
            P("grid"),
            P("grid"),
            P("grid", None),
        ),
        out_specs=P(("parts", "ctx"), "grid"),
        check_vma=False,
    )
```

```python
import functools
import math

import jax
import jax.numpy as jnp
from jax import lax
from jax.experimental import pallas as pl
from jax.experimental.pallas import tpu as pltpu
from jax.sharding import PartitionSpec as P

HEAD_DIM = 64
PAIR = 2 * HEAD_DIM
KERNEL = 31
HALF = 15
HALO = 16
EPSILON = 1e-05
CORES = 2
VMEM_BYTES = 16 * 1024 * 1024
BF16 = jnp.bfloat16
F32 = jnp.float32
SCORE_SCALE = math.log2(math.e) / math.sqrt(HEAD_DIM)


def exchange(cells, axis, distance):
    count = lax.axis_size(axis)
    return lax.ppermute(cells, axis, [(i, i ^ distance) for i in range(count)])


def kernel_call(body, outs, operands, spaces=None, scratch=(), aliases=None):
    spaces = spaces or {}
    operands = [
        pltpu.with_memory_space_constraint(cells, pltpu.HBM) if spaces.get(i) == pltpu.HBM else cells
        for i, cells in enumerate(operands)
    ]
    in_specs = [
        pl.BlockSpec(memory_space=spaces.get(i, pltpu.VMEM)) for i in range(len(operands))
    ]
    return pl.pallas_call(
        body,
        in_specs=in_specs,
        out_specs=tuple(pl.BlockSpec(memory_space=pltpu.VMEM) for _ in outs),
        out_shape=tuple(jax.ShapeDtypeStruct(shape, dtype) for shape, dtype in outs),
        scratch_shapes=list(scratch),
        input_output_aliases=aliases or {},
        compiler_params=pltpu.CompilerParams(vmem_limit_bytes=VMEM_BYTES),
        cost_estimate=pl.CostEstimate(flops=1000, bytes_accessed=1000, transcendentals=0),
    )(*operands)


def after(cells, *done):
    def body(*refs):
        pass

    anywhere = pl.BlockSpec(memory_space=pl.ANY)
    return pl.pallas_call(
        body,
        in_specs=[anywhere] * (1 + len(done)),
        out_specs=anywhere,
        out_shape=jax.ShapeDtypeStruct(cells.shape, cells.dtype),
        input_output_aliases={0: 0},
        compiler_params=pltpu.CompilerParams(vmem_limit_bytes=64 * 1024),
        cost_estimate=pl.CostEstimate(flops=0, bytes_accessed=0, transcendentals=0),
    )(cells, *done)


def fold_kernel(order, which, count, me_ref, gains_ref, *refs):
    sources, (folded_ref, sums_ref), weights, done = refs[:count], refs[count : count + 2], refs[count + 2 : -1], refs[-1]
    copies = [pltpu.make_async_copy(sources[n], weights[n], done.at[n]) for n in range(count)]
    for copy in copies:
        copy.start()
    width = gains_ref.shape[1]
    columns = weights[0].shape[1]
    factors = []
    for r in order:
        gains = gains_ref[pl.ds(pl.multiple_of((me_ref[0] ^ r) * 8, 8), 8), :]
        gain = jnp.transpose(jnp.broadcast_to(gains[which : which + 1, :], (PAIR, width)))
        bias = jnp.broadcast_to(gains[which + 1 : which + 2, :], (8, width)).astype(BF16)
        factors.append((gain, bias))
    for n, ref in enumerate(weights):
        copies[n].wait()
        total = jnp.zeros((8, columns), F32)
        for k, r in enumerate(order):
            gain, bias = factors[k]
            start = pl.multiple_of((me_ref[0] ^ r) * width, width)
            block = ref[pl.ds(start, width), :]
            total = total + jnp.dot(bias, block, preferred_element_type=F32)
            for j in range(columns // PAIR):
                target = (j * count + n) * PAIR
                folded_ref[k * width : (k + 1) * width, target : target + PAIR] = (
                    block[:, j * PAIR : (j + 1) * PAIR].astype(F32) * gain
                ).astype(BF16)
        for j in range(columns // PAIR):
            target = (j * count + n) * PAIR
            sums_ref[1:2, target : target + PAIR] = total[0:1, j * PAIR : (j + 1) * PAIR]
    sums = jnp.dot(jnp.ones((8, folded_ref.shape[0]), BF16), folded_ref[...], preferred_element_type=F32)
    sums_ref[0:1, :] = sums[0:1]


def folded(me, order, which, gains, weights):
    rows, columns = weights[0].shape
    total = columns * len(weights)
    spaces = {2 + n: pltpu.HBM for n in range(len(weights))}
    return kernel_call(
        functools.partial(fold_kernel, order, which, len(weights)),
        [((rows, total), BF16), ((2, total), F32)],
        [me, gains, *weights],
        spaces={0: pltpu.SMEM, **spaces},
        scratch=[pltpu.VMEM((rows, columns), BF16)] * len(weights) + [pltpu.SemaphoreType.DMA((len(weights),))],
    )


def stack_kernel(*refs):
    count = (len(refs) - 2) // 2
    sources, out_ref, rows, done = refs[:count], refs[count], refs[count + 1 : -1], refs[-1]
    copies = [pltpu.make_async_copy(sources[i], rows[i], done.at[i]) for i in range(count)]
    for copy in copies:
        copy.start()
    out_ref[...] = jnp.zeros_like(out_ref)
    for i, copy in enumerate(copies):
        copy.wait()
        out_ref[i : i + 1, :] = rows[i][...].astype(F32).reshape(1, out_ref.shape[1])


def reorder_kernel(order, me_ref, source_ref, out_ref, done):
    width = source_ref.shape[1] // len(order)
    copies = []
    for k, r in enumerate(order):
        cols = pl.ds(pl.multiple_of((me_ref[0] ^ r) * width, PAIR), width)
        copies.append(
            pltpu.make_async_copy(source_ref.at[:, cols], out_ref.at[:, k * width : (k + 1) * width], done.at[k])
        )
        copies[-1].start()
    for copy in copies:
        copy.wait()


def half_kernel(part_ref, source_ref, half_ref, done):
    rows = half_ref.shape[0]
    copy = pltpu.make_async_copy(
        source_ref.at[pl.ds(pl.multiple_of(part_ref[0] * rows, rows), rows), :], half_ref, done.at[0]
    )
    copy.start()
    copy.wait()


def row_statistics(refs):
    rows, width = refs[0].shape
    full = width * len(refs)
    means, scales = [], []
    step = math.gcd(rows, 64)
    for start in range(0, rows, step):
        parts = [ref[start : start + step, :].astype(F32) for ref in refs]
        mean = sum(jnp.sum(part, axis=1, keepdims=True) for part in parts) / full
        variance = sum(jnp.sum(jnp.square(part - mean), axis=1, keepdims=True) for part in parts) / full
        means.append(mean)
        scales.append(lax.rsqrt(variance + EPSILON))
    return jnp.concatenate(means, axis=0), jnp.concatenate(scales, axis=0)


def norm_product(cells, mean, scale, folded_ref, sums_ref, start, columns):
    cols = slice(start, start + columns)
    product = jnp.dot(cells, folded_ref[:, cols], preferred_element_type=F32)
    return (product - mean * sums_ref[0:1, cols]) * scale + sums_ref[1:2, cols]


def lane_masks():
    lanes = lax.broadcasted_iota(jnp.int32, (1, PAIR), 1)
    return lanes < HEAD_DIM


def keys_values(projected):
    low = lane_masks()
    values = projected[:, PAIR : 2 * PAIR]
    return (
        projected[:, :PAIR].astype(BF16),
        jnp.where(low, values, 1.0).astype(BF16),
        jnp.where(low, 1.0, values).astype(BF16),
    )


def project_kernel(count, first, *refs):
    blocks, (folded_ref, sums_ref, *refs) = refs[:count], refs[count:]
    key_ref, value_ref = refs[-2:]
    query_ref = refs[-3] if first else None
    mean, scale = row_statistics(blocks)
    cells = jnp.concatenate([ref[...] for ref in blocks], axis=1)
    low = lane_masks()
    for j in range(key_ref.shape[1] // PAIR):
        columns = (3 if first else 2) * PAIR
        projected = norm_product(cells, mean, scale, folded_ref, sums_ref, j * 3 * PAIR, columns)
        base = 2 * j * PAIR
        (
            key_ref[:, j * PAIR : (j + 1) * PAIR],
            value_ref[:, base : base + PAIR],
            value_ref[:, base + PAIR : base + 2 * PAIR],
        ) = keys_values(projected)
        if first:
            queries = projected[:, 2 * PAIR :] * SCORE_SCALE
            query_ref[:, base : base + PAIR] = jnp.where(low, queries, 0.0).astype(BF16)
            query_ref[:, base + PAIR : base + 2 * PAIR] = jnp.where(low, 0.0, queries).astype(BF16)


def rows_of(ref, spans, cols):
    return jnp.concatenate([ref[start : start + size, cols] for start, size in spans], axis=0)


def attend_pair(pair, spans, query_ref, keys, values, state_ref):
    for head in range(2):
        index = 2 * pair + head
        queries = rows_of(query_ref, spans, slice(index * PAIR, (index + 1) * PAIR))
        scores = lax.dot_general(queries, keys, (((1,), (1,)), ((), ())), preferred_element_type=F32)
        peak = jnp.max(scores, axis=1, keepdims=True)
        soft = jnp.exp2(scores - peak).astype(BF16)
        sums = jnp.dot(soft, values[head], preferred_element_type=F32)
        state_ref[:, 2 * index * PAIR : (2 * index + 1) * PAIR] = sums
        state_ref[:, (2 * index + 1) * PAIR : (2 * index + 2) * PAIR] = jnp.broadcast_to(peak, (peak.shape[0], PAIR))


def merge_head(old_ref, part_ref, spans, index):
    sums = slice(2 * index * PAIR, (2 * index + 1) * PAIR)
    peaks = slice((2 * index + 1) * PAIR, (2 * index + 2) * PAIR)
    old_peak, part_peak = rows_of(old_ref, spans, peaks), part_ref[:, peaks]
    peak = jnp.maximum(old_peak, part_peak)
    total = rows_of(old_ref, spans, sums) * jnp.exp2(old_peak - peak) + part_ref[:, sums] * jnp.exp2(part_peak - peak)
    return total, peak


def attend_kernel(first, last, spans, query_ref, key_ref, value_ref, *refs):
    if last:
        old_ref, attended, part = refs[0], refs[-2], refs[-1]
    elif first:
        part, token_ref = refs[-2:]
    else:
        old_ref, (state_ref, token_ref, part) = refs[0], refs[-3:]
    if not last:
        token_ref[...] = jnp.zeros_like(token_ref)
    pairs = query_ref.shape[1] // (2 * PAIR)
    for j in range(pairs):
        values = [value_ref[:, n * PAIR : (n + 1) * PAIR] for n in (2 * j, 2 * j + 1)]
        attend_pair(j, spans, query_ref, key_ref[:, j * PAIR : (j + 1) * PAIR], values, part)
    if first:
        return
    low = lane_masks()
    for j in range(pairs):
        heads = [merge_head(old_ref, part, spans, 2 * j + head) for head in range(2)]
        if last:
            (one, _), (two, _) = heads
            both = jnp.where(low, one, two)
            weight = pltpu.roll(jnp.where(low, two, one), HEAD_DIM, 1)
            attended[:, j * PAIR : (j + 1) * PAIR] = (both / weight).astype(BF16)
        else:
            for head, (sums, peak) in enumerate(heads):
                at = 2 * (2 * j + head) * PAIR
                state_ref[:, at : at + PAIR] = sums
                state_ref[:, at + PAIR : at + 2 * PAIR] = peak


def middle_kernel(count, order, spans, me_ref, part_ref, *refs):
    attended, frames_refs, refs = refs[:count], refs[count : 2 * count], refs[2 * count :]
    *pieces, folded_ref, sums_ref, _, own_ref, out_ref, head_ref, tail_ref, middle = refs
    total = out_ref.shape[0]
    width = frames_refs[0].shape[1]
    cells = jnp.concatenate([ref[:, :width] for ref in attended], axis=1)
    swap = part_ref[0] != 0

    def weights(k):
        if width % PAIR:
            cols = slice(k * width, (k + 1) * width)
        else:
            cols = pl.ds(pl.multiple_of((me_ref[0] ^ order[k]) * width, PAIR), width)
        rows, index = [], 0
        while index < len(pieces):
            mine = pieces[index][:, cols]
            index += 1
            if mine.shape[0] < width:
                other = pieces[index][:, cols]
                index += 1
                mine = jnp.concatenate([jnp.where(swap, other, mine), jnp.where(swap, mine, other)], axis=0)
            rows.append(mine)
        return jnp.concatenate(rows, axis=0)

    for k in range(0, count, 2):
        both = jnp.concatenate([weights(k), weights(k + 1)], axis=1)
        share = jnp.dot(cells, both, preferred_element_type=F32)
        for n in range(2):
            cols = slice((k + n) * width, (k + n + 1) * width)
            own = jnp.concatenate([frames_refs[k + n][start : start + size, :] for start, size in spans], axis=0)
            middle[:, cols] = (own.astype(F32) + share[:, n * width : (n + 1) * width]).astype(BF16)
    own_ref[...] = middle[:, :width]
    mean, scale = row_statistics((middle,))
    cells = middle[...]
    for j in range(out_ref.shape[1] // PAIR):
        both = norm_product(cells, mean, scale, folded_ref, sums_ref, j * 2 * PAIR, 2 * PAIR)
        out_ref[:, j * PAIR : (j + 1) * PAIR] = (
            both[:, :PAIR] / (1.0 + jnp.exp(-both[:, PAIR:]))
        ).astype(BF16)
    head_ref[...] = out_ref[:HALO, :]
    tail_ref[...] = out_ref[total - HALO :, :]


def conv_rows(padded, start, piece, cols, taps, scale, shift):
    window = padded[pl.ds(start, piece + 2 * HALO), cols]
    convolved = None
    for residue in range(8):
        part = None
        for offset in range(residue, KERNEL + 1, 8):
            if offset == 0:
                continue
            base = offset - residue
            term = taps[offset - 1] * window[base : base + piece + 8]
            part = term if part is None else part + term
        part = part[residue : residue + piece]
        convolved = part if convolved is None else convolved + part
    value = convolved * scale + shift
    return (value / (1.0 + jnp.exp(-value))).astype(BF16)


def conv_kernel(outer, first_ref, second_ref, *refs):
    left_ref, right_ref, *refs = refs
    taps_ref, bn_ref, w_ref, keep_ref, send_ref, padded, activated = refs
    total, width = first_ref.shape
    half = keep_ref.shape[1]
    piece, quarter = 32, total // 2
    if outer:
        runs = (
            (left_ref[...], first_ref[:quarter, :], second_ref[:HALO, :]),
            (second_ref[total - HALO :, :], first_ref[quarter:, :], right_ref[...]),
        )
    else:
        runs = ((first_ref[quarter - HALO : quarter, :], second_ref[...], first_ref[quarter : quarter + HALO, :]),)
    at = 0
    for before, rows, behind in runs:
        count = rows.shape[0]
        padded[0:HALO, :] = before.astype(F32)
        padded[HALO : HALO + count, :] = rows.astype(F32)
        padded[HALO + count : 2 * HALO + count, :] = behind.astype(F32)
        for col in range(0, width, PAIR):
            cols = slice(col, col + PAIR)
            taps = [taps_ref[j : j + 1, cols] for j in range(KERNEL)]
            scale, shift = bn_ref[0:1, cols], bn_ref[1:2, cols]

            def block(index, carry, at=at):
                start = pl.multiple_of(index * piece, piece)
                target = pl.multiple_of(at + index * piece, piece)
                activated[pl.ds(target, piece), cols] = conv_rows(padded, start, piece, cols, taps, scale, shift)
                return carry

            lax.fori_loop(0, count // piece, block, 0, unroll=4)
        at += count
    share = activated[...]
    send_ref[...] = jnp.dot(share, w_ref[:, half:], preferred_element_type=F32).astype(BF16)
    keep_ref[...] = jnp.dot(share, w_ref[:, :half], preferred_element_type=F32).astype(BF16)


def pad_columns(weight, width):
    if weight.shape[1] == width:
        return weight
    return jnp.pad(weight, ((0, 0), (0, width - weight.shape[1])))


def on_device(
    frames_in,
    norm1_gain,
    norm1_bias,
    w_query,
    w_key,
    w_value,
    w_out,
    norm2_gain,
    norm2_bias,
    w_glu_value,
    w_glu_gate,
    depth_kernel,
    bn_scale,
    bn_shift,
    w_proj,
):
    frames, width = frames_in.shape
    grid, ctx = lax.axis_size("grid"), lax.axis_size("ctx")
    me = lax.axis_index("grid")
    place = me.astype(jnp.int32).reshape(1)
    order = list(range(0, grid, CORES)) + list(range(1, grid, CORES))
    padded = -(-width // PAIR) * PAIR
    every = ((0, frames),)

    def by_distance(cells):
        return jnp.concatenate(
            [lax.dynamic_slice_in_dim(cells, (me ^ r) * width, width, 1) for r in order], axis=1
        )

    def over_chips(block):
        return [exchange(block, "grid", CORES * a) for a in range(1, grid // CORES)]

    def other_core(blocks):
        return [exchange(block, "grid", 1) for block in blocks]

    vectors = [norm1_gain, norm1_bias, norm2_gain, norm2_bias]
    (gains,) = kernel_call(
        stack_kernel,
        [((8, width), F32)],
        vectors,
        spaces={i: pltpu.HBM for i in range(len(vectors))},
        scratch=[pltpu.VMEM((width,), BF16)] * len(vectors) + [pltpu.SemaphoreType.DMA((len(vectors),))],
    )
    gains = lax.all_gather(gains, "grid", axis=0, tiled=True)
    raw = {0: frames_in}
    chips = {0: over_chips(frames_in)}
    for k in reversed(range(ctx.bit_length() - 1)):
        raw[1 << k] = exchange(frames_in, "ctx", 1 << k)

    w_query, w_key, w_value, w_glu_value, w_glu_gate = (
        pad_columns(weight, padded) for weight in (w_query, w_key, w_value, w_glu_value, w_glu_gate)
    )
    if width % PAIR:
        row_pad = ((0, padded - width), (0, 0))
        w_p = jnp.pad(by_distance(w_proj), row_pad)
    else:
        (w_p,) = kernel_call(
            functools.partial(reorder_kernel, order),
            [(w_proj.shape, BF16)],
            [place, w_proj],
            spaces={0: pltpu.SMEM, 1: pltpu.HBM},
            scratch=[pltpu.SemaphoreType.DMA((grid,))],
        )
    taps = pad_columns(depth_kernel, padded)
    bn = pad_columns(jnp.stack([bn_scale, bn_shift]), padded)
    qkv, qkv_sums = folded(place, order, 0, gains, (w_key, w_value, w_query))
    chips[0] = [after(block, qkv_sums) for block in chips[0]]
    glu, glu_sums = folded(place, order, 2, gains, (w_glu_value, w_glu_gate))

    parts = lax.axis_size("parts")
    part = lax.axis_index("parts").astype(jnp.int32).reshape(1)
    if parts == 2:
        (half,) = kernel_call(
            half_kernel,
            [((width // 2, w_out.shape[1]), BF16)],
            [part, w_out],
            spaces={0: pltpu.SMEM, 1: pltpu.HBM},
            scratch=[pltpu.SemaphoreType.DMA((1,))],
        )
    else:
        half = w_out
    crossed = over_chips(after(half, *chips[0]))
    state_shape = ((frames, 4 * padded), F32)
    token_shape = ((8, 128), F32)
    wide, narrow = ((frames, 2 * padded), BF16), ((frames, padded), BF16)
    chips[1] = [exchange(block, "ctx", 1) for block in chips[0]]
    own = [frames_in] + chips[0]
    own_blocks = own + other_core(own)
    n = len(own_blocks)
    early = [*[raw[s] for s in raw if s], glu_sums, w_p]
    queries, keys, values = kernel_call(
        functools.partial(project_kernel, n, True),
        [wide, narrow, wide],
        [*own_blocks, qkv, qkv_sums, *early],
        spaces={n + 2 + i: pl.ANY for i in range(len(early))},
    )
    def prepare(s, done):
        if 2 <= s < ctx:
            low = s & -s
            if s != low:
                raw[s] = after(exchange(raw[s ^ low], "ctx", low), done)
            chips[s] = over_chips(raw[s])

    prepare(2, None)
    state, token = kernel_call(
        functools.partial(attend_kernel, True, False, every),
        [state_shape, token_shape],
        [queries, keys, values, *crossed],
        spaces={3 + i: pl.ANY for i in range(len(crossed))},
    )
    crossed = [after(block, token) for block in crossed]
    swapped = [exchange(block, "parts", 1) for block in crossed] if parts == 2 else []
    moved = {1: [after(block, token) for block in chips[1]]}
    for s in range(1, ctx):
        last = s == ctx - 1
        mine = [raw[s]] + moved[s]
        keys, values = kernel_call(
            functools.partial(project_kernel, n, False),
            [narrow, wide],
            [*mine, *other_core(mine), qkv, qkv_sums],
        )
        if last:
            break
        prepare(s + 2, token)
        moved[s + 1] = [after(block, keys if s > 1 else token) for block in chips[s + 1]]
        behind = [raw[s + 2]] if s + 2 < ctx else []
        behind += moved[s + 1]
        state, token = kernel_call(
            functools.partial(attend_kernel, False, False, every),
            [state_shape, token_shape],
            [queries, keys, values, state, *behind],
            spaces={4 + i: pl.ANY for i in range(len(behind))},
            aliases={3: 0},
            scratch=[pltpu.VMEM(*state_shape)],
        )
    rows, quarter = frames // 2, frames // 4
    spans = (((0, quarter), (3 * quarter, quarter)), ((quarter, rows),))
    attended = []
    for h in range(2):
        (mine,) = kernel_call(
            functools.partial(attend_kernel, False, True, spans[h]),
            [((rows, padded), BF16)],
            [queries, keys, values, state],
            scratch=[pltpu.VMEM((rows, 4 * padded), F32)],
        )
        attended.append([mine] + over_chips(mine))
    swapped = [after(block, attended[0][0]) for block in swapped]
    pieces = [w_out]
    for a, block in enumerate(crossed):
        pieces += [block, swapped[a]] if swapped else [block]
    pieces = pieces + other_core(pieces)
    if width % PAIR:
        pieces = [by_distance(piece) for piece in pieces]
    middle, gated = [], []
    for h in range(2):
        mine = attended[h]
        mine = mine[:1] + [after(block, attended[1][0]) for block in mine[1:]]
        results = kernel_call(
            functools.partial(middle_kernel, n, order, spans[h]),
            [((rows, width), BF16), ((rows, padded), BF16), ((HALO, padded), BF16), ((HALO, padded), BF16)],
            [place, part, *mine, *other_core(mine), *own_blocks, *pieces, glu, glu_sums, gated[0] if h else place],
            spaces={0: pltpu.SMEM, 1: pltpu.SMEM, 2 + 2 * n + len(pieces) + 2: pl.ANY},
            scratch=[pltpu.VMEM((rows, grid * width), BF16)],
        )
        middle.append(results[0])
        gated.append(results[1])
        if h == 0:
            left = lax.ppermute(results[3], "ctx", [(i, i + 1) for i in range(ctx - 1)])
            right = lax.ppermute(results[2], "ctx", [(i + 1, i) for i in range(ctx - 1)])
    outs = [None, None]
    for h in (1, 0):
        keep, send = kernel_call(
            functools.partial(conv_kernel, h == 0),
            [((rows, grid // CORES * width), BF16)] * 2,
            [*gated, left, right, taps, bn, w_p],
            spaces={2: pl.ANY, 3: pl.ANY} if h else {},
            scratch=[pltpu.VMEM((rows + 2 * HALO, padded), F32), pltpu.VMEM((rows, padded), BF16)],
        )
        theirs = exchange(send, "grid", 1)

        def pair_sum(a):
            cols = slice(a * width, (a + 1) * width)
            return keep[:, cols].astype(F32) + theirs[:, cols].astype(F32)

        result = middle[h].astype(F32) + pair_sum(0)
        for a in range(1, grid // CORES):
            result = result + exchange(pair_sum(a).astype(BF16), "grid", CORES * a).astype(F32)
        outs[h] = result.astype(BF16)
    return jnp.concatenate([outs[0][:quarter], outs[1], outs[0][quarter:]], axis=0)


def solution(mesh):
    return jax.shard_map(
        on_device,
        mesh=mesh,
        in_specs=(
            P(("parts", "ctx"), "grid"),
            P("grid"),
            P("grid"),
            P(None, "grid"),
            P(None, "grid"),
            P(None, "grid"),
            P("grid", None),
            P("grid"),
            P("grid"),
            P(None, "grid"),
            P(None, "grid"),
            P(None, "grid"),
            P("grid"),
            P("grid"),
            P("grid", None),
        ),
        out_specs=P(("parts", "ctx"), "grid"),
        check_vma=False,
    )
```

```python
import functools
import math

import jax
import jax.numpy as jnp
from jax import lax
from jax.experimental import pallas as pl
from jax.experimental.pallas import tpu as pltpu
from jax.sharding import PartitionSpec as P

HEAD_DIM = 64
PAIR = 2 * HEAD_DIM
KERNEL = 31
HALF = 15
HALO = 16
EPSILON = 1e-05
CORES = 2
VMEM_BYTES = 16 * 1024 * 1024
BF16 = jnp.bfloat16
F32 = jnp.float32
SCORE_SCALE = math.log2(math.e) / math.sqrt(HEAD_DIM)


def exchange(cells, axis, distance):
    count = lax.axis_size(axis)
    return lax.ppermute(cells, axis, [(i, i ^ distance) for i in range(count)])


def kernel_call(body, outs, operands, spaces=None, scratch=(), aliases=None):
    spaces = spaces or {}
    operands = [
        pltpu.with_memory_space_constraint(cells, pltpu.HBM) if spaces.get(i) == pltpu.HBM else cells
        for i, cells in enumerate(operands)
    ]
    in_specs = [
        pl.BlockSpec(memory_space=spaces.get(i, pltpu.VMEM)) for i in range(len(operands))
    ]
    return pl.pallas_call(
        body,
        in_specs=in_specs,
        out_specs=tuple(pl.BlockSpec(memory_space=pltpu.VMEM) for _ in outs),
        out_shape=tuple(jax.ShapeDtypeStruct(shape, dtype) for shape, dtype in outs),
        scratch_shapes=list(scratch),
        input_output_aliases=aliases or {},
        compiler_params=pltpu.CompilerParams(vmem_limit_bytes=VMEM_BYTES),
        cost_estimate=pl.CostEstimate(flops=1000, bytes_accessed=1000, transcendentals=0),
    )(*operands)


def after(cells, *done):
    def body(*refs):
        pass

    anywhere = pl.BlockSpec(memory_space=pl.ANY)
    return pl.pallas_call(
        body,
        in_specs=[anywhere] * (1 + len(done)),
        out_specs=anywhere,
        out_shape=jax.ShapeDtypeStruct(cells.shape, cells.dtype),
        input_output_aliases={0: 0},
        compiler_params=pltpu.CompilerParams(vmem_limit_bytes=64 * 1024),
        cost_estimate=pl.CostEstimate(flops=0, bytes_accessed=0, transcendentals=0),
    )(cells, *done)


def fold_kernel(order, which, count, me_ref, gains_ref, *refs):
    sources, (folded_ref, sums_ref), weights, done = refs[:count], refs[count : count + 2], refs[count + 2 : -1], refs[-1]
    copies = [pltpu.make_async_copy(sources[n], weights[n], done.at[n]) for n in range(count)]
    for copy in copies:
        copy.start()
    width = gains_ref.shape[1]
    columns = weights[0].shape[1]
    factors = []
    for r in order:
        gains = gains_ref[pl.ds(pl.multiple_of((me_ref[0] ^ r) * 8, 8), 8), :]
        gain = jnp.transpose(jnp.broadcast_to(gains[which : which + 1, :], (PAIR, width)))
        bias = jnp.broadcast_to(gains[which + 1 : which + 2, :], (8, width)).astype(BF16)
        factors.append((gain, bias))
    for n, ref in enumerate(weights):
        copies[n].wait()
        total = jnp.zeros((8, columns), F32)
        for k, r in enumerate(order):
            gain, bias = factors[k]
            start = pl.multiple_of((me_ref[0] ^ r) * width, width)
            block = ref[pl.ds(start, width), :]
            total = total + jnp.dot(bias, block, preferred_element_type=F32)
            for j in range(columns // PAIR):
                target = (j * count + n) * PAIR
                folded_ref[k * width : (k + 1) * width, target : target + PAIR] = (
                    block[:, j * PAIR : (j + 1) * PAIR].astype(F32) * gain
                ).astype(BF16)
        for j in range(columns // PAIR):
            target = (j * count + n) * PAIR
            sums_ref[1:2, target : target + PAIR] = total[0:1, j * PAIR : (j + 1) * PAIR]
    sums = jnp.dot(jnp.ones((8, folded_ref.shape[0]), BF16), folded_ref[...], preferred_element_type=F32)
    sums_ref[0:1, :] = sums[0:1]


def folded(me, order, which, gains, weights):
    rows, columns = weights[0].shape
    total = columns * len(weights)
    spaces = {2 + n: pltpu.HBM for n in range(len(weights))}
    return kernel_call(
        functools.partial(fold_kernel, order, which, len(weights)),
        [((rows, total), BF16), ((2, total), F32)],
        [me, gains, *weights],
        spaces={0: pltpu.SMEM, **spaces},
        scratch=[pltpu.VMEM((rows, columns), BF16)] * len(weights) + [pltpu.SemaphoreType.DMA((len(weights),))],
    )


def stack_kernel(*refs):
    count = (len(refs) - 2) // 2
    sources, out_ref, rows, done = refs[:count], refs[count], refs[count + 1 : -1], refs[-1]
    copies = [pltpu.make_async_copy(sources[i], rows[i], done.at[i]) for i in range(count)]
    for copy in copies:
        copy.start()
    out_ref[...] = jnp.zeros_like(out_ref)
    for i, copy in enumerate(copies):
        copy.wait()
        out_ref[i : i + 1, :] = rows[i][...].astype(F32).reshape(1, out_ref.shape[1])


def reorder_kernel(order, me_ref, source_ref, out_ref, done):
    width = source_ref.shape[1] // len(order)
    copies = []
    for k, r in enumerate(order):
        cols = pl.ds(pl.multiple_of((me_ref[0] ^ r) * width, PAIR), width)
        copies.append(
            pltpu.make_async_copy(source_ref.at[:, cols], out_ref.at[:, k * width : (k + 1) * width], done.at[k])
        )
        copies[-1].start()
    for copy in copies:
        copy.wait()


def half_kernel(part_ref, source_ref, half_ref, done):
    rows = half_ref.shape[0]
    copy = pltpu.make_async_copy(
        source_ref.at[pl.ds(pl.multiple_of(part_ref[0] * rows, rows), rows), :], half_ref, done.at[0]
    )
    copy.start()
    copy.wait()


def row_statistics(refs):
    rows, width = refs[0].shape
    full = width * len(refs)
    means, scales = [], []
    step = math.gcd(rows, 64)
    for start in range(0, rows, step):
        parts = [ref[start : start + step, :].astype(F32) for ref in refs]
        mean = sum(jnp.sum(part, axis=1, keepdims=True) for part in parts) / full
        variance = sum(jnp.sum(jnp.square(part - mean), axis=1, keepdims=True) for part in parts) / full
        means.append(mean)
        scales.append(lax.rsqrt(variance + EPSILON))
    return jnp.concatenate(means, axis=0), jnp.concatenate(scales, axis=0)


def norm_product(cells, mean, scale, folded_ref, sums_ref, start, columns):
    cols = slice(start, start + columns)
    product = jnp.dot(cells, folded_ref[:, cols], preferred_element_type=F32)
    return (product - mean * sums_ref[0:1, cols]) * scale + sums_ref[1:2, cols]


def lane_masks():
    lanes = lax.broadcasted_iota(jnp.int32, (1, PAIR), 1)
    return lanes < HEAD_DIM


def keys_values(projected):
    low = lane_masks()
    values = projected[:, PAIR : 2 * PAIR]
    return (
        projected[:, :PAIR].astype(BF16),
        jnp.where(low, values, 1.0).astype(BF16),
        jnp.where(low, 1.0, values).astype(BF16),
    )


def project_kernel(count, first, *refs):
    blocks, (folded_ref, sums_ref, *refs) = refs[:count], refs[count:]
    key_ref, value_ref = refs[-2:]
    query_ref = refs[-3] if first else None
    mean, scale = row_statistics(blocks)
    cells = jnp.concatenate([ref[...] for ref in blocks], axis=1)
    low = lane_masks()
    for j in range(key_ref.shape[1] // PAIR):
        columns = (3 if first else 2) * PAIR
        projected = norm_product(cells, mean, scale, folded_ref, sums_ref, j * 3 * PAIR, columns)
        base = 2 * j * PAIR
        (
            key_ref[:, j * PAIR : (j + 1) * PAIR],
            value_ref[:, base : base + PAIR],
            value_ref[:, base + PAIR : base + 2 * PAIR],
        ) = keys_values(projected)
        if first:
            queries = projected[:, 2 * PAIR :] * SCORE_SCALE
            query_ref[:, base : base + PAIR] = jnp.where(low, queries, 0.0).astype(BF16)
            query_ref[:, base + PAIR : base + 2 * PAIR] = jnp.where(low, 0.0, queries).astype(BF16)


def rows_of(ref, spans, cols):
    return jnp.concatenate([ref[start : start + size, cols] for start, size in spans], axis=0)


def attend_pair(pair, spans, query_ref, keys, values, state_ref):
    for head in range(2):
        index = 2 * pair + head
        queries = rows_of(query_ref, spans, slice(index * PAIR, (index + 1) * PAIR))
        scores = lax.dot_general(queries, keys, (((1,), (1,)), ((), ())), preferred_element_type=F32)
        peak = jnp.max(scores, axis=1, keepdims=True)
        soft = jnp.exp2(scores - peak).astype(BF16)
        sums = jnp.dot(soft, values[head], preferred_element_type=F32)
        state_ref[:, 2 * index * PAIR : (2 * index + 1) * PAIR] = sums
        state_ref[:, (2 * index + 1) * PAIR : (2 * index + 2) * PAIR] = jnp.broadcast_to(peak, (peak.shape[0], PAIR))


def merge_head(old_ref, part_ref, spans, index):
    sums = slice(2 * index * PAIR, (2 * index + 1) * PAIR)
    peaks = slice((2 * index + 1) * PAIR, (2 * index + 2) * PAIR)
    old_peak, part_peak = rows_of(old_ref, spans, peaks), part_ref[:, peaks]
    peak = jnp.maximum(old_peak, part_peak)
    total = rows_of(old_ref, spans, sums) * jnp.exp2(old_peak - peak) + part_ref[:, sums] * jnp.exp2(part_peak - peak)
    return total, peak


def attend_kernel(first, last, spans, query_ref, key_ref, value_ref, *refs):
    if last:
        old_ref, attended, part = refs[0], refs[-2], refs[-1]
    elif first:
        part, token_ref = refs[-2:]
    else:
        old_ref, (state_ref, token_ref, part) = refs[0], refs[-3:]
    if not last:
        token_ref[...] = jnp.zeros_like(token_ref)
    pairs = query_ref.shape[1] // (2 * PAIR)
    for j in range(pairs):
        values = [value_ref[:, n * PAIR : (n + 1) * PAIR] for n in (2 * j, 2 * j + 1)]
        attend_pair(j, spans, query_ref, key_ref[:, j * PAIR : (j + 1) * PAIR], values, part)
    if first:
        return
    low = lane_masks()
    for j in range(pairs):
        heads = [merge_head(old_ref, part, spans, 2 * j + head) for head in range(2)]
        if last:
            (one, _), (two, _) = heads
            both = jnp.where(low, one, two)
            weight = pltpu.roll(jnp.where(low, two, one), HEAD_DIM, 1)
            attended[:, j * PAIR : (j + 1) * PAIR] = (both / weight).astype(BF16)
        else:
            for head, (sums, peak) in enumerate(heads):
                at = 2 * (2 * j + head) * PAIR
                state_ref[:, at : at + PAIR] = sums
                state_ref[:, at + PAIR : at + 2 * PAIR] = peak


def middle_kernel(count, order, spans, me_ref, part_ref, odd_ref, *refs):
    attended, frames_refs, refs = refs[:count], refs[count : 2 * count], refs[2 * count :]
    *pieces, folded_ref, sums_ref, own_ref, out_ref, near_ref, far_ref, middle = refs
    total = out_ref.shape[0]
    width = frames_refs[0].shape[1]
    cells = jnp.concatenate([ref[:, :width] for ref in attended], axis=1)
    swap = part_ref[0] != 0

    def weights(k):
        if width % PAIR:
            cols = slice(k * width, (k + 1) * width)
        else:
            cols = pl.ds(pl.multiple_of((me_ref[0] ^ order[k]) * width, PAIR), width)
        rows, index = [], 0
        while index < len(pieces):
            mine = pieces[index][:, cols]
            index += 1
            if mine.shape[0] < width:
                other = pieces[index][:, cols]
                index += 1
                mine = jnp.concatenate([jnp.where(swap, other, mine), jnp.where(swap, mine, other)], axis=0)
            rows.append(mine)
        return jnp.concatenate(rows, axis=0)

    for k in range(0, count, 2):
        both = jnp.concatenate([weights(k), weights(k + 1)], axis=1)
        share = jnp.dot(cells, both, preferred_element_type=F32)
        for n in range(2):
            cols = slice((k + n) * width, (k + n + 1) * width)
            own = jnp.concatenate([frames_refs[k + n][start : start + size, :] for start, size in spans], axis=0)
            middle[:, cols] = (own.astype(F32) + share[:, n * width : (n + 1) * width]).astype(BF16)
    own_ref[...] = middle[:, :width]
    mean, scale = row_statistics((middle,))
    cells = middle[...]
    for j in range(out_ref.shape[1] // PAIR):
        both = norm_product(cells, mean, scale, folded_ref, sums_ref, j * 2 * PAIR, 2 * PAIR)
        out_ref[:, j * PAIR : (j + 1) * PAIR] = (
            both[:, :PAIR] / (1.0 + jnp.exp(-both[:, PAIR:]))
        ).astype(BF16)
    odd = odd_ref[0] != 0
    head, tail = out_ref[:HALO, :], out_ref[total - HALO :, :]
    near_ref[...] = jnp.where(odd, head, tail)
    far_ref[...] = jnp.where(odd, tail, head)


def conv_rows(padded, start, piece, cols, taps, scale, shift):
    window = padded[pl.ds(start, piece + 2 * HALO), cols]
    convolved = None
    for residue in range(8):
        part = None
        for offset in range(residue, KERNEL + 1, 8):
            if offset == 0:
                continue
            base = offset - residue
            term = taps[offset - 1] * window[base : base + piece + 8]
            part = term if part is None else part + term
        part = part[residue : residue + piece]
        convolved = part if convolved is None else convolved + part
    value = convolved * scale + shift
    return (value / (1.0 + jnp.exp(-value))).astype(BF16)


def conv_kernel(outer, first_ref, second_ref, *refs):
    if outer:
        odd_ref, near_ref, far_ref, *refs = refs
        odd, near, far = odd_ref[0] != 0, near_ref[...], far_ref[...]
    taps_ref, bn_ref, w_ref, keep_ref, send_ref, padded, activated = refs
    total, width = first_ref.shape
    half = keep_ref.shape[1]
    piece, edge = 32, total // 2
    if outer:
        runs = (
            (jnp.where(odd, near, far), first_ref[:edge, :], second_ref[:HALO, :]),
            (second_ref[second_ref.shape[0] - HALO :, :], first_ref[edge:, :], jnp.where(odd, far, near)),
        )
    else:
        runs = ((first_ref[edge - HALO : edge, :], second_ref[...], first_ref[edge : edge + HALO, :]),)
    at = 0
    for before, rows, behind in runs:
        count = rows.shape[0]
        padded[0:HALO, :] = before.astype(F32)
        padded[HALO : HALO + count, :] = rows.astype(F32)
        padded[HALO + count : 2 * HALO + count, :] = behind.astype(F32)
        for col in range(0, width, PAIR):
            cols = slice(col, col + PAIR)
            taps = [taps_ref[j : j + 1, cols] for j in range(KERNEL)]
            scale, shift = bn_ref[0:1, cols], bn_ref[1:2, cols]

            def block(index, carry, at=at):
                start = pl.multiple_of(index * piece, piece)
                target = pl.multiple_of(at + index * piece, piece)
                activated[pl.ds(target, piece), cols] = conv_rows(padded, start, piece, cols, taps, scale, shift)
                return carry

            lax.fori_loop(0, count // piece, block, 0, unroll=4)
        at += count
    share = activated[...]
    send_ref[...] = jnp.dot(share, w_ref[:, half:], preferred_element_type=F32).astype(BF16)
    keep_ref[...] = jnp.dot(share, w_ref[:, :half], preferred_element_type=F32).astype(BF16)


def pad_columns(weight, width):
    if weight.shape[1] == width:
        return weight
    return jnp.pad(weight, ((0, 0), (0, width - weight.shape[1])))


def on_device(
    frames_in,
    norm1_gain,
    norm1_bias,
    w_query,
    w_key,
    w_value,
    w_out,
    norm2_gain,
    norm2_bias,
    w_glu_value,
    w_glu_gate,
    depth_kernel,
    bn_scale,
    bn_shift,
    w_proj,
):
    frames, width = frames_in.shape
    grid, ctx = lax.axis_size("grid"), lax.axis_size("ctx")
    me = lax.axis_index("grid")
    place = me.astype(jnp.int32).reshape(1)
    odd = (lax.axis_index("ctx") % 2).astype(jnp.int32).reshape(1)
    order = list(range(0, grid, CORES)) + list(range(1, grid, CORES))
    padded = -(-width // PAIR) * PAIR
    every = ((0, frames),)

    def by_distance(cells):
        return jnp.concatenate(
            [lax.dynamic_slice_in_dim(cells, (me ^ r) * width, width, 1) for r in order], axis=1
        )

    def over_chips(block):
        return [exchange(block, "grid", CORES * a) for a in range(1, grid // CORES)]

    def other_core(blocks):
        return [exchange(block, "grid", 1) for block in blocks]

    vectors = [norm1_gain, norm1_bias, norm2_gain, norm2_bias]
    (gains,) = kernel_call(
        stack_kernel,
        [((8, width), F32)],
        vectors,
        spaces={i: pltpu.HBM for i in range(len(vectors))},
        scratch=[pltpu.VMEM((width,), BF16)] * len(vectors) + [pltpu.SemaphoreType.DMA((len(vectors),))],
    )
    gains = lax.all_gather(gains, "grid", axis=0, tiled=True)
    raw = {0: frames_in}
    chips = {0: over_chips(frames_in)}
    for k in reversed(range(ctx.bit_length() - 1)):
        raw[1 << k] = exchange(frames_in, "ctx", 1 << k)

    w_query, w_key, w_value, w_glu_value, w_glu_gate = (
        pad_columns(weight, padded) for weight in (w_query, w_key, w_value, w_glu_value, w_glu_gate)
    )
    if width % PAIR:
        row_pad = ((0, padded - width), (0, 0))
        w_p = jnp.pad(by_distance(w_proj), row_pad)
    else:
        (w_p,) = kernel_call(
            functools.partial(reorder_kernel, order),
            [(w_proj.shape, BF16)],
            [place, w_proj],
            spaces={0: pltpu.SMEM, 1: pltpu.HBM},
            scratch=[pltpu.SemaphoreType.DMA((grid,))],
        )
    taps = pad_columns(depth_kernel, padded)
    bn = pad_columns(jnp.stack([bn_scale, bn_shift]), padded)
    qkv, qkv_sums = folded(place, order, 0, gains, (w_key, w_value, w_query))
    chips[0] = [after(block, qkv_sums) for block in chips[0]]
    glu, glu_sums = folded(place, order, 2, gains, (w_glu_value, w_glu_gate))

    parts = lax.axis_size("parts")
    part = lax.axis_index("parts").astype(jnp.int32).reshape(1)
    if parts == 2:
        (half,) = kernel_call(
            half_kernel,
            [((width // 2, w_out.shape[1]), BF16)],
            [part, w_out],
            spaces={0: pltpu.SMEM, 1: pltpu.HBM},
            scratch=[pltpu.SemaphoreType.DMA((1,))],
        )
    else:
        half = w_out
    crossed = over_chips(after(half, *chips[0]))
    state_shape = ((frames, 4 * padded), F32)
    token_shape = ((8, 128), F32)
    wide, narrow = ((frames, 2 * padded), BF16), ((frames, padded), BF16)
    chips[1] = [exchange(block, "ctx", 1) for block in chips[0]]
    own = [frames_in] + chips[0]
    own_blocks = own + other_core(own)
    n = len(own_blocks)
    early = [*[raw[s] for s in raw if s], glu_sums, w_p]
    queries, keys, values = kernel_call(
        functools.partial(project_kernel, n, True),
        [wide, narrow, wide],
        [*own_blocks, qkv, qkv_sums, *early],
        spaces={n + 2 + i: pl.ANY for i in range(len(early))},
    )
    def prepare(s, done):
        if 2 <= s < ctx:
            low = s & -s
            if s != low:
                raw[s] = after(exchange(raw[s ^ low], "ctx", low), done)
            chips[s] = over_chips(raw[s])

    prepare(2, None)
    state, token = kernel_call(
        functools.partial(attend_kernel, True, False, every),
        [state_shape, token_shape],
        [queries, keys, values, *crossed],
        spaces={3 + i: pl.ANY for i in range(len(crossed))},
    )
    crossed = [after(block, token) for block in crossed]
    swapped = [exchange(block, "parts", 1) for block in crossed] if parts == 2 else []
    moved = {1: [after(block, token) for block in chips[1]]}
    for s in range(1, ctx):
        last = s == ctx - 1
        mine = [raw[s]] + moved[s]
        keys, values = kernel_call(
            functools.partial(project_kernel, n, False),
            [narrow, wide],
            [*mine, *other_core(mine), qkv, qkv_sums],
        )
        if last:
            break
        prepare(s + 2, token)
        moved[s + 1] = [after(block, token) for block in chips[s + 1]]
        behind = [raw[s + 2]] if s + 2 < ctx else []
        behind += moved[s + 1]
        state, token = kernel_call(
            functools.partial(attend_kernel, False, False, every),
            [state_shape, token_shape],
            [queries, keys, values, state, *behind],
            spaces={4 + i: pl.ANY for i in range(len(behind))},
            aliases={3: 0},
            scratch=[pltpu.VMEM(*state_shape)],
        )
    edge = frames // 8
    spans = (((0, edge), (frames - edge, edge)), ((edge, frames - 2 * edge),))
    sizes = (2 * edge, frames - 2 * edge)
    attended = []
    for h, rows in enumerate(sizes):
        (mine,) = kernel_call(
            functools.partial(attend_kernel, False, True, spans[h]),
            [((rows, padded), BF16)],
            [queries, keys, values, state, *(attended[0][1:] if h else [])],
            spaces={4 + i: pl.ANY for i in range(len(attended[0]) - 1 if h else 0)},
            scratch=[pltpu.VMEM((rows, 4 * padded), F32)],
        )
        attended.append([mine] + over_chips(mine))
    swapped = [after(block, attended[0][0]) for block in swapped]
    pieces = [w_out]
    for a, block in enumerate(crossed):
        pieces += [block, swapped[a]] if swapped else [block]
    pieces = pieces + other_core(pieces)
    if width % PAIR:
        pieces = [by_distance(piece) for piece in pieces]
    middle, gated = [], []
    for h, rows in enumerate(sizes):
        mine = attended[h]
        if h:
            mine = mine[:1] + [after(block, near, far) for block in mine[1:]]
        results = kernel_call(
            functools.partial(middle_kernel, n, order, spans[h]),
            [((rows, width), BF16), ((rows, padded), BF16), ((HALO, padded), BF16), ((HALO, padded), BF16)],
            [place, part, odd, *mine, *other_core(mine), *own_blocks, *pieces, glu, glu_sums],
            spaces={0: pltpu.SMEM, 1: pltpu.SMEM, 2: pltpu.SMEM},
            scratch=[pltpu.VMEM((rows, grid * width), BF16)],
        )
        middle.append(results[0])
        gated.append(results[1])
        if h == 0:
            near = exchange(results[2], "ctx", 1)
            between = [(i, i + 1) for i in range(1, ctx - 1, 2)]
            far = lax.ppermute(results[3], "ctx", between + [(b, a) for a, b in between])
    outs = [None, None]
    for h, around in ((1, []), (0, [odd, near, far])):
        rows = sizes[h]
        keep, send = kernel_call(
            functools.partial(conv_kernel, h == 0),
            [((rows, grid // CORES * width), BF16)] * 2,
            [*gated, *around, taps, bn, w_p],
            spaces={} if h else {2: pltpu.SMEM},
            scratch=[pltpu.VMEM((rows + 2 * HALO, padded), F32), pltpu.VMEM((rows, padded), BF16)],
        )
        theirs = exchange(send, "grid", 1)

        def pair_sum(a):
            cols = slice(a * width, (a + 1) * width)
            return keep[:, cols].astype(F32) + theirs[:, cols].astype(F32)

        result = middle[h].astype(F32) + pair_sum(0)
        for a in range(1, grid // CORES):
            result = result + exchange(pair_sum(a).astype(BF16), "grid", CORES * a).astype(F32)
        outs[h] = result.astype(BF16)
    return jnp.concatenate([outs[0][:edge], outs[1], outs[0][edge:]], axis=0)


def solution(mesh):
    return jax.shard_map(
        on_device,
        mesh=mesh,
        in_specs=(
            P(("parts", "ctx"), "grid"),
            P("grid"),
            P("grid"),
            P(None, "grid"),
            P(None, "grid"),
            P(None, "grid"),
            P("grid", None),
            P("grid"),
            P("grid"),
            P(None, "grid"),
            P(None, "grid"),
            P(None, "grid"),
            P("grid"),
            P("grid"),
            P("grid", None),
        ),
        out_specs=P(("parts", "ctx"), "grid"),
        check_vma=False,
    )
```

```python
import functools
import math

import jax
import jax.numpy as jnp
from jax import lax
from jax.experimental import pallas as pl
from jax.experimental.pallas import tpu as pltpu
from jax.sharding import PartitionSpec as P

HEAD_DIM = 64
PAIR = 2 * HEAD_DIM
KERNEL = 31
HALF = 15
HALO = 16
EPSILON = 1e-05
CORES = 2
VMEM_BYTES = 16 * 1024 * 1024
BF16 = jnp.bfloat16
F32 = jnp.float32
SCORE_SCALE = math.log2(math.e) / math.sqrt(HEAD_DIM)


def exchange(cells, axis, distance):
    count = lax.axis_size(axis)
    return lax.ppermute(cells, axis, [(i, i ^ distance) for i in range(count)])


def kernel_call(body, outs, operands, spaces=None, scratch=(), aliases=None):
    spaces = spaces or {}
    operands = [
        pltpu.with_memory_space_constraint(cells, pltpu.HBM) if spaces.get(i) == pltpu.HBM else cells
        for i, cells in enumerate(operands)
    ]
    in_specs = [
        pl.BlockSpec(memory_space=spaces.get(i, pltpu.VMEM)) for i in range(len(operands))
    ]
    return pl.pallas_call(
        body,
        in_specs=in_specs,
        out_specs=tuple(pl.BlockSpec(memory_space=pltpu.VMEM) for _ in outs),
        out_shape=tuple(jax.ShapeDtypeStruct(shape, dtype) for shape, dtype in outs),
        scratch_shapes=list(scratch),
        input_output_aliases=aliases or {},
        compiler_params=pltpu.CompilerParams(vmem_limit_bytes=VMEM_BYTES),
        cost_estimate=pl.CostEstimate(flops=1000, bytes_accessed=1000, transcendentals=0),
    )(*operands)


def after(cells, *done):
    def body(*refs):
        pass

    anywhere = pl.BlockSpec(memory_space=pl.ANY)
    return pl.pallas_call(
        body,
        in_specs=[anywhere] * (1 + len(done)),
        out_specs=anywhere,
        out_shape=jax.ShapeDtypeStruct(cells.shape, cells.dtype),
        input_output_aliases={0: 0},
        compiler_params=pltpu.CompilerParams(vmem_limit_bytes=64 * 1024),
        cost_estimate=pl.CostEstimate(flops=0, bytes_accessed=0, transcendentals=0),
    )(cells, *done)


def fold_kernel(order, which, count, me_ref, gains_ref, *refs):
    sources, (folded_ref, sums_ref), weights, done = refs[:count], refs[count : count + 2], refs[count + 2 : -1], refs[-1]
    copies = [pltpu.make_async_copy(sources[n], weights[n], done.at[n]) for n in range(count)]
    for copy in copies:
        copy.start()
    width = gains_ref.shape[1]
    columns = weights[0].shape[1]
    factors = []
    for r in order:
        gains = gains_ref[pl.ds(pl.multiple_of((me_ref[0] ^ r) * 8, 8), 8), :]
        gain = jnp.transpose(jnp.broadcast_to(gains[which : which + 1, :], (PAIR, width)))
        bias = jnp.broadcast_to(gains[which + 1 : which + 2, :], (8, width)).astype(BF16)
        factors.append((gain, bias))
    for n, ref in enumerate(weights):
        copies[n].wait()
        total = jnp.zeros((8, columns), F32)
        for k, r in enumerate(order):
            gain, bias = factors[k]
            start = pl.multiple_of((me_ref[0] ^ r) * width, width)
            block = ref[pl.ds(start, width), :]
            total = total + jnp.dot(bias, block, preferred_element_type=F32)
            for j in range(columns // PAIR):
                target = (j * count + n) * PAIR
                folded_ref[k * width : (k + 1) * width, target : target + PAIR] = (
                    block[:, j * PAIR : (j + 1) * PAIR].astype(F32) * gain
                ).astype(BF16)
        for j in range(columns // PAIR):
            target = (j * count + n) * PAIR
            sums_ref[1:2, target : target + PAIR] = total[0:1, j * PAIR : (j + 1) * PAIR]
    sums = jnp.dot(jnp.ones((8, folded_ref.shape[0]), BF16), folded_ref[...], preferred_element_type=F32)
    sums_ref[0:1, :] = sums[0:1]


def folded(me, order, which, gains, weights):
    rows, columns = weights[0].shape
    total = columns * len(weights)
    spaces = {2 + n: pltpu.HBM for n in range(len(weights))}
    return kernel_call(
        functools.partial(fold_kernel, order, which, len(weights)),
        [((rows, total), BF16), ((2, total), F32)],
        [me, gains, *weights],
        spaces={0: pltpu.SMEM, **spaces},
        scratch=[pltpu.VMEM((rows, columns), BF16)] * len(weights) + [pltpu.SemaphoreType.DMA((len(weights),))],
    )


def stack_kernel(*refs):
    count = (len(refs) - 2) // 2
    sources, out_ref, rows, done = refs[:count], refs[count], refs[count + 1 : -1], refs[-1]
    copies = [pltpu.make_async_copy(sources[i], rows[i], done.at[i]) for i in range(count)]
    for copy in copies:
        copy.start()
    out_ref[...] = jnp.zeros_like(out_ref)
    for i, copy in enumerate(copies):
        copy.wait()
        out_ref[i : i + 1, :] = rows[i][...].astype(F32).reshape(1, out_ref.shape[1])


def reorder_kernel(order, me_ref, source_ref, out_ref, done):
    width = source_ref.shape[1] // len(order)
    copies = []
    for k, r in enumerate(order):
        cols = pl.ds(pl.multiple_of((me_ref[0] ^ r) * width, PAIR), width)
        copies.append(
            pltpu.make_async_copy(source_ref.at[:, cols], out_ref.at[:, k * width : (k + 1) * width], done.at[k])
        )
        copies[-1].start()
    for copy in copies:
        copy.wait()


def half_kernel(part_ref, source_ref, half_ref, done):
    rows = half_ref.shape[0]
    copy = pltpu.make_async_copy(
        source_ref.at[pl.ds(pl.multiple_of(part_ref[0] * rows, rows), rows), :], half_ref, done.at[0]
    )
    copy.start()
    copy.wait()


def row_statistics(refs):
    rows, width = refs[0].shape
    full = width * len(refs)
    means, scales = [], []
    step = math.gcd(rows, 64)
    for start in range(0, rows, step):
        parts = [ref[start : start + step, :].astype(F32) for ref in refs]
        mean = sum(jnp.sum(part, axis=1, keepdims=True) for part in parts) / full
        variance = sum(jnp.sum(jnp.square(part - mean), axis=1, keepdims=True) for part in parts) / full
        means.append(mean)
        scales.append(lax.rsqrt(variance + EPSILON))
    return jnp.concatenate(means, axis=0), jnp.concatenate(scales, axis=0)


def norm_product(cells, mean, scale, folded_ref, sums_ref, start, columns):
    cols = slice(start, start + columns)
    product = jnp.dot(cells, folded_ref[:, cols], preferred_element_type=F32)
    return (product - mean * sums_ref[0:1, cols]) * scale + sums_ref[1:2, cols]


def lane_masks():
    lanes = lax.broadcasted_iota(jnp.int32, (1, PAIR), 1)
    return lanes < HEAD_DIM


def keys_values(projected):
    low = lane_masks()
    values = projected[:, PAIR : 2 * PAIR]
    return (
        projected[:, :PAIR].astype(BF16),
        jnp.where(low, values, 1.0).astype(BF16),
        jnp.where(low, 1.0, values).astype(BF16),
    )


def project_kernel(count, first, *refs):
    blocks, (folded_ref, sums_ref, *refs) = refs[:count], refs[count:]
    key_ref, value_ref = refs[-2:]
    query_ref = refs[-3] if first else None
    mean, scale = row_statistics(blocks)
    cells = jnp.concatenate([ref[...] for ref in blocks], axis=1)
    low = lane_masks()
    for j in range(key_ref.shape[1] // PAIR):
        columns = (3 if first else 2) * PAIR
        projected = norm_product(cells, mean, scale, folded_ref, sums_ref, j * 3 * PAIR, columns)
        base = 2 * j * PAIR
        (
            key_ref[:, j * PAIR : (j + 1) * PAIR],
            value_ref[:, base : base + PAIR],
            value_ref[:, base + PAIR : base + 2 * PAIR],
        ) = keys_values(projected)
        if first:
            queries = projected[:, 2 * PAIR :] * SCORE_SCALE
            query_ref[:, base : base + PAIR] = jnp.where(low, queries, 0.0).astype(BF16)
            query_ref[:, base + PAIR : base + 2 * PAIR] = jnp.where(low, 0.0, queries).astype(BF16)


def rows_of(ref, spans, cols):
    return jnp.concatenate([ref[start : start + size, cols] for start, size in spans], axis=0)


def attend_pair(pair, spans, query_ref, keys, values, state_ref):
    for head in range(2):
        index = 2 * pair + head
        queries = rows_of(query_ref, spans, slice(index * PAIR, (index + 1) * PAIR))
        scores = lax.dot_general(queries, keys, (((1,), (1,)), ((), ())), preferred_element_type=F32)
        peak = jnp.max(scores, axis=1, keepdims=True)
        soft = jnp.exp2(scores - peak).astype(BF16)
        sums = jnp.dot(soft, values[head], preferred_element_type=F32)
        state_ref[:, 2 * index * PAIR : (2 * index + 1) * PAIR] = sums
        state_ref[:, (2 * index + 1) * PAIR : (2 * index + 2) * PAIR] = jnp.broadcast_to(peak, (peak.shape[0], PAIR))


def merge_head(old_ref, part_ref, spans, index):
    sums = slice(2 * index * PAIR, (2 * index + 1) * PAIR)
    peaks = slice((2 * index + 1) * PAIR, (2 * index + 2) * PAIR)
    old_peak, part_peak = rows_of(old_ref, spans, peaks), part_ref[:, peaks]
    peak = jnp.maximum(old_peak, part_peak)
    total = rows_of(old_ref, spans, sums) * jnp.exp2(old_peak - peak) + part_ref[:, sums] * jnp.exp2(part_peak - peak)
    return total, peak


def attend_kernel(first, last, spans, query_ref, key_ref, value_ref, *refs):
    if last:
        old_ref, attended, part = refs[0], refs[-2], refs[-1]
    elif first:
        part, token_ref = refs[-2:]
    else:
        old_ref, (state_ref, token_ref, part) = refs[0], refs[-3:]
    if not last:
        token_ref[...] = jnp.zeros_like(token_ref)
    pairs = query_ref.shape[1] // (2 * PAIR)
    for j in range(pairs):
        values = [value_ref[:, n * PAIR : (n + 1) * PAIR] for n in (2 * j, 2 * j + 1)]
        attend_pair(j, spans, query_ref, key_ref[:, j * PAIR : (j + 1) * PAIR], values, part)
    if first:
        return
    low = lane_masks()
    for j in range(pairs):
        heads = [merge_head(old_ref, part, spans, 2 * j + head) for head in range(2)]
        if last:
            (one, _), (two, _) = heads
            both = jnp.where(low, one, two)
            weight = pltpu.roll(jnp.where(low, two, one), HEAD_DIM, 1)
            attended[:, j * PAIR : (j + 1) * PAIR] = (both / weight).astype(BF16)
        else:
            for head, (sums, peak) in enumerate(heads):
                at = 2 * (2 * j + head) * PAIR
                state_ref[:, at : at + PAIR] = sums
                state_ref[:, at + PAIR : at + 2 * PAIR] = peak


def middle_kernel(count, order, spans, me_ref, part_ref, odd_ref, *refs):
    attended, frames_refs, refs = refs[:count], refs[count : 2 * count], refs[2 * count :]
    *pieces, folded_ref, sums_ref, own_ref, out_ref, near_ref, far_ref, middle = refs
    total = out_ref.shape[0]
    width = frames_refs[0].shape[1]
    cells = jnp.concatenate([ref[:, :width] for ref in attended], axis=1)
    swap = part_ref[0] != 0

    def weights(k):
        if width % PAIR:
            cols = slice(k * width, (k + 1) * width)
        else:
            cols = pl.ds(pl.multiple_of((me_ref[0] ^ order[k]) * width, PAIR), width)
        rows, index = [], 0
        while index < len(pieces):
            mine = pieces[index][:, cols]
            index += 1
            if mine.shape[0] < width:
                other = pieces[index][:, cols]
                index += 1
                mine = jnp.concatenate([jnp.where(swap, other, mine), jnp.where(swap, mine, other)], axis=0)
            rows.append(mine)
        return jnp.concatenate(rows, axis=0)

    for k in range(0, count, 2):
        both = jnp.concatenate([weights(k), weights(k + 1)], axis=1)
        share = jnp.dot(cells, both, preferred_element_type=F32)
        for n in range(2):
            cols = slice((k + n) * width, (k + n + 1) * width)
            own = jnp.concatenate([frames_refs[k + n][start : start + size, :] for start, size in spans], axis=0)
            middle[:, cols] = (own.astype(F32) + share[:, n * width : (n + 1) * width]).astype(BF16)
    own_ref[...] = middle[:, :width]
    mean, scale = row_statistics((middle,))
    cells = middle[...]
    for j in range(out_ref.shape[1] // PAIR):
        both = norm_product(cells, mean, scale, folded_ref, sums_ref, j * 2 * PAIR, 2 * PAIR)
        out_ref[:, j * PAIR : (j + 1) * PAIR] = (
            both[:, :PAIR] / (1.0 + jnp.exp(-both[:, PAIR:]))
        ).astype(BF16)
    odd = odd_ref[0] != 0
    head, tail = out_ref[:HALO, :], out_ref[total - HALO :, :]
    near_ref[...] = jnp.where(odd, head, tail)
    far_ref[...] = jnp.where(odd, tail, head)


def conv_rows(padded, start, piece, cols, taps, scale, shift):
    window = padded[pl.ds(start, piece + 2 * HALO), cols]
    convolved = None
    for residue in range(8):
        part = None
        for offset in range(residue, KERNEL + 1, 8):
            if offset == 0:
                continue
            base = offset - residue
            term = taps[offset - 1] * window[base : base + piece + 8]
            part = term if part is None else part + term
        part = part[residue : residue + piece]
        convolved = part if convolved is None else convolved + part
    value = convolved * scale + shift
    return (value / (1.0 + jnp.exp(-value))).astype(BF16)


def conv_kernel(outer, first_ref, second_ref, *refs):
    if outer:
        odd_ref, near_ref, far_ref, *refs = refs
        odd, near, far = odd_ref[0] != 0, near_ref[...], far_ref[...]
    taps_ref, bn_ref, w_ref, keep_ref, send_ref, padded, activated = refs
    total, width = first_ref.shape
    half = keep_ref.shape[1]
    piece, quarter = 32, total // 2
    if outer:
        runs = (
            (jnp.where(odd, near, far), first_ref[:quarter, :], second_ref[:HALO, :]),
            (second_ref[total - HALO :, :], first_ref[quarter:, :], jnp.where(odd, far, near)),
        )
    else:
        runs = ((first_ref[quarter - HALO : quarter, :], second_ref[...], first_ref[quarter : quarter + HALO, :]),)
    at = 0
    for before, rows, behind in runs:
        count = rows.shape[0]
        padded[0:HALO, :] = before.astype(F32)
        padded[HALO : HALO + count, :] = rows.astype(F32)
        padded[HALO + count : 2 * HALO + count, :] = behind.astype(F32)
        for col in range(0, width, PAIR):
            cols = slice(col, col + PAIR)
            taps = [taps_ref[j : j + 1, cols] for j in range(KERNEL)]
            scale, shift = bn_ref[0:1, cols], bn_ref[1:2, cols]

            def block(index, carry, at=at):
                start = pl.multiple_of(index * piece, piece)
                target = pl.multiple_of(at + index * piece, piece)
                activated[pl.ds(target, piece), cols] = conv_rows(padded, start, piece, cols, taps, scale, shift)
                return carry

            lax.fori_loop(0, count // piece, block, 0, unroll=4)
        at += count
    share = activated[...]
    send_ref[...] = jnp.dot(share, w_ref[:, half:], preferred_element_type=F32).astype(BF16)
    keep_ref[...] = jnp.dot(share, w_ref[:, :half], preferred_element_type=F32).astype(BF16)


def pad_columns(weight, width):
    if weight.shape[1] == width:
        return weight
    return jnp.pad(weight, ((0, 0), (0, width - weight.shape[1])))


def on_device(
    frames_in,
    norm1_gain,
    norm1_bias,
    w_query,
    w_key,
    w_value,
    w_out,
    norm2_gain,
    norm2_bias,
    w_glu_value,
    w_glu_gate,
    depth_kernel,
    bn_scale,
    bn_shift,
    w_proj,
):
    frames, width = frames_in.shape
    grid, ctx = lax.axis_size("grid"), lax.axis_size("ctx")
    me = lax.axis_index("grid")
    place = me.astype(jnp.int32).reshape(1)
    odd = (lax.axis_index("ctx") % 2).astype(jnp.int32).reshape(1)
    order = list(range(0, grid, CORES)) + list(range(1, grid, CORES))
    padded = -(-width // PAIR) * PAIR
    every = ((0, frames),)

    def by_distance(cells):
        return jnp.concatenate(
            [lax.dynamic_slice_in_dim(cells, (me ^ r) * width, width, 1) for r in order], axis=1
        )

    def over_chips(block):
        return [exchange(block, "grid", CORES * a) for a in range(1, grid // CORES)]

    def other_core(blocks):
        return [exchange(block, "grid", 1) for block in blocks]

    vectors = [norm1_gain, norm1_bias, norm2_gain, norm2_bias]
    (gains,) = kernel_call(
        stack_kernel,
        [((8, width), F32)],
        vectors,
        spaces={i: pltpu.HBM for i in range(len(vectors))},
        scratch=[pltpu.VMEM((width,), BF16)] * len(vectors) + [pltpu.SemaphoreType.DMA((len(vectors),))],
    )
    gains = lax.all_gather(gains, "grid", axis=0, tiled=True)
    raw = {0: frames_in}
    chips = {0: over_chips(frames_in)}
    for k in reversed(range(ctx.bit_length() - 1)):
        raw[1 << k] = exchange(frames_in, "ctx", 1 << k)

    w_query, w_key, w_value, w_glu_value, w_glu_gate = (
        pad_columns(weight, padded) for weight in (w_query, w_key, w_value, w_glu_value, w_glu_gate)
    )
    if width % PAIR:
        row_pad = ((0, padded - width), (0, 0))
        w_p = jnp.pad(by_distance(w_proj), row_pad)
    else:
        (w_p,) = kernel_call(
            functools.partial(reorder_kernel, order),
            [(w_proj.shape, BF16)],
            [place, w_proj],
            spaces={0: pltpu.SMEM, 1: pltpu.HBM},
            scratch=[pltpu.SemaphoreType.DMA((grid,))],
        )
    taps = pad_columns(depth_kernel, padded)
    bn = pad_columns(jnp.stack([bn_scale, bn_shift]), padded)
    qkv, qkv_sums = folded(place, order, 0, gains, (w_key, w_value, w_query))
    chips[0] = [after(block, qkv_sums) for block in chips[0]]
    glu, glu_sums = folded(place, order, 2, gains, (w_glu_value, w_glu_gate))

    parts = lax.axis_size("parts")
    part = lax.axis_index("parts").astype(jnp.int32).reshape(1)
    if parts == 2:
        (half,) = kernel_call(
            half_kernel,
            [((width // 2, w_out.shape[1]), BF16)],
            [part, w_out],
            spaces={0: pltpu.SMEM, 1: pltpu.HBM},
            scratch=[pltpu.SemaphoreType.DMA((1,))],
        )
    else:
        half = w_out
    crossed = over_chips(after(half, *chips[0]))
    state_shape = ((frames, 4 * padded), F32)
    token_shape = ((8, 128), F32)
    wide, narrow = ((frames, 2 * padded), BF16), ((frames, padded), BF16)
    chips[1] = [exchange(block, "ctx", 1) for block in chips[0]]
    own = [frames_in] + chips[0]
    own_blocks = own + other_core(own)
    n = len(own_blocks)
    early = [*[raw[s] for s in raw if s], glu_sums, w_p]
    queries, keys, values = kernel_call(
        functools.partial(project_kernel, n, True),
        [wide, narrow, wide],
        [*own_blocks, qkv, qkv_sums, *early],
        spaces={n + 2 + i: pl.ANY for i in range(len(early))},
    )
    def prepare(s, done):
        if 2 <= s < ctx:
            low = s & -s
            if s != low:
                raw[s] = after(exchange(raw[s ^ low], "ctx", low), done)
            chips[s] = over_chips(raw[s])

    prepare(2, None)
    state, token = kernel_call(
        functools.partial(attend_kernel, True, False, every),
        [state_shape, token_shape],
        [queries, keys, values, *crossed],
        spaces={3 + i: pl.ANY for i in range(len(crossed))},
    )
    crossed = [after(block, token) for block in crossed]
    swapped = [exchange(block, "parts", 1) for block in crossed] if parts == 2 else []
    moved = {1: [after(block, token) for block in chips[1]]}
    for s in range(1, ctx):
        last = s == ctx - 1
        mine = [raw[s]] + moved[s]
        keys, values = kernel_call(
            functools.partial(project_kernel, n, False),
            [narrow, wide],
            [*mine, *other_core(mine), qkv, qkv_sums],
        )
        if last:
            break
        prepare(s + 2, token)
        moved[s + 1] = [after(block, token) for block in chips[s + 1]]
        behind = [raw[s + 2]] if s + 2 < ctx else []
        behind += moved[s + 1]
        state, token = kernel_call(
            functools.partial(attend_kernel, False, False, every),
            [state_shape, token_shape],
            [queries, keys, values, state, *behind],
            spaces={4 + i: pl.ANY for i in range(len(behind))},
            aliases={3: 0},
            scratch=[pltpu.VMEM(*state_shape)],
        )
    rows, quarter = frames // 2, frames // 4
    spans = (((0, quarter), (3 * quarter, quarter)), ((quarter, rows),))
    attended = []
    for h in range(2):
        (mine,) = kernel_call(
            functools.partial(attend_kernel, False, True, spans[h]),
            [((rows, padded), BF16)],
            [queries, keys, values, state],
            scratch=[pltpu.VMEM((rows, 4 * padded), F32)],
        )
        attended.append([mine] + over_chips(mine))
    swapped = [after(block, attended[0][0]) for block in swapped]
    pieces = [w_out]
    for a, block in enumerate(crossed):
        pieces += [block, swapped[a]] if swapped else [block]
    pieces = pieces + other_core(pieces)
    if width % PAIR:
        pieces = [by_distance(piece) for piece in pieces]
    middle, gated = [], []
    for h in range(2):
        mine = attended[h]
        done = gated[0] if h else attended[1][0]
        mine = mine[:1] + [after(block, done) for block in mine[1:]]
        results = kernel_call(
            functools.partial(middle_kernel, n, order, spans[h]),
            [((rows, width), BF16), ((rows, padded), BF16), ((HALO, padded), BF16), ((HALO, padded), BF16)],
            [place, part, odd, *mine, *other_core(mine), *own_blocks, *pieces, glu, glu_sums],
            spaces={0: pltpu.SMEM, 1: pltpu.SMEM, 2: pltpu.SMEM},
            scratch=[pltpu.VMEM((rows, grid * width), BF16)],
        )
        middle.append(results[0])
        gated.append(results[1])
        if h == 0:
            near = exchange(results[2], "ctx", 1)
            between = [(i, i + 1) for i in range(1, ctx - 1, 2)]
            far = lax.ppermute(results[3], "ctx", between + [(b, a) for a, b in between])
    outs = [None, None]
    for h, around in ((1, []), (0, [odd, near, far])):
        keep, send = kernel_call(
            functools.partial(conv_kernel, h == 0),
            [((rows, grid // CORES * width), BF16)] * 2,
            [*gated, *around, taps, bn, w_p],
            spaces={} if h else {2: pltpu.SMEM},
            scratch=[pltpu.VMEM((rows + 2 * HALO, padded), F32), pltpu.VMEM((rows, padded), BF16)],
        )
        theirs = exchange(send, "grid", 1)

        def pair_sum(a):
            cols = slice(a * width, (a + 1) * width)
            return keep[:, cols].astype(F32) + theirs[:, cols].astype(F32)

        result = middle[h].astype(F32) + pair_sum(0)
        for a in range(1, grid // CORES):
            result = result + exchange(pair_sum(a).astype(BF16), "grid", CORES * a).astype(F32)
        outs[h] = result.astype(BF16)
    return jnp.concatenate([outs[0][:quarter], outs[1], outs[0][quarter:]], axis=0)


def solution(mesh):
    return jax.shard_map(
        on_device,
        mesh=mesh,
        in_specs=(
            P(("parts", "ctx"), "grid"),
            P("grid"),
            P("grid"),
            P(None, "grid"),
            P(None, "grid"),
            P(None, "grid"),
            P("grid", None),
            P("grid"),
            P("grid"),
            P(None, "grid"),
            P(None, "grid"),
            P(None, "grid"),
            P("grid"),
            P("grid"),
            P("grid", None),
        ),
        out_specs=P(("parts", "ctx"), "grid"),
        check_vma=False,
    )
```

```python
import functools
import math

import jax
import jax.numpy as jnp
from jax import lax
from jax.experimental import pallas as pl
from jax.experimental.pallas import tpu as pltpu
from jax.sharding import PartitionSpec as P

HEAD_DIM = 64
PAIR = 2 * HEAD_DIM
KERNEL = 31
HALF = 15
HALO = 16
EPSILON = 1e-05
CORES = 2
VMEM_BYTES = 16 * 1024 * 1024
BF16 = jnp.bfloat16
F32 = jnp.float32
SCORE_SCALE = math.log2(math.e) / math.sqrt(HEAD_DIM)


def exchange(cells, axis, distance):
    count = lax.axis_size(axis)
    return lax.ppermute(cells, axis, [(i, i ^ distance) for i in range(count)])


def kernel_call(body, outs, operands, spaces=None, scratch=(), aliases=None):
    spaces = spaces or {}
    operands = [
        pltpu.with_memory_space_constraint(cells, pltpu.HBM) if spaces.get(i) == pltpu.HBM else cells
        for i, cells in enumerate(operands)
    ]
    in_specs = [
        pl.BlockSpec(memory_space=spaces.get(i, pltpu.VMEM)) for i in range(len(operands))
    ]
    return pl.pallas_call(
        body,
        in_specs=in_specs,
        out_specs=tuple(pl.BlockSpec(memory_space=pltpu.VMEM) for _ in outs),
        out_shape=tuple(jax.ShapeDtypeStruct(shape, dtype) for shape, dtype in outs),
        scratch_shapes=list(scratch),
        input_output_aliases=aliases or {},
        compiler_params=pltpu.CompilerParams(vmem_limit_bytes=VMEM_BYTES),
        cost_estimate=pl.CostEstimate(flops=1000, bytes_accessed=1000, transcendentals=0),
    )(*operands)


def after(cells, *done):
    def body(*refs):
        pass

    anywhere = pl.BlockSpec(memory_space=pl.ANY)
    return pl.pallas_call(
        body,
        in_specs=[anywhere] * (1 + len(done)),
        out_specs=anywhere,
        out_shape=jax.ShapeDtypeStruct(cells.shape, cells.dtype),
        input_output_aliases={0: 0},
        compiler_params=pltpu.CompilerParams(vmem_limit_bytes=64 * 1024),
        cost_estimate=pl.CostEstimate(flops=0, bytes_accessed=0, transcendentals=0),
    )(cells, *done)


def fold_kernel(order, which, count, me_ref, gains_ref, *refs):
    sources, (folded_ref, sums_ref), weights, done = refs[:count], refs[count : count + 2], refs[count + 2 : -1], refs[-1]
    copies = [pltpu.make_async_copy(sources[n], weights[n], done.at[n]) for n in range(count)]
    for copy in copies:
        copy.start()
    width = gains_ref.shape[1]
    columns = weights[0].shape[1]
    factors = []
    for r in order:
        gains = gains_ref[pl.ds(pl.multiple_of((me_ref[0] ^ r) * 8, 8), 8), :]
        gain = jnp.transpose(jnp.broadcast_to(gains[which : which + 1, :], (PAIR, width)))
        bias = jnp.broadcast_to(gains[which + 1 : which + 2, :], (8, width)).astype(BF16)
        factors.append((gain, bias))
    for n, ref in enumerate(weights):
        copies[n].wait()
        total = jnp.zeros((8, columns), F32)
        for k, r in enumerate(order):
            gain, bias = factors[k]
            start = pl.multiple_of((me_ref[0] ^ r) * width, width)
            block = ref[pl.ds(start, width), :]
            total = total + jnp.dot(bias, block, preferred_element_type=F32)
            for j in range(columns // PAIR):
                target = (j * count + n) * PAIR
                folded_ref[k * width : (k + 1) * width, target : target + PAIR] = (
                    block[:, j * PAIR : (j + 1) * PAIR].astype(F32) * gain
                ).astype(BF16)
        for j in range(columns // PAIR):
            target = (j * count + n) * PAIR
            sums_ref[1:2, target : target + PAIR] = total[0:1, j * PAIR : (j + 1) * PAIR]
    sums = jnp.dot(jnp.ones((8, folded_ref.shape[0]), BF16), folded_ref[...], preferred_element_type=F32)
    sums_ref[0:1, :] = sums[0:1]


def folded(me, order, which, gains, weights):
    rows, columns = weights[0].shape
    total = columns * len(weights)
    spaces = {2 + n: pltpu.HBM for n in range(len(weights))}
    return kernel_call(
        functools.partial(fold_kernel, order, which, len(weights)),
        [((rows, total), BF16), ((2, total), F32)],
        [me, gains, *weights],
        spaces={0: pltpu.SMEM, **spaces},
        scratch=[pltpu.VMEM((rows, columns), BF16)] * len(weights) + [pltpu.SemaphoreType.DMA((len(weights),))],
    )


def stack_kernel(*refs):
    count = (len(refs) - 2) // 2
    sources, out_ref, rows, done = refs[:count], refs[count], refs[count + 1 : -1], refs[-1]
    copies = [pltpu.make_async_copy(sources[i], rows[i], done.at[i]) for i in range(count)]
    for copy in copies:
        copy.start()
    out_ref[...] = jnp.zeros_like(out_ref)
    for i, copy in enumerate(copies):
        copy.wait()
        out_ref[i : i + 1, :] = rows[i][...].astype(F32).reshape(1, out_ref.shape[1])


def reorder_kernel(order, me_ref, source_ref, out_ref, done):
    width = source_ref.shape[1] // len(order)
    copies = []
    for k, r in enumerate(order):
        cols = pl.ds(pl.multiple_of((me_ref[0] ^ r) * width, PAIR), width)
        copies.append(
            pltpu.make_async_copy(source_ref.at[:, cols], out_ref.at[:, k * width : (k + 1) * width], done.at[k])
        )
        copies[-1].start()
    for copy in copies:
        copy.wait()


def half_kernel(place_ref, source_ref, half_ref, done):
    rows = half_ref.shape[0]
    copy = pltpu.make_async_copy(
        source_ref.at[pl.ds(pl.multiple_of(place_ref[1] * rows, rows), rows), :], half_ref, done.at[0]
    )
    copy.start()
    copy.wait()


def row_statistics(refs):
    rows, width = refs[0].shape
    full = width * len(refs)
    means, scales = [], []
    step = math.gcd(rows, 64)
    for start in range(0, rows, step):
        parts = [ref[start : start + step, :].astype(F32) for ref in refs]
        mean = sum(jnp.sum(part, axis=1, keepdims=True) for part in parts) / full
        variance = sum(jnp.sum(jnp.square(part - mean), axis=1, keepdims=True) for part in parts) / full
        means.append(mean)
        scales.append(lax.rsqrt(variance + EPSILON))
    return jnp.concatenate(means, axis=0), jnp.concatenate(scales, axis=0)


def norm_product(cells, mean, scale, folded_ref, sums_ref, start, columns):
    cols = slice(start, start + columns)
    product = jnp.dot(cells, folded_ref[:, cols], preferred_element_type=F32)
    return (product - mean * sums_ref[0:1, cols]) * scale + sums_ref[1:2, cols]


def lane_masks():
    lanes = lax.broadcasted_iota(jnp.int32, (1, PAIR), 1)
    return lanes < HEAD_DIM


def keys_values(projected):
    low = lane_masks()
    values = projected[:, PAIR : 2 * PAIR]
    return (
        projected[:, :PAIR].astype(BF16),
        jnp.where(low, values, 1.0).astype(BF16),
        jnp.where(low, 1.0, values).astype(BF16),
    )


def project_kernel(count, first, *refs):
    blocks, (folded_ref, sums_ref, *refs) = refs[:count], refs[count:]
    key_ref, value_ref = refs[-2:]
    query_ref = refs[-3] if first else None
    mean, scale = row_statistics(blocks)
    cells = jnp.concatenate([ref[...] for ref in blocks], axis=1)
    low = lane_masks()
    for j in range(key_ref.shape[1] // PAIR):
        columns = (3 if first else 2) * PAIR
        projected = norm_product(cells, mean, scale, folded_ref, sums_ref, j * 3 * PAIR, columns)
        base = 2 * j * PAIR
        (
            key_ref[:, j * PAIR : (j + 1) * PAIR],
            value_ref[:, base : base + PAIR],
            value_ref[:, base + PAIR : base + 2 * PAIR],
        ) = keys_values(projected)
        if first:
            queries = projected[:, 2 * PAIR :] * SCORE_SCALE
            query_ref[:, base : base + PAIR] = jnp.where(low, queries, 0.0).astype(BF16)
            query_ref[:, base + PAIR : base + 2 * PAIR] = jnp.where(low, 0.0, queries).astype(BF16)


def rows_of(ref, spans, cols):
    return jnp.concatenate([ref[start : start + size, cols] for start, size in spans], axis=0)


def attend_pair(pair, spans, query_ref, keys, values, state_ref):
    for head in range(2):
        index = 2 * pair + head
        queries = rows_of(query_ref, spans, slice(index * PAIR, (index + 1) * PAIR))
        scores = lax.dot_general(queries, keys, (((1,), (1,)), ((), ())), preferred_element_type=F32)
        peak = jnp.max(scores, axis=1, keepdims=True)
        soft = jnp.exp2(scores - peak).astype(BF16)
        sums = jnp.dot(soft, values[head], preferred_element_type=F32)
        state_ref[:, 2 * index * PAIR : (2 * index + 1) * PAIR] = sums
        state_ref[:, (2 * index + 1) * PAIR : (2 * index + 2) * PAIR] = jnp.broadcast_to(peak, (peak.shape[0], PAIR))


def merge_head(old_ref, part_ref, spans, index):
    sums = slice(2 * index * PAIR, (2 * index + 1) * PAIR)
    peaks = slice((2 * index + 1) * PAIR, (2 * index + 2) * PAIR)
    old_peak, part_peak = rows_of(old_ref, spans, peaks), part_ref[:, peaks]
    peak = jnp.maximum(old_peak, part_peak)
    total = rows_of(old_ref, spans, sums) * jnp.exp2(old_peak - peak) + part_ref[:, sums] * jnp.exp2(part_peak - peak)
    return total, peak


def attend_kernel(first, last, spans, query_ref, key_ref, value_ref, *refs):
    if last:
        old_ref, attended, part = refs[0], refs[-2], refs[-1]
    elif first:
        part, token_ref = refs[-2:]
    else:
        old_ref, (state_ref, token_ref, part) = refs[0], refs[-3:]
    if not last:
        token_ref[...] = jnp.zeros_like(token_ref)
    pairs = query_ref.shape[1] // (2 * PAIR)
    for j in range(pairs):
        values = [value_ref[:, n * PAIR : (n + 1) * PAIR] for n in (2 * j, 2 * j + 1)]
        attend_pair(j, spans, query_ref, key_ref[:, j * PAIR : (j + 1) * PAIR], values, part)
    if first:
        return
    low = lane_masks()
    for j in range(pairs):
        heads = [merge_head(old_ref, part, spans, 2 * j + head) for head in range(2)]
        if last:
            (one, _), (two, _) = heads
            both = jnp.where(low, one, two)
            weight = pltpu.roll(jnp.where(low, two, one), HEAD_DIM, 1)
            attended[:, j * PAIR : (j + 1) * PAIR] = (both / weight).astype(BF16)
        else:
            for head, (sums, peak) in enumerate(heads):
                at = 2 * (2 * j + head) * PAIR
                state_ref[:, at : at + PAIR] = sums
                state_ref[:, at + PAIR : at + 2 * PAIR] = peak


def middle_kernel(count, order, spans, me_ref, *refs):
    attended, frames_refs, refs = refs[:count], refs[count : 2 * count], refs[2 * count :]
    *pieces, folded_ref, sums_ref, own_ref, out_ref, near_ref, far_ref, middle = refs
    total = out_ref.shape[0]
    width = frames_refs[0].shape[1]
    cells = jnp.concatenate([ref[:, :width] for ref in attended], axis=1)
    swap = me_ref[1] != 0

    def weights(k):
        if width % PAIR:
            cols = slice(k * width, (k + 1) * width)
        else:
            cols = pl.ds(pl.multiple_of((me_ref[0] ^ order[k]) * width, PAIR), width)
        rows, index = [], 0
        while index < len(pieces):
            mine = pieces[index][:, cols]
            index += 1
            if mine.shape[0] < width:
                other = pieces[index][:, cols]
                index += 1
                mine = jnp.concatenate([jnp.where(swap, other, mine), jnp.where(swap, mine, other)], axis=0)
            rows.append(mine)
        return jnp.concatenate(rows, axis=0)

    for k in range(0, count, 2):
        both = jnp.concatenate([weights(k), weights(k + 1)], axis=1)
        share = jnp.dot(cells, both, preferred_element_type=F32)
        for n in range(2):
            cols = slice((k + n) * width, (k + n + 1) * width)
            own = jnp.concatenate([frames_refs[k + n][start : start + size, :] for start, size in spans], axis=0)
            middle[:, cols] = (own.astype(F32) + share[:, n * width : (n + 1) * width]).astype(BF16)
    own_ref[...] = middle[:, :width]
    mean, scale = row_statistics((middle,))
    cells = middle[...]
    for j in range(out_ref.shape[1] // PAIR):
        both = norm_product(cells, mean, scale, folded_ref, sums_ref, j * 2 * PAIR, 2 * PAIR)
        out_ref[:, j * PAIR : (j + 1) * PAIR] = (
            both[:, :PAIR] / (1.0 + jnp.exp(-both[:, PAIR:]))
        ).astype(BF16)
    odd = me_ref[2] != 0
    head, tail = out_ref[:HALO, :], out_ref[total - HALO :, :]
    near_ref[...] = jnp.where(odd, head, tail)
    far_ref[...] = jnp.where(odd, tail, head)


def conv_rows(padded, start, piece, cols, taps, scale, shift):
    window = padded[pl.ds(start, piece + 2 * HALO), cols]
    convolved = None
    for residue in range(8):
        part = None
        for offset in range(residue, KERNEL + 1, 8):
            if offset == 0:
                continue
            base = offset - residue
            term = taps[offset - 1] * window[base : base + piece + 8]
            part = term if part is None else part + term
        part = part[residue : residue + piece]
        convolved = part if convolved is None else convolved + part
    value = convolved * scale + shift
    return (value / (1.0 + jnp.exp(-value))).astype(BF16)


def conv_kernel(outer, first_ref, second_ref, *refs):
    if outer:
        place_ref, near_ref, far_ref, *refs = refs
        odd, near, far = place_ref[2] != 0, near_ref[...], far_ref[...]
    taps_ref, bn_ref, w_ref, keep_ref, send_ref, padded, activated = refs
    total, width = first_ref.shape
    half = keep_ref.shape[1]
    piece, quarter = 32, total // 2
    if outer:
        runs = (
            (jnp.where(odd, near, far), first_ref[:quarter, :], second_ref[:HALO, :]),
            (second_ref[total - HALO :, :], first_ref[quarter:, :], jnp.where(odd, far, near)),
        )
    else:
        runs = ((first_ref[quarter - HALO : quarter, :], second_ref[...], first_ref[quarter : quarter + HALO, :]),)
    at = 0
    for before, rows, behind in runs:
        count = rows.shape[0]
        padded[0:HALO, :] = before.astype(F32)
        padded[HALO : HALO + count, :] = rows.astype(F32)
        padded[HALO + count : 2 * HALO + count, :] = behind.astype(F32)
        for col in range(0, width, PAIR):
            cols = slice(col, col + PAIR)
            taps = [taps_ref[j : j + 1, cols] for j in range(KERNEL)]
            scale, shift = bn_ref[0:1, cols], bn_ref[1:2, cols]

            def block(index, carry, at=at):
                start = pl.multiple_of(index * piece, piece)
                target = pl.multiple_of(at + index * piece, piece)
                activated[pl.ds(target, piece), cols] = conv_rows(padded, start, piece, cols, taps, scale, shift)
                return carry

            lax.fori_loop(0, count // piece, block, 0, unroll=4)
        at += count
    share = activated[...]
    send_ref[...] = jnp.dot(share, w_ref[:, half:], preferred_element_type=F32).astype(BF16)
    keep_ref[...] = jnp.dot(share, w_ref[:, :half], preferred_element_type=F32).astype(BF16)


def pad_columns(weight, width):
    if weight.shape[1] == width:
        return weight
    return jnp.pad(weight, ((0, 0), (0, width - weight.shape[1])))


def on_device(
    frames_in,
    norm1_gain,
    norm1_bias,
    w_query,
    w_key,
    w_value,
    w_out,
    norm2_gain,
    norm2_bias,
    w_glu_value,
    w_glu_gate,
    depth_kernel,
    bn_scale,
    bn_shift,
    w_proj,
):
    frames, width = frames_in.shape
    grid, ctx = lax.axis_size("grid"), lax.axis_size("ctx")
    me = lax.axis_index("grid")
    place = jnp.stack([me, lax.axis_index("parts"), lax.axis_index("ctx") % 2]).astype(jnp.int32)
    order = list(range(0, grid, CORES)) + list(range(1, grid, CORES))
    padded = -(-width // PAIR) * PAIR
    every = ((0, frames),)

    def by_distance(cells):
        return jnp.concatenate(
            [lax.dynamic_slice_in_dim(cells, (me ^ r) * width, width, 1) for r in order], axis=1
        )

    def over_chips(block):
        return [exchange(block, "grid", CORES * a) for a in range(1, grid // CORES)]

    def other_core(blocks):
        return [exchange(block, "grid", 1) for block in blocks]

    vectors = [norm1_gain, norm1_bias, norm2_gain, norm2_bias]
    (gains,) = kernel_call(
        stack_kernel,
        [((8, width), F32)],
        vectors,
        spaces={i: pltpu.HBM for i in range(len(vectors))},
        scratch=[pltpu.VMEM((width,), BF16)] * len(vectors) + [pltpu.SemaphoreType.DMA((len(vectors),))],
    )
    gains = lax.all_gather(gains, "grid", axis=0, tiled=True)
    raw = {0: frames_in}
    chips = {0: over_chips(frames_in)}
    for k in reversed(range(ctx.bit_length() - 1)):
        raw[1 << k] = exchange(frames_in, "ctx", 1 << k)

    w_query, w_key, w_value, w_glu_value, w_glu_gate = (
        pad_columns(weight, padded) for weight in (w_query, w_key, w_value, w_glu_value, w_glu_gate)
    )
    if width % PAIR:
        row_pad = ((0, padded - width), (0, 0))
        w_p = jnp.pad(by_distance(w_proj), row_pad)
    else:
        (w_p,) = kernel_call(
            functools.partial(reorder_kernel, order),
            [(w_proj.shape, BF16)],
            [place, w_proj],
            spaces={0: pltpu.SMEM, 1: pltpu.HBM},
            scratch=[pltpu.SemaphoreType.DMA((grid,))],
        )
    taps = pad_columns(depth_kernel, padded)
    bn = pad_columns(jnp.stack([bn_scale, bn_shift]), padded)
    qkv, qkv_sums = folded(place, order, 0, gains, (w_key, w_value, w_query))
    chips[0] = [after(block, qkv_sums) for block in chips[0]]
    glu, glu_sums = folded(place, order, 2, gains, (w_glu_value, w_glu_gate))

    parts = lax.axis_size("parts")
    if parts == 2:
        (half,) = kernel_call(
            half_kernel,
            [((width // 2, w_out.shape[1]), BF16)],
            [place, w_out],
            spaces={0: pltpu.SMEM, 1: pltpu.HBM},
            scratch=[pltpu.SemaphoreType.DMA((1,))],
        )
    else:
        half = w_out
    crossed = over_chips(after(half, *chips[0]))
    state_shape = ((frames, 4 * padded), F32)
    token_shape = ((8, 128), F32)
    wide, narrow = ((frames, 2 * padded), BF16), ((frames, padded), BF16)
    chips[1] = [exchange(block, "ctx", 1) for block in chips[0]]
    own = [frames_in] + chips[0]
    own_blocks = own + other_core(own)
    n = len(own_blocks)
    early = [*[raw[s] for s in raw if s], glu_sums, w_p]
    queries, keys, values = kernel_call(
        functools.partial(project_kernel, n, True),
        [wide, narrow, wide],
        [*own_blocks, qkv, qkv_sums, *early],
        spaces={n + 2 + i: pl.ANY for i in range(len(early))},
    )
    def prepare(s, done):
        if 2 <= s < ctx:
            low = s & -s
            if s != low:
                raw[s] = after(exchange(raw[s ^ low], "ctx", low), done)
            chips[s] = over_chips(raw[s])

    prepare(2, None)
    state, token = kernel_call(
        functools.partial(attend_kernel, True, False, every),
        [state_shape, token_shape],
        [queries, keys, values, *crossed],
        spaces={3 + i: pl.ANY for i in range(len(crossed))},
    )
    crossed = [after(block, token) for block in crossed]
    swapped = [exchange(block, "parts", 1) for block in crossed] if parts == 2 else []
    moved = {1: [after(block, token) for block in chips[1]]}
    for s in range(1, ctx):
        last = s == ctx - 1
        mine = [raw[s]] + moved[s]
        keys, values = kernel_call(
            functools.partial(project_kernel, n, False),
            [narrow, wide],
            [*mine, *other_core(mine), qkv, qkv_sums],
        )
        if last:
            break
        prepare(s + 2, token)
        moved[s + 1] = [after(block, token) for block in chips[s + 1]]
        behind = [raw[s + 2]] if s + 2 < ctx else []
        behind += moved[s + 1]
        state, token = kernel_call(
            functools.partial(attend_kernel, False, False, every),
            [state_shape, token_shape],
            [queries, keys, values, state, *behind],
            spaces={4 + i: pl.ANY for i in range(len(behind))},
            aliases={3: 0},
            scratch=[pltpu.VMEM(*state_shape)],
        )
    rows, quarter = frames // 2, frames // 4
    spans = (((0, quarter), (3 * quarter, quarter)), ((quarter, rows),))
    attended = []
    for h in range(2):
        (mine,) = kernel_call(
            functools.partial(attend_kernel, False, True, spans[h]),
            [((rows, padded), BF16)],
            [queries, keys, values, state],
            scratch=[pltpu.VMEM((rows, 4 * padded), F32)],
        )
        attended.append([mine] + over_chips(mine))
    swapped = [after(block, attended[0][0]) for block in swapped]
    pieces = [w_out]
    for a, block in enumerate(crossed):
        pieces += [block, swapped[a]] if swapped else [block]
    pieces = pieces + other_core(pieces)
    if width % PAIR:
        pieces = [by_distance(piece) for piece in pieces]
    middle, gated = [], []
    for h in range(2):
        mine = attended[h]
        done = gated[0] if h else attended[1][0]
        mine = mine[:1] + [after(block, done) for block in mine[1:]]
        results = kernel_call(
            functools.partial(middle_kernel, n, order, spans[h]),
            [((rows, width), BF16), ((rows, padded), BF16), ((HALO, padded), BF16), ((HALO, padded), BF16)],
            [place, *mine, *other_core(mine), *own_blocks, *pieces, glu, glu_sums],
            spaces={0: pltpu.SMEM},
            scratch=[pltpu.VMEM((rows, grid * width), BF16)],
        )
        middle.append(results[0])
        gated.append(results[1])
        if h == 0:
            near = exchange(results[2], "ctx", 1)
            between = [(i, i + 1) for i in range(1, ctx - 1, 2)]
            far = lax.ppermute(results[3], "ctx", between + [(b, a) for a, b in between])
    outs = [None, None]
    for h, around in ((1, []), (0, [place, near, far])):
        keep, send = kernel_call(
            functools.partial(conv_kernel, h == 0),
            [((rows, grid // CORES * width), BF16)] * 2,
            [*gated, *around, taps, bn, w_p],
            spaces={} if h else {2: pltpu.SMEM},
            scratch=[pltpu.VMEM((rows + 2 * HALO, padded), F32), pltpu.VMEM((rows, padded), BF16)],
        )
        theirs = exchange(send, "grid", 1)

        def pair_sum(a):
            cols = slice(a * width, (a + 1) * width)
            return keep[:, cols].astype(F32) + theirs[:, cols].astype(F32)

        result = middle[h].astype(F32) + pair_sum(0)
        for a in range(1, grid // CORES):
            result = result + exchange(pair_sum(a).astype(BF16), "grid", CORES * a).astype(F32)
        outs[h] = result.astype(BF16)
    return jnp.concatenate([outs[0][:quarter], outs[1], outs[0][quarter:]], axis=0)


def solution(mesh):
    return jax.shard_map(
        on_device,
        mesh=mesh,
        in_specs=(
            P(("parts", "ctx"), "grid"),
            P("grid"),
            P("grid"),
            P(None, "grid"),
            P(None, "grid"),
            P(None, "grid"),
            P("grid", None),
            P("grid"),
            P("grid"),
            P(None, "grid"),
            P(None, "grid"),
            P(None, "grid"),
            P("grid"),
            P("grid"),
            P("grid", None),
        ),
        out_specs=P(("parts", "ctx"), "grid"),
        check_vma=False,
    )
```

```python
import functools
import math

import jax
import jax.numpy as jnp
from jax import lax
from jax.experimental import pallas as pl
from jax.experimental.pallas import tpu as pltpu
from jax.sharding import PartitionSpec as P

HEAD_DIM = 64
PAIR = 2 * HEAD_DIM
KERNEL = 31
HALF = 15
HALO = 16
EPSILON = 1e-05
CORES = 2
VMEM_BYTES = 16 * 1024 * 1024
BF16 = jnp.bfloat16
F32 = jnp.float32
SCORE_SCALE = math.log2(math.e) / math.sqrt(HEAD_DIM)


def exchange(cells, axis, distance):
    count = lax.axis_size(axis)
    return lax.ppermute(cells, axis, [(i, i ^ distance) for i in range(count)])


def kernel_call(body, outs, operands, spaces=None, scratch=(), aliases=None):
    spaces = spaces or {}
    operands = [
        pltpu.with_memory_space_constraint(cells, pltpu.HBM) if spaces.get(i) == pltpu.HBM else cells
        for i, cells in enumerate(operands)
    ]
    in_specs = [
        pl.BlockSpec(memory_space=spaces.get(i, pltpu.VMEM)) for i in range(len(operands))
    ]
    return pl.pallas_call(
        body,
        in_specs=in_specs,
        out_specs=tuple(pl.BlockSpec(memory_space=pltpu.VMEM) for _ in outs),
        out_shape=tuple(jax.ShapeDtypeStruct(shape, dtype) for shape, dtype in outs),
        scratch_shapes=list(scratch),
        input_output_aliases=aliases or {},
        compiler_params=pltpu.CompilerParams(vmem_limit_bytes=VMEM_BYTES),
        cost_estimate=pl.CostEstimate(flops=1000, bytes_accessed=1000, transcendentals=0),
    )(*operands)


def after(cells, *done):
    def body(*refs):
        pass

    anywhere = pl.BlockSpec(memory_space=pl.ANY)
    return pl.pallas_call(
        body,
        in_specs=[anywhere] * (1 + len(done)),
        out_specs=anywhere,
        out_shape=jax.ShapeDtypeStruct(cells.shape, cells.dtype),
        input_output_aliases={0: 0},
        compiler_params=pltpu.CompilerParams(vmem_limit_bytes=64 * 1024),
        cost_estimate=pl.CostEstimate(flops=0, bytes_accessed=0, transcendentals=0),
    )(cells, *done)


def fold_kernel(order, which, count, me_ref, gains_ref, *refs):
    sources, (folded_ref, sums_ref), weights, done = refs[:count], refs[count : count + 2], refs[count + 2 : -1], refs[-1]
    copies = [pltpu.make_async_copy(sources[n], weights[n], done.at[n]) for n in range(count)]
    for copy in copies:
        copy.start()
    width = gains_ref.shape[1]
    columns = weights[0].shape[1]
    factors = []
    for r in order:
        gains = gains_ref[pl.ds(pl.multiple_of((me_ref[0] ^ r) * 8, 8), 8), :]
        gain = jnp.transpose(jnp.broadcast_to(gains[which : which + 1, :], (PAIR, width)))
        bias = jnp.broadcast_to(gains[which + 1 : which + 2, :], (8, width)).astype(BF16)
        factors.append((gain, bias))
    for n, ref in enumerate(weights):
        copies[n].wait()
        total = jnp.zeros((8, columns), F32)
        for k, r in enumerate(order):
            gain, bias = factors[k]
            start = pl.multiple_of((me_ref[0] ^ r) * width, width)
            block = ref[pl.ds(start, width), :]
            total = total + jnp.dot(bias, block, preferred_element_type=F32)
            for j in range(columns // PAIR):
                target = (j * count + n) * PAIR
                folded_ref[k * width : (k + 1) * width, target : target + PAIR] = (
                    block[:, j * PAIR : (j + 1) * PAIR].astype(F32) * gain
                ).astype(BF16)
        for j in range(columns // PAIR):
            target = (j * count + n) * PAIR
            sums_ref[1:2, target : target + PAIR] = total[0:1, j * PAIR : (j + 1) * PAIR]
    sums = jnp.dot(jnp.ones((8, folded_ref.shape[0]), BF16), folded_ref[...], preferred_element_type=F32)
    sums_ref[0:1, :] = sums[0:1]


def folded(me, order, which, gains, weights):
    rows, columns = weights[0].shape
    total = columns * len(weights)
    spaces = {2 + n: pltpu.HBM for n in range(len(weights))}
    return kernel_call(
        functools.partial(fold_kernel, order, which, len(weights)),
        [((rows, total), BF16), ((2, total), F32)],
        [me, gains, *weights],
        spaces={0: pltpu.SMEM, **spaces},
        scratch=[pltpu.VMEM((rows, columns), BF16)] * len(weights) + [pltpu.SemaphoreType.DMA((len(weights),))],
    )


def stack_kernel(*refs):
    count = (len(refs) - 2) // 2
    sources, out_ref, rows, done = refs[:count], refs[count], refs[count + 1 : -1], refs[-1]
    copies = [pltpu.make_async_copy(sources[i], rows[i], done.at[i]) for i in range(count)]
    for copy in copies:
        copy.start()
    out_ref[...] = jnp.zeros_like(out_ref)
    for i, copy in enumerate(copies):
        copy.wait()
        out_ref[i : i + 1, :] = rows[i][...].astype(F32).reshape(1, out_ref.shape[1])


def reorder_kernel(order, me_ref, source_ref, out_ref, done):
    width = source_ref.shape[1] // len(order)
    copies = []
    for k, r in enumerate(order):
        cols = pl.ds(pl.multiple_of((me_ref[0] ^ r) * width, PAIR), width)
        copies.append(
            pltpu.make_async_copy(source_ref.at[:, cols], out_ref.at[:, k * width : (k + 1) * width], done.at[k])
        )
        copies[-1].start()
    for copy in copies:
        copy.wait()


def half_kernel(part_ref, source_ref, _, half_ref, done):
    rows = half_ref.shape[0]
    copy = pltpu.make_async_copy(
        source_ref.at[pl.ds(pl.multiple_of(part_ref[0] * rows, rows), rows), :], half_ref, done.at[0]
    )
    copy.start()
    copy.wait()


def row_statistics(refs):
    rows, width = refs[0].shape
    full = width * len(refs)
    means, scales = [], []
    step = math.gcd(rows, 64)
    for start in range(0, rows, step):
        parts = [ref[start : start + step, :].astype(F32) for ref in refs]
        mean = sum(jnp.sum(part, axis=1, keepdims=True) for part in parts) / full
        variance = sum(jnp.sum(jnp.square(part - mean), axis=1, keepdims=True) for part in parts) / full
        means.append(mean)
        scales.append(lax.rsqrt(variance + EPSILON))
    return jnp.concatenate(means, axis=0), jnp.concatenate(scales, axis=0)


def norm_product(cells, mean, scale, folded_ref, sums_ref, start, columns):
    cols = slice(start, start + columns)
    product = jnp.dot(cells, folded_ref[:, cols], preferred_element_type=F32)
    return (product - mean * sums_ref[0:1, cols]) * scale + sums_ref[1:2, cols]


def lane_masks():
    lanes = lax.broadcasted_iota(jnp.int32, (1, PAIR), 1)
    return lanes < HEAD_DIM


def keys_values(projected):
    low = lane_masks()
    values = projected[:, PAIR : 2 * PAIR]
    return (
        projected[:, :PAIR].astype(BF16),
        jnp.where(low, values, 1.0).astype(BF16),
        jnp.where(low, 1.0, values).astype(BF16),
    )


def project_kernel(count, first, *refs):
    blocks, (folded_ref, sums_ref, *refs) = refs[:count], refs[count:]
    key_ref, value_ref = refs[-2:]
    query_ref = refs[-3] if first else None
    mean, scale = row_statistics(blocks)
    cells = jnp.concatenate([ref[...] for ref in blocks], axis=1)
    low = lane_masks()
    for j in range(key_ref.shape[1] // PAIR):
        columns = (3 if first else 2) * PAIR
        projected = norm_product(cells, mean, scale, folded_ref, sums_ref, j * 3 * PAIR, columns)
        base = 2 * j * PAIR
        (
            key_ref[:, j * PAIR : (j + 1) * PAIR],
            value_ref[:, base : base + PAIR],
            value_ref[:, base + PAIR : base + 2 * PAIR],
        ) = keys_values(projected)
        if first:
            queries = projected[:, 2 * PAIR :] * SCORE_SCALE
            query_ref[:, base : base + PAIR] = jnp.where(low, queries, 0.0).astype(BF16)
            query_ref[:, base + PAIR : base + 2 * PAIR] = jnp.where(low, 0.0, queries).astype(BF16)


def rows_of(ref, spans, cols):
    return jnp.concatenate([ref[start : start + size, cols] for start, size in spans], axis=0)


def attend_pair(pair, spans, query_ref, keys, values, state_ref):
    for head in range(2):
        index = 2 * pair + head
        queries = rows_of(query_ref, spans, slice(index * PAIR, (index + 1) * PAIR))
        scores = lax.dot_general(queries, keys, (((1,), (1,)), ((), ())), preferred_element_type=F32)
        peak = jnp.max(scores, axis=1, keepdims=True)
        soft = jnp.exp2(scores - peak).astype(BF16)
        sums = jnp.dot(soft, values[head], preferred_element_type=F32)
        state_ref[:, 2 * index * PAIR : (2 * index + 1) * PAIR] = sums
        state_ref[:, (2 * index + 1) * PAIR : (2 * index + 2) * PAIR] = jnp.broadcast_to(peak, (peak.shape[0], PAIR))


def merge_head(old_ref, part_ref, spans, index):
    sums = slice(2 * index * PAIR, (2 * index + 1) * PAIR)
    peaks = slice((2 * index + 1) * PAIR, (2 * index + 2) * PAIR)
    old_peak, part_peak = rows_of(old_ref, spans, peaks), part_ref[:, peaks]
    peak = jnp.maximum(old_peak, part_peak)
    total = rows_of(old_ref, spans, sums) * jnp.exp2(old_peak - peak) + part_ref[:, sums] * jnp.exp2(part_peak - peak)
    return total, peak


def attend_kernel(first, last, spans, query_ref, key_ref, value_ref, *refs):
    if last:
        old_ref, attended, part = refs[0], refs[-2], refs[-1]
    elif first:
        part, token_ref = refs[-2:]
    else:
        old_ref, (state_ref, token_ref, part) = refs[0], refs[-3:]
    if not last:
        token_ref[...] = jnp.zeros_like(token_ref)
    pairs = query_ref.shape[1] // (2 * PAIR)
    for j in range(pairs):
        values = [value_ref[:, n * PAIR : (n + 1) * PAIR] for n in (2 * j, 2 * j + 1)]
        attend_pair(j, spans, query_ref, key_ref[:, j * PAIR : (j + 1) * PAIR], values, part)
    if first:
        return
    low = lane_masks()
    for j in range(pairs):
        heads = [merge_head(old_ref, part, spans, 2 * j + head) for head in range(2)]
        if last:
            (one, _), (two, _) = heads
            both = jnp.where(low, one, two)
            weight = pltpu.roll(jnp.where(low, two, one), HEAD_DIM, 1)
            attended[:, j * PAIR : (j + 1) * PAIR] = (both / weight).astype(BF16)
        else:
            for head, (sums, peak) in enumerate(heads):
                at = 2 * (2 * j + head) * PAIR
                state_ref[:, at : at + PAIR] = sums
                state_ref[:, at + PAIR : at + 2 * PAIR] = peak


def middle_kernel(count, order, spans, me_ref, part_ref, odd_ref, *refs):
    attended, frames_refs, refs = refs[:count], refs[count : 2 * count], refs[2 * count :]
    *pieces, folded_ref, sums_ref, own_ref, out_ref, near_ref, far_ref, middle = refs
    total = out_ref.shape[0]
    width = frames_refs[0].shape[1]
    cells = jnp.concatenate([ref[:, :width] for ref in attended], axis=1)
    swap = part_ref[0] != 0

    def weights(k):
        if width % PAIR:
            cols = slice(k * width, (k + 1) * width)
        else:
            cols = pl.ds(pl.multiple_of((me_ref[0] ^ order[k]) * width, PAIR), width)
        rows, index = [], 0
        while index < len(pieces):
            mine = pieces[index][:, cols]
            index += 1
            if mine.shape[0] < width:
                other = pieces[index][:, cols]
                index += 1
                mine = jnp.concatenate([jnp.where(swap, other, mine), jnp.where(swap, mine, other)], axis=0)
            rows.append(mine)
        return jnp.concatenate(rows, axis=0)

    for k in range(0, count, 2):
        both = jnp.concatenate([weights(k), weights(k + 1)], axis=1)
        share = jnp.dot(cells, both, preferred_element_type=F32)
        for n in range(2):
            cols = slice((k + n) * width, (k + n + 1) * width)
            own = jnp.concatenate([frames_refs[k + n][start : start + size, :] for start, size in spans], axis=0)
            middle[:, cols] = (own.astype(F32) + share[:, n * width : (n + 1) * width]).astype(BF16)
    own_ref[...] = middle[:, :width]
    mean, scale = row_statistics((middle,))
    cells = middle[...]
    for j in range(out_ref.shape[1] // PAIR):
        both = norm_product(cells, mean, scale, folded_ref, sums_ref, j * 2 * PAIR, 2 * PAIR)
        out_ref[:, j * PAIR : (j + 1) * PAIR] = (
            both[:, :PAIR] / (1.0 + jnp.exp(-both[:, PAIR:]))
        ).astype(BF16)
    odd = odd_ref[0] != 0
    head, tail = out_ref[:HALO, :], out_ref[total - HALO :, :]
    near_ref[...] = jnp.where(odd, head, tail)
    far_ref[...] = jnp.where(odd, tail, head)


def conv_rows(padded, start, piece, cols, taps, scale, shift):
    window = padded[pl.ds(start, piece + 2 * HALO), cols]
    convolved = None
    for residue in range(8):
        part = None
        for offset in range(residue, KERNEL + 1, 8):
            if offset == 0:
                continue
            base = offset - residue
            term = taps[offset - 1] * window[base : base + piece + 8]
            part = term if part is None else part + term
        part = part[residue : residue + piece]
        convolved = part if convolved is None else convolved + part
    value = convolved * scale + shift
    return (value / (1.0 + jnp.exp(-value))).astype(BF16)


def conv_kernel(outer, first_ref, second_ref, *refs):
    if outer:
        odd_ref, near_ref, far_ref, *refs = refs
        odd, near, far = odd_ref[0] != 0, near_ref[...], far_ref[...]
    taps_ref, bn_ref, w_ref, keep_ref, send_ref, padded, activated = refs
    total, width = first_ref.shape
    half = keep_ref.shape[1]
    piece, quarter = 32, total // 2
    if outer:
        runs = (
            (jnp.where(odd, near, far), first_ref[:quarter, :], second_ref[:HALO, :]),
            (second_ref[total - HALO :, :], first_ref[quarter:, :], jnp.where(odd, far, near)),
        )
    else:
        runs = ((first_ref[quarter - HALO : quarter, :], second_ref[...], first_ref[quarter : quarter + HALO, :]),)
    at = 0
    for before, rows, behind in runs:
        count = rows.shape[0]
        padded[0:HALO, :] = before.astype(F32)
        padded[HALO : HALO + count, :] = rows.astype(F32)
        padded[HALO + count : 2 * HALO + count, :] = behind.astype(F32)
        for col in range(0, width, PAIR):
            cols = slice(col, col + PAIR)
            taps = [taps_ref[j : j + 1, cols] for j in range(KERNEL)]
            scale, shift = bn_ref[0:1, cols], bn_ref[1:2, cols]

            def block(index, carry, at=at):
                start = pl.multiple_of(index * piece, piece)
                target = pl.multiple_of(at + index * piece, piece)
                activated[pl.ds(target, piece), cols] = conv_rows(padded, start, piece, cols, taps, scale, shift)
                return carry

            lax.fori_loop(0, count // piece, block, 0, unroll=4)
        at += count
    share = activated[...]
    send_ref[...] = jnp.dot(share, w_ref[:, half:], preferred_element_type=F32).astype(BF16)
    keep_ref[...] = jnp.dot(share, w_ref[:, :half], preferred_element_type=F32).astype(BF16)


def pad_columns(weight, width):
    if weight.shape[1] == width:
        return weight
    return jnp.pad(weight, ((0, 0), (0, width - weight.shape[1])))


def on_device(
    frames_in,
    norm1_gain,
    norm1_bias,
    w_query,
    w_key,
    w_value,
    w_out,
    norm2_gain,
    norm2_bias,
    w_glu_value,
    w_glu_gate,
    depth_kernel,
    bn_scale,
    bn_shift,
    w_proj,
):
    frames, width = frames_in.shape
    grid, ctx = lax.axis_size("grid"), lax.axis_size("ctx")
    me = lax.axis_index("grid")
    place = me.astype(jnp.int32).reshape(1)
    odd = (lax.axis_index("ctx") & 1).astype(jnp.int32).reshape(1)
    order = list(range(0, grid, CORES)) + list(range(1, grid, CORES))
    padded = -(-width // PAIR) * PAIR
    every = ((0, frames),)

    def by_distance(cells):
        return jnp.concatenate(
            [lax.dynamic_slice_in_dim(cells, (me ^ r) * width, width, 1) for r in order], axis=1
        )

    def over_chips(block):
        return [exchange(block, "grid", CORES * a) for a in range(1, grid // CORES)]

    def other_core(blocks):
        return [exchange(block, "grid", 1) for block in blocks]

    vectors = [norm1_gain, norm1_bias, norm2_gain, norm2_bias]
    (gains,) = kernel_call(
        stack_kernel,
        [((8, width), F32)],
        vectors,
        spaces={i: pltpu.HBM for i in range(len(vectors))},
        scratch=[pltpu.VMEM((width,), BF16)] * len(vectors) + [pltpu.SemaphoreType.DMA((len(vectors),))],
    )
    gains = lax.all_gather(gains, "grid", axis=0, tiled=True)
    raw = {0: frames_in}
    chips = {0: over_chips(frames_in)}
    for k in reversed(range(ctx.bit_length() - 1)):
        raw[1 << k] = exchange(frames_in, "ctx", 1 << k)

    w_query, w_key, w_value, w_glu_value, w_glu_gate = (
        pad_columns(weight, padded) for weight in (w_query, w_key, w_value, w_glu_value, w_glu_gate)
    )
    if width % PAIR:
        row_pad = ((0, padded - width), (0, 0))
        w_p = jnp.pad(by_distance(w_proj), row_pad)
    else:
        (w_p,) = kernel_call(
            functools.partial(reorder_kernel, order),
            [(w_proj.shape, BF16)],
            [place, w_proj],
            spaces={0: pltpu.SMEM, 1: pltpu.HBM},
            scratch=[pltpu.SemaphoreType.DMA((grid,))],
        )
    taps = pad_columns(depth_kernel, padded)
    bn = pad_columns(jnp.stack([bn_scale, bn_shift]), padded)
    qkv, qkv_sums = folded(place, order, 0, gains, (w_key, w_value, w_query))
    chips[0] = [after(block, qkv_sums) for block in chips[0]]
    glu, glu_sums = folded(place, order, 2, gains, (w_glu_value, w_glu_gate))

    parts = lax.axis_size("parts")
    part = lax.axis_index("parts").astype(jnp.int32).reshape(1)
    if parts == 2:
        (half,) = kernel_call(
            half_kernel,
            [((width // 2, w_out.shape[1]), BF16)],
            [part, w_out, odd],
            spaces={0: pltpu.SMEM, 1: pltpu.HBM, 2: pltpu.SMEM},
            scratch=[pltpu.SemaphoreType.DMA((1,))],
        )
    else:
        half = w_out
    crossed = over_chips(after(half, *chips[0]))
    state_shape = ((frames, 4 * padded), F32)
    token_shape = ((8, 128), F32)
    wide, narrow = ((frames, 2 * padded), BF16), ((frames, padded), BF16)
    chips[1] = [exchange(block, "ctx", 1) for block in chips[0]]
    own = [frames_in] + chips[0]
    own_blocks = own + other_core(own)
    n = len(own_blocks)
    early = [*[raw[s] for s in raw if s], glu_sums, w_p]
    queries, keys, values = kernel_call(
        functools.partial(project_kernel, n, True),
        [wide, narrow, wide],
        [*own_blocks, qkv, qkv_sums, *early],
        spaces={n + 2 + i: pl.ANY for i in range(len(early))},
    )
    def prepare(s, done):
        if 2 <= s < ctx:
            low = s & -s
            if s != low:
                raw[s] = after(exchange(raw[s ^ low], "ctx", low), done)
            chips[s] = over_chips(raw[s])

    prepare(2, None)
    state, token = kernel_call(
        functools.partial(attend_kernel, True, False, every),
        [state_shape, token_shape],
        [queries, keys, values, *crossed],
        spaces={3 + i: pl.ANY for i in range(len(crossed))},
    )
    crossed = [after(block, token) for block in crossed]
    swapped = [exchange(block, "parts", 1) for block in crossed] if parts == 2 else []
    moved = {1: [after(block, token) for block in chips[1]]}
    for s in range(1, ctx):
        last = s == ctx - 1
        mine = [raw[s]] + moved[s]
        keys, values = kernel_call(
            functools.partial(project_kernel, n, False),
            [narrow, wide],
            [*mine, *other_core(mine), qkv, qkv_sums],
        )
        if last:
            break
        prepare(s + 2, token)
        moved[s + 1] = [after(block, token) for block in chips[s + 1]]
        behind = [raw[s + 2]] if s + 2 < ctx else []
        behind += moved[s + 1]
        state, token = kernel_call(
            functools.partial(attend_kernel, False, False, every),
            [state_shape, token_shape],
            [queries, keys, values, state, *behind],
            spaces={4 + i: pl.ANY for i in range(len(behind))},
            aliases={3: 0},
            scratch=[pltpu.VMEM(*state_shape)],
        )
    rows, quarter = frames // 2, frames // 4
    spans = (((0, quarter), (3 * quarter, quarter)), ((quarter, rows),))
    attended = []
    for h in range(2):
        (mine,) = kernel_call(
            functools.partial(attend_kernel, False, True, spans[h]),
            [((rows, padded), BF16)],
            [queries, keys, values, state],
            scratch=[pltpu.VMEM((rows, 4 * padded), F32)],
        )
        attended.append([mine] + over_chips(mine))
    swapped = [after(block, attended[0][0]) for block in swapped]
    pieces = [w_out]
    for a, block in enumerate(crossed):
        pieces += [block, swapped[a]] if swapped else [block]
    pieces = pieces + other_core(pieces)
    if width % PAIR:
        pieces = [by_distance(piece) for piece in pieces]
    middle, gated = [], []
    for h in range(2):
        mine = attended[h]
        done = gated[0] if h else attended[1][0]
        mine = mine[:1] + [after(block, done) for block in mine[1:]]
        results = kernel_call(
            functools.partial(middle_kernel, n, order, spans[h]),
            [((rows, width), BF16), ((rows, padded), BF16), ((HALO, padded), BF16), ((HALO, padded), BF16)],
            [place, part, odd, *mine, *other_core(mine), *own_blocks, *pieces, glu, glu_sums],
            spaces={0: pltpu.SMEM, 1: pltpu.SMEM, 2: pltpu.SMEM},
            scratch=[pltpu.VMEM((rows, grid * width), BF16)],
        )
        middle.append(results[0])
        gated.append(results[1])
        if h == 0:
            near = exchange(results[2], "ctx", 1)
            between = [(i, i + 1) for i in range(1, ctx - 1, 2)]
            far = lax.ppermute(results[3], "ctx", between + [(b, a) for a, b in between])
    outs = [None, None]
    for h, around in ((1, []), (0, [odd, near, far])):
        keep, send = kernel_call(
            functools.partial(conv_kernel, h == 0),
            [((rows, grid // CORES * width), BF16)] * 2,
            [*gated, *around, taps, bn, w_p],
            spaces={} if h else {2: pltpu.SMEM},
            scratch=[pltpu.VMEM((rows + 2 * HALO, padded), F32), pltpu.VMEM((rows, padded), BF16)],
        )
        theirs = exchange(send, "grid", 1)

        def pair_sum(a):
            cols = slice(a * width, (a + 1) * width)
            return keep[:, cols].astype(F32) + theirs[:, cols].astype(F32)

        result = middle[h].astype(F32) + pair_sum(0)
        for a in range(1, grid // CORES):
            result = result + exchange(pair_sum(a).astype(BF16), "grid", CORES * a).astype(F32)
        outs[h] = result.astype(BF16)
    return jnp.concatenate([outs[0][:quarter], outs[1], outs[0][quarter:]], axis=0)


def solution(mesh):
    return jax.shard_map(
        on_device,
        mesh=mesh,
        in_specs=(
            P(("parts", "ctx"), "grid"),
            P("grid"),
            P("grid"),
            P(None, "grid"),
            P(None, "grid"),
            P(None, "grid"),
            P("grid", None),
            P("grid"),
            P("grid"),
            P(None, "grid"),
            P(None, "grid"),
            P(None, "grid"),
            P("grid"),
            P("grid"),
            P("grid", None),
        ),
        out_specs=P(("parts", "ctx"), "grid"),
        check_vma=False,
    )
```

```python
import functools
import math

import jax
import jax.numpy as jnp
from jax import lax
from jax.experimental import pallas as pl
from jax.experimental.pallas import tpu as pltpu
from jax.sharding import PartitionSpec as P

HEAD_DIM = 64
PAIR = 2 * HEAD_DIM
KERNEL = 31
HALF = 15
HALO = 16
EPSILON = 1e-05
CORES = 2
VMEM_BYTES = 16 * 1024 * 1024
BF16 = jnp.bfloat16
F32 = jnp.float32
SCORE_SCALE = math.log2(math.e) / math.sqrt(HEAD_DIM)


def exchange(cells, axis, distance):
    count = lax.axis_size(axis)
    return lax.ppermute(cells, axis, [(i, i ^ distance) for i in range(count)])


def kernel_call(body, outs, operands, spaces=None, scratch=(), aliases=None):
    spaces = spaces or {}
    operands = [
        pltpu.with_memory_space_constraint(cells, pltpu.HBM) if spaces.get(i) == pltpu.HBM else cells
        for i, cells in enumerate(operands)
    ]
    in_specs = [
        pl.BlockSpec(memory_space=spaces.get(i, pltpu.VMEM)) for i in range(len(operands))
    ]
    return pl.pallas_call(
        body,
        in_specs=in_specs,
        out_specs=tuple(pl.BlockSpec(memory_space=pltpu.VMEM) for _ in outs),
        out_shape=tuple(jax.ShapeDtypeStruct(shape, dtype) for shape, dtype in outs),
        scratch_shapes=list(scratch),
        input_output_aliases=aliases or {},
        compiler_params=pltpu.CompilerParams(vmem_limit_bytes=VMEM_BYTES),
        cost_estimate=pl.CostEstimate(flops=1000, bytes_accessed=1000, transcendentals=0),
    )(*operands)


def after(cells, *done):
    def body(*refs):
        pass

    anywhere = pl.BlockSpec(memory_space=pl.ANY)
    return pl.pallas_call(
        body,
        in_specs=[anywhere] * (1 + len(done)),
        out_specs=anywhere,
        out_shape=jax.ShapeDtypeStruct(cells.shape, cells.dtype),
        input_output_aliases={0: 0},
        compiler_params=pltpu.CompilerParams(vmem_limit_bytes=64 * 1024),
        cost_estimate=pl.CostEstimate(flops=0, bytes_accessed=0, transcendentals=0),
    )(cells, *done)


def fold_kernel(order, which, count, me_ref, gains_ref, *refs):
    sources, (folded_ref, sums_ref), weights, done = refs[:count], refs[count : count + 2], refs[count + 2 : -1], refs[-1]
    copies = [pltpu.make_async_copy(sources[n], weights[n], done.at[n]) for n in range(count)]
    for copy in copies:
        copy.start()
    width = gains_ref.shape[1]
    columns = weights[0].shape[1]
    factors = []
    for r in order:
        gains = gains_ref[pl.ds(pl.multiple_of((me_ref[0] ^ r) * 8, 8), 8), :]
        gain = jnp.transpose(jnp.broadcast_to(gains[which : which + 1, :], (PAIR, width)))
        bias = jnp.broadcast_to(gains[which + 1 : which + 2, :], (8, width)).astype(BF16)
        factors.append((gain, bias))
    for n, ref in enumerate(weights):
        copies[n].wait()
        total = jnp.zeros((8, columns), F32)
        for k, r in enumerate(order):
            gain, bias = factors[k]
            start = pl.multiple_of((me_ref[0] ^ r) * width, width)
            block = ref[pl.ds(start, width), :]
            total = total + jnp.dot(bias, block, preferred_element_type=F32)
            for j in range(columns // PAIR):
                target = (j * count + n) * PAIR
                folded_ref[k * width : (k + 1) * width, target : target + PAIR] = (
                    block[:, j * PAIR : (j + 1) * PAIR].astype(F32) * gain
                ).astype(BF16)
        for j in range(columns // PAIR):
            target = (j * count + n) * PAIR
            sums_ref[1:2, target : target + PAIR] = total[0:1, j * PAIR : (j + 1) * PAIR]
    sums = jnp.dot(jnp.ones((8, folded_ref.shape[0]), BF16), folded_ref[...], preferred_element_type=F32)
    sums_ref[0:1, :] = sums[0:1]


def folded(me, order, which, gains, weights):
    rows, columns = weights[0].shape
    total = columns * len(weights)
    spaces = {2 + n: pltpu.HBM for n in range(len(weights))}
    return kernel_call(
        functools.partial(fold_kernel, order, which, len(weights)),
        [((rows, total), BF16), ((2, total), F32)],
        [me, gains, *weights],
        spaces={0: pltpu.SMEM, **spaces},
        scratch=[pltpu.VMEM((rows, columns), BF16)] * len(weights) + [pltpu.SemaphoreType.DMA((len(weights),))],
    )


def stack_kernel(*refs):
    count = (len(refs) - 2) // 2
    sources, out_ref, rows, done = refs[:count], refs[count], refs[count + 1 : -1], refs[-1]
    copies = [pltpu.make_async_copy(sources[i], rows[i], done.at[i]) for i in range(count)]
    for copy in copies:
        copy.start()
    out_ref[...] = jnp.zeros_like(out_ref)
    for i, copy in enumerate(copies):
        copy.wait()
        out_ref[i : i + 1, :] = rows[i][...].astype(F32).reshape(1, out_ref.shape[1])


def reorder_kernel(order, me_ref, source_ref, out_ref, done):
    width = source_ref.shape[1] // len(order)
    copies = []
    for k, r in enumerate(order):
        cols = pl.ds(pl.multiple_of((me_ref[0] ^ r) * width, PAIR), width)
        copies.append(
            pltpu.make_async_copy(source_ref.at[:, cols], out_ref.at[:, k * width : (k + 1) * width], done.at[k])
        )
        copies[-1].start()
    for copy in copies:
        copy.wait()


def half_kernel(part_ref, source_ref, _, half_ref, done):
    rows = half_ref.shape[0]
    copy = pltpu.make_async_copy(
        source_ref.at[pl.ds(pl.multiple_of(part_ref[0] * rows, rows), rows), :], half_ref, done.at[0]
    )
    copy.start()
    copy.wait()


def row_statistics(refs):
    rows, width = refs[0].shape
    full = width * len(refs)
    means, scales = [], []
    step = math.gcd(rows, 64)
    for start in range(0, rows, step):
        parts = [ref[start : start + step, :].astype(F32) for ref in refs]
        mean = sum(jnp.sum(part, axis=1, keepdims=True) for part in parts) / full
        variance = sum(jnp.sum(jnp.square(part - mean), axis=1, keepdims=True) for part in parts) / full
        means.append(mean)
        scales.append(lax.rsqrt(variance + EPSILON))
    return jnp.concatenate(means, axis=0), jnp.concatenate(scales, axis=0)


def norm_product(cells, mean, scale, folded_ref, sums_ref, start, columns):
    cols = slice(start, start + columns)
    product = jnp.dot(cells, folded_ref[:, cols], preferred_element_type=F32)
    return (product - mean * sums_ref[0:1, cols]) * scale + sums_ref[1:2, cols]


def lane_masks():
    lanes = lax.broadcasted_iota(jnp.int32, (1, PAIR), 1)
    return lanes < HEAD_DIM


def keys_values(projected):
    low = lane_masks()
    values = projected[:, PAIR : 2 * PAIR]
    return (
        projected[:, :PAIR].astype(BF16),
        jnp.where(low, values, 1.0).astype(BF16),
        jnp.where(low, 1.0, values).astype(BF16),
    )


def project_kernel(count, first, *refs):
    blocks, (folded_ref, sums_ref, *refs) = refs[:count], refs[count:]
    key_ref, value_ref = refs[-2:]
    query_ref = refs[-3] if first else None
    mean, scale = row_statistics(blocks)
    cells = jnp.concatenate([ref[...] for ref in blocks], axis=1)
    low = lane_masks()
    for j in range(key_ref.shape[1] // PAIR):
        columns = (3 if first else 2) * PAIR
        projected = norm_product(cells, mean, scale, folded_ref, sums_ref, j * 3 * PAIR, columns)
        base = 2 * j * PAIR
        (
            key_ref[:, j * PAIR : (j + 1) * PAIR],
            value_ref[:, base : base + PAIR],
            value_ref[:, base + PAIR : base + 2 * PAIR],
        ) = keys_values(projected)
        if first:
            queries = projected[:, 2 * PAIR :] * SCORE_SCALE
            query_ref[:, base : base + PAIR] = jnp.where(low, queries, 0.0).astype(BF16)
            query_ref[:, base + PAIR : base + 2 * PAIR] = jnp.where(low, 0.0, queries).astype(BF16)


def rows_of(ref, spans, cols):
    return jnp.concatenate([ref[start : start + size, cols] for start, size in spans], axis=0)


def attend_pair(pair, spans, query_ref, keys, values, state_ref):
    for head in range(2):
        index = 2 * pair + head
        queries = rows_of(query_ref, spans, slice(index * PAIR, (index + 1) * PAIR))
        scores = lax.dot_general(queries, keys, (((1,), (1,)), ((), ())), preferred_element_type=F32)
        peak = jnp.max(scores, axis=1, keepdims=True)
        soft = jnp.exp2(scores - peak).astype(BF16)
        sums = jnp.dot(soft, values[head], preferred_element_type=F32)
        state_ref[:, 2 * index * PAIR : (2 * index + 1) * PAIR] = sums
        state_ref[:, (2 * index + 1) * PAIR : (2 * index + 2) * PAIR] = jnp.broadcast_to(peak, (peak.shape[0], PAIR))


def merge_head(old_ref, part_ref, spans, index):
    sums = slice(2 * index * PAIR, (2 * index + 1) * PAIR)
    peaks = slice((2 * index + 1) * PAIR, (2 * index + 2) * PAIR)
    old_peak, part_peak = rows_of(old_ref, spans, peaks), part_ref[:, peaks]
    peak = jnp.maximum(old_peak, part_peak)
    total = rows_of(old_ref, spans, sums) * jnp.exp2(old_peak - peak) + part_ref[:, sums] * jnp.exp2(part_peak - peak)
    return total, peak


def attend_kernel(first, last, spans, query_ref, key_ref, value_ref, *refs):
    if last:
        old_ref, attended, part = refs[0], refs[-2], refs[-1]
    elif first:
        part, token_ref = refs[-2:]
    else:
        old_ref, (state_ref, token_ref, part) = refs[0], refs[-3:]
    if not last:
        token_ref[...] = jnp.zeros_like(token_ref)
    pairs = query_ref.shape[1] // (2 * PAIR)
    key_refs, value_refs = [key_ref], [value_ref]
    if last:
        key_refs, value_refs = key_refs + [refs[1]], value_refs + [refs[2]]
    for j in range(pairs):
        keys = jnp.concatenate([ref[:, j * PAIR : (j + 1) * PAIR] for ref in key_refs], axis=0)
        values = [
            jnp.concatenate([ref[:, n * PAIR : (n + 1) * PAIR] for ref in value_refs], axis=0)
            for n in (2 * j, 2 * j + 1)
        ]
        attend_pair(j, spans, query_ref, keys, values, part)
    if first:
        return
    low = lane_masks()
    for j in range(pairs):
        heads = [merge_head(old_ref, part, spans, 2 * j + head) for head in range(2)]
        if last:
            (one, _), (two, _) = heads
            both = jnp.where(low, one, two)
            weight = pltpu.roll(jnp.where(low, two, one), HEAD_DIM, 1)
            attended[:, j * PAIR : (j + 1) * PAIR] = (both / weight).astype(BF16)
        else:
            for head, (sums, peak) in enumerate(heads):
                at = 2 * (2 * j + head) * PAIR
                state_ref[:, at : at + PAIR] = sums
                state_ref[:, at + PAIR : at + 2 * PAIR] = peak


def middle_kernel(count, order, spans, me_ref, part_ref, odd_ref, *refs):
    attended, frames_refs, refs = refs[:count], refs[count : 2 * count], refs[2 * count :]
    *pieces, folded_ref, sums_ref, own_ref, out_ref, near_ref, far_ref, middle = refs
    total = out_ref.shape[0]
    width = frames_refs[0].shape[1]
    cells = jnp.concatenate([ref[:, :width] for ref in attended], axis=1)
    swap = part_ref[0] != 0

    def weights(k):
        if width % PAIR:
            cols = slice(k * width, (k + 1) * width)
        else:
            cols = pl.ds(pl.multiple_of((me_ref[0] ^ order[k]) * width, PAIR), width)
        rows, index = [], 0
        while index < len(pieces):
            mine = pieces[index][:, cols]
            index += 1
            if mine.shape[0] < width:
                other = pieces[index][:, cols]
                index += 1
                mine = jnp.concatenate([jnp.where(swap, other, mine), jnp.where(swap, mine, other)], axis=0)
            rows.append(mine)
        return jnp.concatenate(rows, axis=0)

    for k in range(0, count, 2):
        both = jnp.concatenate([weights(k), weights(k + 1)], axis=1)
        share = jnp.dot(cells, both, preferred_element_type=F32)
        for n in range(2):
            cols = slice((k + n) * width, (k + n + 1) * width)
            own = jnp.concatenate([frames_refs[k + n][start : start + size, :] for start, size in spans], axis=0)
            middle[:, cols] = (own.astype(F32) + share[:, n * width : (n + 1) * width]).astype(BF16)
    own_ref[...] = middle[:, :width]
    mean, scale = row_statistics((middle,))
    cells = middle[...]
    for j in range(out_ref.shape[1] // PAIR):
        both = norm_product(cells, mean, scale, folded_ref, sums_ref, j * 2 * PAIR, 2 * PAIR)
        out_ref[:, j * PAIR : (j + 1) * PAIR] = (
            both[:, :PAIR] / (1.0 + jnp.exp(-both[:, PAIR:]))
        ).astype(BF16)
    odd = odd_ref[0] != 0
    head, tail = out_ref[:HALO, :], out_ref[total - HALO :, :]
    near_ref[...] = jnp.where(odd, head, tail)
    far_ref[...] = jnp.where(odd, tail, head)


def conv_rows(padded, start, piece, cols, taps, scale, shift):
    window = padded[pl.ds(start, piece + 2 * HALO), cols]
    convolved = None
    for residue in range(8):
        part = None
        for offset in range(residue, KERNEL + 1, 8):
            if offset == 0:
                continue
            base = offset - residue
            term = taps[offset - 1] * window[base : base + piece + 8]
            part = term if part is None else part + term
        part = part[residue : residue + piece]
        convolved = part if convolved is None else convolved + part
    value = convolved * scale + shift
    return (value / (1.0 + jnp.exp(-value))).astype(BF16)


def conv_kernel(outer, first_ref, second_ref, *refs):
    if outer:
        odd_ref, near_ref, far_ref, *refs = refs
        odd, near, far = odd_ref[0] != 0, near_ref[...], far_ref[...]
    taps_ref, bn_ref, w_ref, keep_ref, send_ref, padded, activated = refs
    total, width = first_ref.shape
    half = keep_ref.shape[1]
    piece, quarter = 32, total // 2
    if outer:
        runs = (
            (jnp.where(odd, near, far), first_ref[:quarter, :], second_ref[:HALO, :]),
            (second_ref[total - HALO :, :], first_ref[quarter:, :], jnp.where(odd, far, near)),
        )
    else:
        runs = ((first_ref[quarter - HALO : quarter, :], second_ref[...], first_ref[quarter : quarter + HALO, :]),)
    at = 0
    for before, rows, behind in runs:
        count = rows.shape[0]
        padded[0:HALO, :] = before.astype(F32)
        padded[HALO : HALO + count, :] = rows.astype(F32)
        padded[HALO + count : 2 * HALO + count, :] = behind.astype(F32)
        for col in range(0, width, PAIR):
            cols = slice(col, col + PAIR)
            taps = [taps_ref[j : j + 1, cols] for j in range(KERNEL)]
            scale, shift = bn_ref[0:1, cols], bn_ref[1:2, cols]

            def block(index, carry, at=at):
                start = pl.multiple_of(index * piece, piece)
                target = pl.multiple_of(at + index * piece, piece)
                activated[pl.ds(target, piece), cols] = conv_rows(padded, start, piece, cols, taps, scale, shift)
                return carry

            lax.fori_loop(0, count // piece, block, 0, unroll=4)
        at += count
    share = activated[...]
    send_ref[...] = jnp.dot(share, w_ref[:, half:], preferred_element_type=F32).astype(BF16)
    keep_ref[...] = jnp.dot(share, w_ref[:, :half], preferred_element_type=F32).astype(BF16)


def pad_columns(weight, width):
    if weight.shape[1] == width:
        return weight
    return jnp.pad(weight, ((0, 0), (0, width - weight.shape[1])))


def on_device(
    frames_in,
    norm1_gain,
    norm1_bias,
    w_query,
    w_key,
    w_value,
    w_out,
    norm2_gain,
    norm2_bias,
    w_glu_value,
    w_glu_gate,
    depth_kernel,
    bn_scale,
    bn_shift,
    w_proj,
):
    frames, width = frames_in.shape
    grid, ctx = lax.axis_size("grid"), lax.axis_size("ctx")
    me = lax.axis_index("grid")
    place = me.astype(jnp.int32).reshape(1)
    odd = (lax.axis_index("ctx") & 1).astype(jnp.int32).reshape(1)
    order = list(range(0, grid, CORES)) + list(range(1, grid, CORES))
    padded = -(-width // PAIR) * PAIR
    every = ((0, frames),)

    def by_distance(cells):
        return jnp.concatenate(
            [lax.dynamic_slice_in_dim(cells, (me ^ r) * width, width, 1) for r in order], axis=1
        )

    def over_chips(block):
        return [exchange(block, "grid", CORES * a) for a in range(1, grid // CORES)]

    def other_core(blocks):
        return [exchange(block, "grid", 1) for block in blocks]

    vectors = [norm1_gain, norm1_bias, norm2_gain, norm2_bias]
    (gains,) = kernel_call(
        stack_kernel,
        [((8, width), F32)],
        vectors,
        spaces={i: pltpu.HBM for i in range(len(vectors))},
        scratch=[pltpu.VMEM((width,), BF16)] * len(vectors) + [pltpu.SemaphoreType.DMA((len(vectors),))],
    )
    gains = lax.all_gather(gains, "grid", axis=0, tiled=True)
    raw = {0: frames_in}
    chips = {0: over_chips(frames_in)}
    for k in reversed(range(ctx.bit_length() - 1)):
        raw[1 << k] = exchange(frames_in, "ctx", 1 << k)

    w_query, w_key, w_value, w_glu_value, w_glu_gate = (
        pad_columns(weight, padded) for weight in (w_query, w_key, w_value, w_glu_value, w_glu_gate)
    )
    if width % PAIR:
        row_pad = ((0, padded - width), (0, 0))
        w_p = jnp.pad(by_distance(w_proj), row_pad)
    else:
        (w_p,) = kernel_call(
            functools.partial(reorder_kernel, order),
            [(w_proj.shape, BF16)],
            [place, w_proj],
            spaces={0: pltpu.SMEM, 1: pltpu.HBM},
            scratch=[pltpu.SemaphoreType.DMA((grid,))],
        )
    taps = pad_columns(depth_kernel, padded)
    bn = pad_columns(jnp.stack([bn_scale, bn_shift]), padded)
    qkv, qkv_sums = folded(place, order, 0, gains, (w_key, w_value, w_query))
    chips[0] = [after(block, qkv_sums) for block in chips[0]]
    glu, glu_sums = folded(place, order, 2, gains, (w_glu_value, w_glu_gate))

    parts = lax.axis_size("parts")
    part = lax.axis_index("parts").astype(jnp.int32).reshape(1)
    if parts == 2:
        (half,) = kernel_call(
            half_kernel,
            [((width // 2, w_out.shape[1]), BF16)],
            [part, w_out, odd],
            spaces={0: pltpu.SMEM, 1: pltpu.HBM, 2: pltpu.SMEM},
            scratch=[pltpu.SemaphoreType.DMA((1,))],
        )
    else:
        half = w_out
    crossed = over_chips(after(half, *chips[0]))
    state_shape = ((frames, 4 * padded), F32)
    token_shape = ((8, 128), F32)
    wide, narrow = ((frames, 2 * padded), BF16), ((frames, padded), BF16)
    chips[1] = [exchange(block, "ctx", 1) for block in chips[0]]
    own = [frames_in] + chips[0]
    own_blocks = own + other_core(own)
    n = len(own_blocks)
    early = [*[raw[s] for s in raw if s], glu_sums, w_p]
    queries, keys, values = kernel_call(
        functools.partial(project_kernel, n, True),
        [wide, narrow, wide],
        [*own_blocks, qkv, qkv_sums, *early],
        spaces={n + 2 + i: pl.ANY for i in range(len(early))},
    )
    def prepare(s, done):
        if 2 <= s < ctx:
            low = s & -s
            if s != low:
                raw[s] = after(exchange(raw[s ^ low], "ctx", low), done)
            chips[s] = over_chips(raw[s])

    prepare(2, None)
    state, token = kernel_call(
        functools.partial(attend_kernel, True, False, every),
        [state_shape, token_shape],
        [queries, keys, values, *crossed],
        spaces={3 + i: pl.ANY for i in range(len(crossed))},
    )
    crossed = [after(block, token) for block in crossed]
    swapped = [exchange(block, "parts", 1) for block in crossed] if parts == 2 else []
    moved = {1: [after(block, token) for block in chips[1]]}
    for s in range(1, ctx):
        last = s == ctx - 1
        mine = [raw[s]] + moved[s]
        keys, values = kernel_call(
            functools.partial(project_kernel, n, False),
            [narrow, wide],
            [*mine, *other_core(mine), qkv, qkv_sums],
        )
        if last:
            break
        before = keys, values
        prepare(s + 2, token)
        moved[s + 1] = [after(block, token) for block in chips[s + 1]]
        behind = [raw[s + 2]] if s + 2 < ctx else []
        behind += moved[s + 1]
        if s == ctx - 2:
            continue
        state, token = kernel_call(
            functools.partial(attend_kernel, False, False, every),
            [state_shape, token_shape],
            [queries, keys, values, state, *behind],
            spaces={4 + i: pl.ANY for i in range(len(behind))},
            aliases={3: 0},
            scratch=[pltpu.VMEM(*state_shape)],
        )
    rows, quarter = frames // 2, frames // 4
    spans = (((0, quarter), (3 * quarter, quarter)), ((quarter, rows),))
    attended = []
    for h in range(2):
        (mine,) = kernel_call(
            functools.partial(attend_kernel, False, True, spans[h]),
            [((rows, padded), BF16)],
            [queries, keys, values, state, *before],
            scratch=[pltpu.VMEM((rows, 4 * padded), F32)],
        )
        attended.append([mine] + over_chips(mine))
    swapped = [after(block, attended[0][0]) for block in swapped]
    pieces = [w_out]
    for a, block in enumerate(crossed):
        pieces += [block, swapped[a]] if swapped else [block]
    pieces = pieces + other_core(pieces)
    if width % PAIR:
        pieces = [by_distance(piece) for piece in pieces]
    middle, gated = [], []
    for h in range(2):
        mine = attended[h]
        done = gated[0] if h else attended[1][0]
        mine = mine[:1] + [after(block, done) for block in mine[1:]]
        results = kernel_call(
            functools.partial(middle_kernel, n, order, spans[h]),
            [((rows, width), BF16), ((rows, padded), BF16), ((HALO, padded), BF16), ((HALO, padded), BF16)],
            [place, part, odd, *mine, *other_core(mine), *own_blocks, *pieces, glu, glu_sums],
            spaces={0: pltpu.SMEM, 1: pltpu.SMEM, 2: pltpu.SMEM},
            scratch=[pltpu.VMEM((rows, grid * width), BF16)],
        )
        middle.append(results[0])
        gated.append(results[1])
        if h == 0:
            near = exchange(results[2], "ctx", 1)
            between = [(i, i + 1) for i in range(1, ctx - 1, 2)]
            far = lax.ppermute(results[3], "ctx", between + [(b, a) for a, b in between])
    outs = [None, None]
    for h, around in ((1, []), (0, [odd, near, far])):
        keep, send = kernel_call(
            functools.partial(conv_kernel, h == 0),
            [((rows, grid // CORES * width), BF16)] * 2,
            [*gated, *around, taps, bn, w_p],
            spaces={} if h else {2: pltpu.SMEM},
            scratch=[pltpu.VMEM((rows + 2 * HALO, padded), F32), pltpu.VMEM((rows, padded), BF16)],
        )
        theirs = exchange(send, "grid", 1)

        def pair_sum(a):
            cols = slice(a * width, (a + 1) * width)
            return keep[:, cols].astype(F32) + theirs[:, cols].astype(F32)

        result = middle[h].astype(F32) + pair_sum(0)
        for a in range(1, grid // CORES):
            result = result + exchange(pair_sum(a).astype(BF16), "grid", CORES * a).astype(F32)
        outs[h] = result.astype(BF16)
    return jnp.concatenate([outs[0][:quarter], outs[1], outs[0][quarter:]], axis=0)


def solution(mesh):
    return jax.shard_map(
        on_device,
        mesh=mesh,
        in_specs=(
            P(("parts", "ctx"), "grid"),
            P("grid"),
            P("grid"),
            P(None, "grid"),
            P(None, "grid"),
            P(None, "grid"),
            P("grid", None),
            P("grid"),
            P("grid"),
            P(None, "grid"),
            P(None, "grid"),
            P(None, "grid"),
            P("grid"),
            P("grid"),
            P("grid", None),
        ),
        out_specs=P(("parts", "ctx"), "grid"),
        check_vma=False,
    )
```
